32 devices in a mesh: row: 4 (over y, core), col: 8 (over z, x).
Axes of the slice: x: 2, y: 2, z: 4, core: 2. Of those that a mesh axis runs over, the one named last changes fastest.
Arguments:
- features: bfloat16 [65536, 256], P(('row', 'col')), may hold values from -6 to 6
- hub_features: bfloat16 [512, 256], P(('row', 'col')), may hold values from -6 to 6
- w_self: bfloat16 [256, 256], replicated, may hold values from -0.375 to 0.375
- w_neigh: bfloat16 [256, 256], replicated, may hold values from -0.375 to 0.375
- out_bias: float32 [256], replicated, may hold values from -4 to 4
- local_edges: int32 [65536, 4], P(('row', 'col')), may hold values from 0 to 2047
- hub_edges: int32 [65536, 2], P(('row', 'col')), may hold values from 0 to 511
- remote_edges: int32 [65536, 4], P(('row', 'col')), may hold values from 0 to 511
- send_rows: int32 [32, 512], P(('row', 'col')), may hold values from 0 to 2047
- cotangent: bfloat16 [65536, 256], P(('row', 'col')), may hold values from -6 to 6
Outputs:
- activated: bfloat16 [65536, 256], P(('row', 'col'))
- grad_features: float32 [65536, 256], P(('row', 'col'))
- grad_hubs: float32 [512, 256], P(('row', 'col'))
- grad_w_self: float32 [256, 256], replicated
- grad_w_neigh: float32 [256, 256], replicated
- grad_bias: float32 [256], replicated
The draws below stay inside these ranges and needn't reach their ends.
All inputs are finite; a program needn't handle non-finite values.
Results may differ from the reference program's by a relative error of at most 0.0075.
Values may be sent and summed in bfloat16 or wider, within the bound.
No kernel may reach another device: no remote copies, remote signals or barrier semaphores. Data moves between devices by JAX's collectives and lax.ppermute only.
A program may use at most 64 MiB of HBM per device.

```python
import math
import jax
import jax.numpy as jnp
import numpy as np

D = 256
NODE_DEV = 2048
BND = 16
FL = 4
FH = 2
FR = 4
NODES = 65536
HUBS = 512
REMOTE = 512
DEVICES = 32


def set_ends(array, rng, smallest, high):
    longest = array.shape.index(max(array.shape))
    spots = []
    for shift in (0, 1):
        where = [jax.random.randint(jax.random.fold_in(rng, axis), (), 0, length) for axis, length in enumerate(array.shape)]
        where[longest] = (where[longest] + shift) % array.shape[longest]
        spots.append(tuple(where))
    return array.at[spots[0]].set(smallest).at[spots[1]].set(high)


def steps_of(key, dims, pieces, least, top_value):
    factor_of, own = 1.0, jax.random.fold_in(key, 6)
    for dim, shards_of in pieces:
        heights = jnp.exp(jax.random.uniform(jax.random.fold_in(own, dim), (shards_of,), jnp.float32, least / len(pieces), top_value / len(pieces)))
        factor_of = factor_of * jnp.repeat(heights, dims[dim] // shards_of).reshape([-1 if axis == dim else 1 for axis in range(len(dims))])
    return factor_of


def rank_table(count, slope):
    weights = [(1 << 20) // math.isqrt(grade ** slope) + 1 for grade in range(1, count + 1)]
    spread = 1 + sum(weights) // (1 << 30)
    return np.cumsum(np.array([max(1, weight // spread) for weight in weights]))


def skewed_ids(rng, shape, amount, skew):
    table = rank_table(amount, skew)
    pick = jax.random.randint(jax.random.fold_in(rng, 1), shape, 0, int(table[amount - 1]))
    rank = jnp.searchsorted(jnp.asarray(table, jnp.int32), pick, side="right")
    return jax.random.permutation(jax.random.fold_in(rng, 2), amount)[rank].astype(jnp.int32)


def centred(key, dims, deviation, bound, shards=(), held_as=jnp.bfloat16):
    drawn = jax.random.normal(key, dims, jnp.float32) * deviation
    if len(shards) > 0:
        drawn = steps_of(key, dims, shards, -0.22, 0.18) * drawn
    return jnp.clip(drawn, min=-bound, max=bound).astype(held_as)


def setup_inputs(seed: int = 0) -> dict:
    keys = jax.random.split(jax.random.key(seed), 11)
    return {
        "features": centred(keys[0], (NODES, D), 1.0, 6.0, ((0, 32),)),
        "hub_features": centred(keys[1], (HUBS, D), 1.0, 6.0, ((0, 32),)),
        "w_self": centred(keys[2], (D, D), D ** -0.5, 0.375),
        "w_neigh": centred(keys[3], (D, D), D ** -0.5, 0.375),
        "out_bias": centred(keys[4], (D,), 1.0, 4.0, (), jnp.float32),
        "local_edges": set_ends(jax.random.randint(keys[5], (NODES, FL), 0, NODE_DEV), jax.random.fold_in(keys[5], 1), 0, NODE_DEV - 1).astype(jnp.int32),
        "hub_edges": set_ends(skewed_ids(keys[6], (NODES, FH), HUBS, 2), jax.random.fold_in(keys[6], 3), 0, HUBS - 1).astype(jnp.int32),
        "remote_edges": set_ends(jax.random.randint(keys[7], (NODES, FR), 0, REMOTE), jax.random.fold_in(keys[7], 1), 0, REMOTE - 1).astype(jnp.int32),
        "send_rows": set_ends(jax.random.randint(keys[8], (DEVICES, DEVICES * BND), 0, NODE_DEV), jax.random.fold_in(keys[8], 1), 0, NODE_DEV - 1).astype(jnp.int32),
        "cotangent": centred(keys[9], (NODES, D), 1.0, 6.0, ((0, 32),)),
    }


def reference(features, hub_features, w_self, w_neigh, out_bias, local_edges, hub_edges, remote_edges, send_rows, cotangent):
    node_count = features.shape[0]
    block = (jnp.arange(node_count, dtype=jnp.int32) // NODE_DEV)[:, None]
    local_index = (block * NODE_DEV + local_edges).astype(jnp.int32)
    source = remote_edges // BND
    slot = remote_edges % BND
    remote_rows = send_rows[source, block * BND + slot]
    remote_index = (source * NODE_DEV + remote_rows).astype(jnp.int32)
    fanout = FL + FH + FR
    summed = jnp.zeros(features.shape, jnp.float32)
    for column in range(FL):
        summed = summed + features[local_index[:, column]].astype(jnp.float32)
    for column in range(FH):
        summed = summed + hub_features[hub_edges[:, column]].astype(jnp.float32)
    for column in range(FR):
        summed = summed + features[remote_index[:, column]].astype(jnp.float32)
    neighbour_mean = (summed / fanout).astype(jnp.bfloat16)
    pre_act = jnp.dot(features, w_self, preferred_element_type=jnp.float32)
    pre_act = pre_act + jnp.dot(neighbour_mean, w_neigh, preferred_element_type=jnp.float32)
    pre_act = pre_act + out_bias.astype(jnp.float32)
    sigmoid_pre = jax.nn.sigmoid(pre_act)
    activated = (pre_act * sigmoid_pre).astype(jnp.bfloat16)
    grad_pre = (cotangent.astype(jnp.float32) * sigmoid_pre * (1.0 + pre_act * (1.0 - sigmoid_pre))).astype(jnp.bfloat16)
    grad_w_self = jnp.dot(features.T, grad_pre, preferred_element_type=jnp.float32)
    grad_w_neigh = jnp.dot(neighbour_mean.T, grad_pre, preferred_element_type=jnp.float32)
    grad_bias = jnp.sum(grad_pre.astype(jnp.float32), axis=0)
    grad_mean = jnp.dot(grad_pre, w_neigh.T, preferred_element_type=jnp.float32) / fanout
    grad_features = jnp.dot(grad_pre, w_self.T, preferred_element_type=jnp.float32)
    for column in range(FL):
        grad_features = grad_features.at[local_index[:, column]].add(grad_mean)
    for column in range(FR):
        grad_features = grad_features.at[remote_index[:, column]].add(grad_mean)
    grad_hubs = jnp.zeros(hub_features.shape, jnp.float32)
    for column in range(FH):
        grad_hubs = grad_hubs.at[hub_edges[:, column]].add(grad_mean)
    return (activated, grad_features, grad_hubs, grad_w_self, grad_w_neigh, grad_bias)
```

```python
import functools

import jax
import jax.numpy as jnp
from jax import lax
from jax.experimental import pallas as pl
from jax.experimental.pallas import tpu as pltpu
from jax.sharding import PartitionSpec as P

AXES = ("row", "col")
LANES = 128
VMEM_LIMIT = 44 * 1024 * 1024
NT = (((1,), (1,)), ((), ()))
TN = (((0,), (0,)), ((), ()))


def params():
    return pltpu.CompilerParams(vmem_limit_bytes=VMEM_LIMIT)


def cost(flops, moved):
    return pl.CostEstimate(flops=int(flops), bytes_accessed=int(moved), transcendentals=0)


def full(shape):
    return pl.BlockSpec(shape, lambda *_: (0,) * len(shape))


def along_rows(index_row):
    count = index_row.shape[1]
    return jnp.transpose(jnp.broadcast_to(index_row, (LANES, count))).astype(jnp.int16)


def hits_by_row(columns, first, width):
    rows = columns[0].shape[0]
    lane = lax.broadcasted_iota(jnp.int32, (rows, LANES), 1).astype(jnp.int16)
    one = jnp.ones((rows, LANES), jnp.bfloat16)
    zero = jnp.zeros((rows, LANES), jnp.bfloat16)
    tiles = []
    for start in range(first, first + width, LANES):
        here = lane + jnp.int16(start)
        total = None
        for column in columns:
            hit = jnp.where(column == here, one, zero)
            total = hit if total is None else total + hit
        tiles.append(total)
    return jnp.concatenate(tiles, axis=1) if len(tiles) > 1 else tiles[0]


def hits_by_column(index_rows, first, height):
    count = index_rows[0].shape[1]
    down = lax.broadcasted_iota(jnp.int32, (height, count), 0).astype(jnp.int16)
    one = jnp.ones((height, count), jnp.bfloat16)
    zero = jnp.zeros((height, count), jnp.bfloat16)
    total = None
    for row in index_rows:
        entry = jnp.broadcast_to(row - first, (16, count)).astype(jnp.int16)
        entry = jnp.broadcast_to(entry[None], (height // 16, 16, count)).reshape(height, count)
        hit = jnp.where(entry == down, one, zero)
        total = hit if total is None else total + hit
    return total


def dot(a, b, dims=(((1,), (0,)), ((), ()))):
    return lax.dot_general(a, b, dims, preferred_element_type=jnp.float32)


def pick_kernel(send_ref, feat_ref, hub_ref, out_ref):
    parts, slab, width = out_ref.shape
    hub_rows = hub_ref.shape[0]
    slots = slab - hub_rows
    total = send_ref.shape[1]
    step = min(512, total)
    for start in range(0, total, step):
        column = along_rows(send_ref[:, start : start + step])
        picked = dot(hits_by_row([column], 0, feat_ref.shape[0]), feat_ref[...])
        out_ref[start // slots : (start + step) // slots, :slots, :] = (
            picked.astype(jnp.bfloat16).reshape(step // slots, slots, width)
        )
    out_ref[:, slots:, :] = jnp.broadcast_to(hub_ref[...][None], (parts, hub_rows, width))


def table_rows_of(hub_ref, remote_ref, slots, hub_rows):
    rows = []
    for j in range(remote_ref.shape[0]):
        entry = remote_ref[j : j + 1, :]
        rows.append(entry + lax.div(entry, jnp.int32(slots)) * hub_rows)
    for j in range(hub_ref.shape[0]):
        entry = hub_ref[j : j + 1, :]
        rows.append(entry + (lax.div(entry, jnp.int32(hub_rows)) + 1) * slots)
    return rows


def local_kernel(slots, hub_rows, local_ref, hub_ref, remote_ref, feat_ref, sum_ref, by_row_ref, by_col_ref):
    tile = 256
    local_rows = [local_ref[j : j + 1, :] for j in range(local_ref.shape[0])]
    columns = [along_rows(row) for row in local_rows]
    total = None
    for start in range(0, feat_ref.shape[0], tile):
        part = dot(hits_by_row(columns, start, tile), feat_ref[start : start + tile, :])
        total = part if total is None else total + part
    sum_ref[...] = total
    table = table_rows_of(hub_ref, remote_ref, slots, hub_rows)
    columns = [along_rows(row) for row in table]
    for start in range(0, by_row_ref.shape[1], tile):
        by_row_ref[:, start : start + tile] = hits_by_row(columns, start, tile)
        by_col_ref[start : start + tile, :] = hits_by_column(table, start, tile)


def middle_kernel(
    fanout,
    slots,
    feat_ref,
    sum_ref,
    by_row_ref,
    by_col_ref,
    table_ref,
    cot_ref,
    ws_ref,
    wn_ref,
    bias_ref,
    act_ref,
    grad_ref,
    pay_ref,
    table_acc,
    weight_acc,
    bias_acc,
):
    step = pl.program_id(0)
    width = feat_ref.shape[1]
    parts, slab, _ = table_ref.shape

    @pl.when(step == 0)
    def _():
        table_acc[...] = jnp.zeros_like(table_acc)
        weight_acc[...] = jnp.zeros_like(weight_acc)
        bias_acc[...] = jnp.zeros_like(bias_acc)

    feat = feat_ref[...]
    table = table_ref[...].reshape(parts * slab, width)
    mean = ((sum_ref[...] + dot(by_row_ref[...], table)) / fanout).astype(jnp.bfloat16)
    pre = dot(feat, ws_ref[...]) + dot(mean, wn_ref[...]) + bias_ref[...]
    sig = jax.nn.sigmoid(pre)
    act_ref[...] = (pre * sig).astype(jnp.bfloat16)
    grad = (cot_ref[...].astype(jnp.float32) * sig * (1.0 + pre * (1.0 - sig))).astype(jnp.bfloat16)
    grad_ref[...] = grad
    table_acc[...] += dot(by_col_ref[...], grad)
    weight_acc[:width, :] += dot(feat, grad, TN)
    weight_acc[width:, :] += dot(mean, grad, TN)
    bias_acc[...] += jnp.sum(grad.astype(jnp.float32), axis=0, keepdims=True)

    @pl.when(step == pl.num_programs(0) - 1)
    def _():
        pay_ref[:, :slab, :] = table_acc[...].astype(jnp.bfloat16).reshape(parts, slab, width)
        holders = 2 * width // 16
        pay_ref[:holders, slab : slab + 16, :] = (
            weight_acc[...].astype(jnp.bfloat16).reshape(holders, 16, width)
        )
        if parts > holders:
            pay_ref[holders:, slab : slab + 16, :] = jnp.zeros((parts - holders, 16, width), jnp.bfloat16)
        whole = bias_acc[...]
        high = whole.astype(jnp.bfloat16).astype(jnp.float32)
        place = lax.broadcasted_iota(jnp.int32, (8, width), 0)
        rows = jnp.where(place == 0, high, jnp.where(place == 1, whole - high, 0.0)).astype(jnp.bfloat16)
        pay_ref[:, slab + 16 :, :] = jnp.broadcast_to(rows[None], (parts, 8, width))


def scatter_kernel(local_ref, grad_ref, out_ref):
    height = out_ref.shape[0]
    first = pl.program_id(0) * height
    total = None
    for start in range(0, grad_ref.shape[0], 256):
        rows = [local_ref[j : j + 1, start : start + 256] for j in range(local_ref.shape[0])]
        part = dot(hits_by_column(rows, first, height), grad_ref[start : start + 256, :])
        total = part if total is None else total + part
    out_ref[...] = total


def sums_kernel(fanout, slots, hub_rows, back_ref, wn_ref, weight_ref, bias_ref, hub_ref):
    slab = slots + hub_rows
    parts, _, width = back_ref.shape
    weight = jnp.sum(back_ref[:, slab : slab + 16, :].astype(jnp.float32), axis=0)
    weight_ref[...] = jnp.broadcast_to(weight.astype(jnp.bfloat16)[None], (parts, 16, width))
    tail = jnp.sum(back_ref[:, slab + 16 :, :].astype(jnp.float32), axis=0)
    bias_ref[...] = jnp.sum(tail, axis=0, keepdims=True)
    hub = jnp.sum(back_ref[:, slots:slab, :].astype(jnp.float32), axis=0)
    high = hub.astype(jnp.bfloat16)
    low = (hub - high.astype(jnp.float32)).astype(jnp.bfloat16)
    hub_ref[...] = (dot(high, wn_ref[...], NT) + dot(low, wn_ref[...], NT)) / fanout


def final_kernel(fanout, slots, send_ref, back_ref, scat_ref, grad_ref, ws_ref, wn_ref, out_ref):
    height, width = out_ref.shape
    first = pl.program_id(0) * height
    parts = back_ref.shape[0]
    returned = back_ref[:, :slots, :].reshape(parts * slots, width)
    total = scat_ref[...]
    count = send_ref.shape[1]
    for start in range(0, count, 512):
        stop = min(count, start + 512)
        total = total + dot(hits_by_column([send_ref[:, start:stop]], first, height), returned[start:stop, :])
    out_ref[...] = dot(grad_ref[...], ws_ref[...], NT) + dot((total / fanout).astype(jnp.bfloat16), wn_ref[...], NT)


def body(
    features,
    hub_features,
    w_self,
    w_neigh,
    out_bias,
    local_edges,
    hub_edges,
    remote_edges,
    send_rows,
    cotangent,
):
    nodes, width = features.shape
    hub_rows = hub_features.shape[0]
    parts = lax.axis_size(AXES)
    slots = send_rows.shape[1] // parts
    slab = slots + hub_rows
    table_rows = parts * slab
    fanout = float(local_edges.shape[1] + hub_edges.shape[1] + remote_edges.shape[1])
    bf16, f32 = jnp.bfloat16, jnp.float32
    local_t, hub_t, remote_t = local_edges.T, hub_edges.T, remote_edges.T
    bias = out_bias.reshape(1, width)

    def exchange(value):
        return lax.all_to_all(value, AXES, split_axis=0, concat_axis=0, tiled=True)

    payload = pl.pallas_call(
        pick_kernel,
        out_shape=jax.ShapeDtypeStruct((parts, slab, width), bf16),
        compiler_params=params(),
        cost_estimate=cost(2 * parts * slots * nodes * width, nodes * width * 2),
        name="pick_rows",
    )(send_rows, features, hub_features)
    table = exchange(payload)

    block = 256
    local_sum, by_row, by_col = pl.pallas_call(
        functools.partial(local_kernel, slots, hub_rows),
        grid=(nodes // block,),
        in_specs=[
            pl.BlockSpec((local_t.shape[0], block), lambda i: (0, i)),
            pl.BlockSpec((hub_t.shape[0], block), lambda i: (0, i)),
            pl.BlockSpec((remote_t.shape[0], block), lambda i: (0, i)),
            full((nodes, width)),
        ],
        out_specs=[
            pl.BlockSpec((block, width), lambda i: (i, 0)),
            pl.BlockSpec((block, table_rows), lambda i: (i, 0)),
            pl.BlockSpec((table_rows, block), lambda i: (0, i)),
        ],
        out_shape=[
            jax.ShapeDtypeStruct((nodes, width), f32),
            jax.ShapeDtypeStruct((nodes, table_rows), bf16),
            jax.ShapeDtypeStruct((table_rows, nodes), bf16),
        ],
        compiler_params=params(),
        cost_estimate=cost(8 * nodes * nodes * width, nodes * table_rows * 4),
        name="local_gather",
    )(local_t, hub_t, remote_t, features)

    block = 512
    activated, grad_pre, terms = pl.pallas_call(
        functools.partial(middle_kernel, fanout, slots),
        grid=(nodes // block,),
        in_specs=[
            pl.BlockSpec((block, width), lambda i: (i, 0)),
            pl.BlockSpec((block, width), lambda i: (i, 0)),
            pl.BlockSpec((block, table_rows), lambda i: (i, 0)),
            pl.BlockSpec((table_rows, block), lambda i: (0, i)),
            full((parts, slab, width)),
            pl.BlockSpec((block, width), lambda i: (i, 0)),
            full((width, width)),
            full((width, width)),
            full((1, width)),
        ],
        out_specs=[
            pl.BlockSpec((block, width), lambda i: (i, 0)),
            pl.BlockSpec((block, width), lambda i: (i, 0)),
            full((parts, slab + 24, width)),
        ],
        out_shape=[
            jax.ShapeDtypeStruct((nodes, width), bf16),
            jax.ShapeDtypeStruct((nodes, width), bf16),
            jax.ShapeDtypeStruct((parts, slab + 24, width), bf16),
        ],
        scratch_shapes=[
            pltpu.VMEM((table_rows, width), f32),
            pltpu.VMEM((2 * width, width), f32),
            pltpu.VMEM((1, width), f32),
        ],
        compiler_params=params(),
        cost_estimate=cost(4 * nodes * table_rows * width, nodes * table_rows * 4),
        name="activate",
    )(features, local_sum, by_row, by_col, table, cotangent, w_self, w_neigh, bias)
    back = exchange(terms)

    block = 256
    local_back = pl.pallas_call(
        scatter_kernel,
        grid=(nodes // block,),
        in_specs=[full(local_t.shape), full((nodes, width))],
        out_specs=pl.BlockSpec((block, width), lambda i: (i, 0)),
        out_shape=jax.ShapeDtypeStruct((nodes, width), f32),
        compiler_params=params(),
        cost_estimate=cost(8 * nodes * nodes * width, nodes * width * 6),
        name="local_scatter",
    )(local_t, grad_pre)

    weight_rows, grad_bias, grad_hubs = pl.pallas_call(
        functools.partial(sums_kernel, fanout, slots, hub_rows),
        out_shape=[
            jax.ShapeDtypeStruct((parts, 16, width), bf16),
            jax.ShapeDtypeStruct((1, width), f32),
            jax.ShapeDtypeStruct((hub_rows, width), f32),
        ],
        compiler_params=params(),
        cost_estimate=cost(0, parts * 72 * width * 2),
        name="sums",
    )(back, w_neigh)
    weights = exchange(weight_rows)

    block = 512
    grad_features = pl.pallas_call(
        functools.partial(final_kernel, fanout, slots),
        grid=(nodes // block,),
        in_specs=[
            full(send_rows.shape),
            full((parts, slab + 24, width)),
            pl.BlockSpec((block, width), lambda i: (i, 0)),
            pl.BlockSpec((block, width), lambda i: (i, 0)),
            full((width, width)),
            full((width, width)),
        ],
        out_specs=pl.BlockSpec((block, width), lambda i: (i, 0)),
        out_shape=jax.ShapeDtypeStruct((nodes, width), f32),
        compiler_params=params(),
        cost_estimate=cost(2 * nodes * parts * slots * width, nodes * width * 10),
        name="return_scatter",
    )(send_rows, back, local_back, grad_pre, w_self, w_neigh)

    weights = weights[: 2 * width // 16].reshape(2, width, width).astype(f32)
    return (activated, grad_features, grad_hubs, weights[0], weights[1], grad_bias.reshape(width))


def solution(mesh):
    split = P(AXES, None)
    return jax.shard_map(
        body,
        mesh=mesh,
        in_specs=(split, split, P(), P(), P(), split, split, split, split, split),
        out_specs=(split, split, split, P(), P(), P()),
        check_vma=False,
    )
```

```python
import functools

import jax
import jax.numpy as jnp
from jax import lax
from jax.experimental import pallas as pl
from jax.experimental.pallas import tpu as pltpu
from jax.sharding import PartitionSpec as P

AXES = ("row", "col")
LANES = 128
TILE = 256
VMEM_LIMIT = 18 * 1024 * 1024
NT = (((1,), (1,)), ((), ()))
TN = (((0,), (0,)), ((), ()))
VMEM = pl.BlockSpec(memory_space=pltpu.VMEM)
SMEM = pl.BlockSpec(memory_space=pltpu.SMEM)
HBM = pl.BlockSpec(memory_space=pltpu.HBM)
bf16, f32 = jnp.bfloat16, jnp.float32


def params():
    return pltpu.CompilerParams(vmem_limit_bytes=VMEM_LIMIT)


def cost(flops, moved):
    return pl.CostEstimate(flops=int(flops), bytes_accessed=int(moved), transcendentals=0)


def along_rows(index_row):
    count = index_row.shape[1]
    return jnp.transpose(jnp.broadcast_to(index_row, (LANES, count))).astype(jnp.int16)


def hits_by_row(columns, first, width):
    rows = columns[0].shape[0]
    lane = lax.broadcasted_iota(jnp.int32, (rows, LANES), 1).astype(jnp.int16)
    one = jnp.ones((rows, LANES), bf16)
    zero = jnp.zeros((rows, LANES), bf16)
    tiles = []
    for start in range(first, first + width, LANES):
        here = lane + jnp.int16(start)
        total = None
        for column in columns:
            hit = jnp.where(column == here, one, zero)
            total = hit if total is None else total + hit
        tiles.append(total)
    return jnp.concatenate(tiles, axis=1) if len(tiles) > 1 else tiles[0]


def hits_by_column(index_rows, first, height):
    count = index_rows[0].shape[1]
    down = lax.broadcasted_iota(jnp.int32, (height, count), 0).astype(jnp.int16)
    one = jnp.ones((height, count), bf16)
    zero = jnp.zeros((height, count), bf16)
    total = None
    for row in index_rows:
        entry = jnp.broadcast_to(row - first, (16, count)).astype(jnp.int16)
        entry = jnp.broadcast_to(entry[None], (height // 16, 16, count)).reshape(height, count)
        hit = jnp.where(entry == down, one, zero)
        total = hit if total is None else total + hit
    return total


def dot(a, b, dims=(((1,), (0,)), ((), ()))):
    return lax.dot_general(a, b, dims, preferred_element_type=f32)


def index_rows(ref, start, count):
    return [ref[j : j + 1, pl.ds(start, count)] for j in range(ref.shape[0])]


def spread_kernel(hub_ref, out_ref):
    out_ref[...] = jnp.broadcast_to(hub_ref[...][None], out_ref.shape)


def pick_kernel(send_ref, feat_hbm, out_ref, feat_ref, sem):
    load = pltpu.make_async_copy(feat_hbm, feat_ref, sem)
    load.start()
    parts, slots, width = out_ref.shape
    total = send_ref.shape[1]
    step = min(512, total)
    load.wait()
    for start in range(0, total, step):
        column = along_rows(send_ref[:, start : start + step])
        picked = dot(hits_by_row([column], 0, feat_ref.shape[0]), feat_ref[...])
        out_ref[start // slots : (start + step) // slots] = picked.astype(bf16).reshape(step // slots, slots, width)


def local_kernel(local_ref, hub_ref, remote_ref, feat_ref, sum_ref, hub_by_row, hub_by_col, rem_by_row, rem_by_col):
    nodes = feat_ref.shape[0]

    @pl.loop(0, nodes // TILE)
    def _(block):
        start = pl.multiple_of(block * TILE, TILE)
        rows = index_rows(local_ref, start, TILE)
        columns = [along_rows(row) for row in rows]
        total = None
        for first in range(0, nodes, TILE):
            part = dot(hits_by_row(columns, first, TILE), feat_ref[first : first + TILE, :])
            total = part if total is None else total + part
        sum_ref[pl.ds(start, TILE), :] = total
        for edge_ref, by_row, by_col in ((remote_ref, rem_by_row, rem_by_col), (hub_ref, hub_by_row, hub_by_col)):
            rows = index_rows(edge_ref, start, TILE)
            columns = [along_rows(row) for row in rows]
            for first in range(0, by_row.shape[1], TILE):
                by_row[pl.ds(start, TILE), first : first + TILE] = hits_by_row(columns, first, TILE)
                by_col[first : first + TILE, pl.ds(start, TILE)] = hits_by_column(rows, first, TILE)


def middle_kernel(
    fanout,
    core_ref,
    feat_ref,
    sum_ref,
    hub_by_row,
    hub_by_col,
    rem_by_row,
    rem_by_col,
    bound_ref,
    hub_ref,
    cot_hbm,
    ws_ref,
    wn_ref,
    bias_ref,
    act_hbm,
    grad_ref,
    bound_out,
    keep_out,
    give_out,
    bias_out,
    cot_ref,
    act_ref,
    mean_ref,
    cot_sem,
    act_sem,
):
    nodes, width = feat_ref.shape
    parts, slots, _ = bound_ref.shape
    hub_rows = hub_ref.shape[1]
    half = hub_rows // 2
    blocks = nodes // TILE
    load = pltpu.make_async_copy(cot_hbm, cot_ref, cot_sem)
    load.start()
    bound = bound_ref[...].reshape(parts * slots, width)
    hubs = hub_ref[...].reshape(parts * hub_rows, width)
    stores = []
    bias_total = jnp.zeros((1, width), f32)
    for block in range(blocks):
        here = slice(block * TILE, (block + 1) * TILE)
        total = sum_ref[here, :] + dot(rem_by_row[here, :], bound) + dot(hub_by_row[here, :], hubs)
        mean = (total / fanout).astype(bf16)
        mean_ref[here, :] = mean
        pre = dot(feat_ref[here, :], ws_ref[...]) + dot(mean, wn_ref[...]) + bias_ref[...]
        sig = jax.nn.sigmoid(pre)
        if block == 0:
            load.wait()
        act_ref[here, :] = (pre * sig).astype(bf16)
        grad = (cot_ref[here, :].astype(f32) * sig * (1.0 + pre * (1.0 - sig))).astype(bf16)
        grad_ref[here, :] = grad
        bias_total = bias_total + jnp.sum(grad.astype(f32), axis=0, keepdims=True)
        store = pltpu.make_async_copy(act_ref.at[here, :], act_hbm.at[here, :], act_sem.at[block])
        store.start()
        stores.append(store)
    grad = grad_ref[...]
    bound_out[...] = dot(rem_by_col[...], grad).astype(bf16).reshape(parts, slots, width)
    hub_terms = dot(hub_by_col[...], grad).reshape(parts, 2, half, width)
    first_core = core_ref[0] == 0
    keep_out[:, :half, :] = jnp.where(first_core, hub_terms[:, 0], hub_terms[:, 1])
    give_out[:, :half, :] = jnp.where(first_core, hub_terms[:, 1], hub_terms[:, 0]).astype(bf16)
    per = width // 16
    for which, source in enumerate((feat_ref, mean_ref)):
        terms = dot(source[...], grad, TN).reshape(per, 2, 8, width)
        held = slice(which * per, (which + 1) * per)
        keep_out[held, half:, :] = jnp.where(first_core, terms[:, 0], terms[:, 1])
        give_out[held, half:, :] = jnp.where(first_core, terms[:, 1], terms[:, 0]).astype(bf16)
    if parts > 2 * per:
        keep_out[2 * per :, half:, :] = jnp.zeros((parts - 2 * per, 8, width), f32)
        give_out[2 * per :, half:, :] = jnp.zeros((parts - 2 * per, 8, width), bf16)
    bias_out[...] = jnp.broadcast_to(bias_total[None], bias_out.shape)
    for store in stores:
        store.wait()


def join_kernel(keep_ref, got_ref, out_ref):
    out_ref[...] = (keep_ref[...] + got_ref[...].astype(f32)).astype(bf16)


def scatter_kernel(local_ref, send_ref, grad_ref, out_ref, hits_ref):
    nodes = out_ref.shape[0]

    @pl.loop(0, nodes // TILE)
    def _(block):
        first = pl.multiple_of(block * TILE, TILE)
        total = None
        for start in range(0, nodes, TILE):
            rows = index_rows(local_ref, start, TILE)
            part = dot(hits_by_column(rows, first, TILE), grad_ref[start : start + TILE, :])
            total = part if total is None else total + part
        out_ref[pl.ds(first, TILE), :] = total
        for start in range(0, send_ref.shape[1], TILE):
            hits_ref[pl.ds(first, TILE), start : start + TILE] = hits_by_column(
                index_rows(send_ref, start, TILE), first, TILE
            )


def sums_kernel(fanout, rows, half, back_ref, wn_ref, weight_ref, hub_ref):
    parts, slab, width = back_ref.shape
    cols = parts // rows
    back = back_ref[...].astype(f32).reshape(rows // 2, 2, cols, slab, width)
    total = jnp.sum(jnp.sum(back, axis=2), axis=0)
    weight = jnp.concatenate([total[0, half:], total[1, half:]], axis=0)
    weight_ref[...] = jnp.broadcast_to(weight.astype(bf16)[None], weight_ref.shape)
    hub = jnp.concatenate([total[0, :half], total[1, :half]], axis=0)
    high = hub.astype(bf16)
    low = (hub - high.astype(f32)).astype(bf16)
    hub_ref[...] = (dot(high, wn_ref[...], NT) + dot(low, wn_ref[...], NT)) / fanout


def final_kernel(fanout, hits_ref, bound_ref, scat_ref, grad_ref, ws_ref, wn_ref, out_hbm, out_ref, sem):
    nodes, width = scat_ref.shape
    returned = bound_ref[...].reshape(hits_ref.shape[1], width)
    stores = []
    for block in range(nodes // TILE):
        here = slice(block * TILE, (block + 1) * TILE)
        total = scat_ref[here, :] + dot(hits_ref[here, :], returned)
        out_ref[here, :] = dot(grad_ref[here, :], ws_ref[...], NT) + dot(
            (total / fanout).astype(bf16), wn_ref[...], NT
        )
        store = pltpu.make_async_copy(out_ref.at[here, :], out_hbm.at[here, :], sem.at[block])
        store.start()
        stores.append(store)
    for store in stores:
        store.wait()


def call(kernel, ins, in_specs, outs, out_specs, scratch, flops, moved, name):
    return pl.pallas_call(
        kernel,
        in_specs=in_specs,
        out_specs=out_specs,
        out_shape=outs,
        scratch_shapes=scratch,
        compiler_params=params(),
        cost_estimate=cost(flops, moved),
        name=name,
    )(*ins)


def body(
    features,
    hub_features,
    w_self,
    w_neigh,
    out_bias,
    local_edges,
    hub_edges,
    remote_edges,
    send_rows,
    cotangent,
):
    nodes, width = features.shape
    hub_rows = hub_features.shape[0]
    half = hub_rows // 2
    rows = lax.axis_size("row")
    parts = lax.axis_size(AXES)
    slots = send_rows.shape[1] // parts
    hubs, bounds = parts * hub_rows, parts * slots
    blocks = nodes // TILE
    fanout = float(local_edges.shape[1] + hub_edges.shape[1] + remote_edges.shape[1])
    local_t, hub_t, remote_t = local_edges.T, hub_edges.T, remote_edges.T
    bias = out_bias.reshape(1, width)
    core = (lax.axis_index("row") % 2).astype(jnp.int32).reshape(1)
    shape = jax.ShapeDtypeStruct

    def exchange(value):
        return lax.all_to_all(value, AXES, split_axis=0, concat_axis=0, tiled=True)

    hub_send = call(
        spread_kernel,
        (hub_features,),
        [VMEM],
        pltpu.HBM((parts, hub_rows, width), bf16),
        pl.BlockSpec((parts, hub_rows, width), lambda: (0, 0, 0)),
        [],
        0,
        hubs * width * 2,
        "spread_hubs",
    )
    hub_all = exchange(hub_send)
    bound_send, feat = call(
        pick_kernel,
        (send_rows, features),
        [VMEM, HBM],
        [pltpu.HBM((parts, slots, width), bf16), pltpu.VMEM((nodes, width), bf16)],
        [pl.BlockSpec((parts, slots, width), lambda: (0, 0, 0)), VMEM],
        [pltpu.SemaphoreType.DMA],
        2 * bounds * nodes * width,
        nodes * width * 2,
        "pick_rows",
    )
    bound_all = exchange(bound_send)

    local_sum, hub_by_row, hub_by_col, rem_by_row, rem_by_col = call(
        local_kernel,
        (local_t, hub_t, remote_t, feat),
        [VMEM] * 4,
        [
            pltpu.VMEM((nodes, width), f32),
            pltpu.VMEM((nodes, hubs), bf16),
            pltpu.VMEM((hubs, nodes), bf16),
            pltpu.VMEM((nodes, bounds), bf16),
            pltpu.VMEM((bounds, nodes), bf16),
        ],
        [VMEM] * 5,
        [],
        8 * nodes * nodes * width,
        nodes * width * 6,
        "local_gather",
    )

    activated, grad_pre, bound_terms, keep, give, bias_rows = call(
        functools.partial(middle_kernel, fanout),
        (
            core,
            feat,
            local_sum,
            hub_by_row,
            hub_by_col,
            rem_by_row,
            rem_by_col,
            bound_all,
            hub_all,
            cotangent,
            w_self,
            w_neigh,
            bias,
        ),
        [SMEM] + [VMEM] * 8 + [HBM] + [VMEM] * 3,
        [
            pltpu.HBM((nodes, width), bf16),
            pltpu.VMEM((nodes, width), bf16),
            pltpu.HBM((parts, slots, width), bf16),
            pltpu.VMEM((parts, half + 8, width), f32),
            pltpu.HBM((parts, half + 8, width), bf16),
            pltpu.HBM((parts, 1, width), f32),
        ],
        [
            HBM,
            VMEM,
            pl.BlockSpec((parts, slots, width), lambda: (0, 0, 0)),
            VMEM,
            pl.BlockSpec((parts, half + 8, width), lambda: (0, 0, 0)),
            pl.BlockSpec((parts, 1, width), lambda: (0, 0, 0)),
        ],
        [
            pltpu.VMEM((nodes, width), bf16),
            pltpu.VMEM((nodes, width), bf16),
            pltpu.VMEM((nodes, width), bf16),
            pltpu.SemaphoreType.DMA,
            pltpu.SemaphoreType.DMA((blocks,)),
        ],
        4 * nodes * (hubs + bounds) * width,
        nodes * width * 8,
        "activate",
    )
    got = lax.ppermute(give, "row", [(r, r ^ 1) for r in range(rows)])
    bound_back = exchange(bound_terms)
    joined = call(
        join_kernel,
        (keep, got),
        [VMEM, VMEM],
        pltpu.HBM((parts, half + 8, width), bf16),
        pl.BlockSpec((parts, half + 8, width), lambda: (0, 0, 0)),
        [],
        0,
        parts * (half + 8) * width * 8,
        "join_siblings",
    )
    sum_back = exchange(joined)
    bias_back = exchange(bias_rows)

    scattered, hits = call(
        scatter_kernel,
        (local_t, send_rows, grad_pre),
        [VMEM] * 3,
        [pltpu.VMEM((nodes, width), f32), pltpu.VMEM((nodes, bounds), bf16)],
        [VMEM] * 2,
        [],
        8 * nodes * nodes * width,
        nodes * width * 6,
        "local_scatter",
    )
    sum_back, scattered = lax.optimization_barrier((sum_back, scattered))

    weight_rows, grad_hubs = call(
        functools.partial(sums_kernel, fanout, rows, half),
        (sum_back, w_neigh),
        [VMEM, VMEM],
        [pltpu.HBM((parts, 16, width), bf16), shape((hub_rows, width), f32)],
        [pl.BlockSpec((parts, 16, width), lambda: (0, 0, 0)), pl.BlockSpec((hub_rows, width), lambda: (0, 0))],
        [],
        0,
        parts * 32 * width * 2,
        "sums",
    )
    weights = exchange(weight_rows)
    grad_bias = jnp.sum(bias_back, axis=(0, 1))

    grad_features = call(
        functools.partial(final_kernel, fanout),
        (hits, bound_back, scattered, grad_pre, w_self, w_neigh),
        [VMEM] * 6,
        pltpu.HBM((nodes, width), f32),
        HBM,
        [pltpu.VMEM((nodes, width), f32), pltpu.SemaphoreType.DMA((blocks,))],
        2 * nodes * bounds * width,
        nodes * width * 10,
        "return_scatter",
    )

    weights = weights[: 2 * width // 16].reshape(2, width, width).astype(f32)
    return (activated, grad_features, grad_hubs, weights[0], weights[1], grad_bias)


def solution(mesh):
    split = P(AXES, None)
    return jax.shard_map(
        body,
        mesh=mesh,
        in_specs=(split, split, P(), P(), P(), split, split, split, split, split),
        out_specs=(split, split, split, P(), P(), P()),
        check_vma=False,
    )
```

```python
import functools

import jax
import jax.numpy as jnp
from jax import lax
from jax.experimental import pallas as pl
from jax.experimental.pallas import tpu as pltpu
from jax.sharding import PartitionSpec as P

AXES = ("row", "col")
LANES = 128
TILE = 256
MOST_VMEM = 60928 * 1024
LESS_VMEM = 8 * 1024 * 1024
NT = (((1,), (1,)), ((), ()))
TN = (((0,), (0,)), ((), ()))
VMEM = pl.BlockSpec(memory_space=pltpu.VMEM)
SMEM = pl.BlockSpec(memory_space=pltpu.SMEM)
HBM = pl.BlockSpec(memory_space=pltpu.HBM)
bf16, f32 = jnp.bfloat16, jnp.float32


def params(limit):
    return pltpu.CompilerParams(vmem_limit_bytes=limit)


def cost(flops, moved):
    return pl.CostEstimate(flops=int(flops), bytes_accessed=int(moved), transcendentals=0)


def along_rows(index_row):
    count = index_row.shape[1]
    return jnp.transpose(jnp.broadcast_to(index_row, (LANES, count))).astype(jnp.int16)


def hits_by_row(columns, first, width):
    rows = columns[0].shape[0]
    lane = lax.broadcasted_iota(jnp.int32, (rows, LANES), 1).astype(jnp.int16)
    one = jnp.ones((rows, LANES), bf16)
    zero = jnp.zeros((rows, LANES), bf16)
    tiles = []
    for start in range(first, first + width, LANES):
        here = lane + jnp.int16(start)
        total = None
        for column in columns:
            hit = jnp.where(column == here, one, zero)
            total = hit if total is None else total + hit
        tiles.append(total)
    return jnp.concatenate(tiles, axis=1) if len(tiles) > 1 else tiles[0]


def hits_by_column(index_rows, first, height):
    count = index_rows[0].shape[1]
    down = lax.broadcasted_iota(jnp.int32, (height, count), 0).astype(jnp.int16)
    one = jnp.ones((height, count), bf16)
    zero = jnp.zeros((height, count), bf16)
    total = None
    for row in index_rows:
        entry = jnp.broadcast_to(row - first, (16, count)).astype(jnp.int16)
        entry = jnp.broadcast_to(entry[None], (height // 16, 16, count)).reshape(height, count)
        hit = jnp.where(entry == down, one, zero)
        total = hit if total is None else total + hit
    return total


def dot(a, b, dims=(((1,), (0,)), ((), ()))):
    return lax.dot_general(a, b, dims, preferred_element_type=f32)


def index_rows(ref, start, count):
    return [ref[j : j + 1, pl.ds(start, count)] for j in range(ref.shape[0])]


def pick_kernel(send_ref, feat_ref, out_ref):
    parts, slots, width = out_ref.shape
    total = send_ref.shape[1]
    step = min(512, total)
    for start in range(0, total, step):
        column = along_rows(send_ref[:, start : start + step])
        picked = dot(hits_by_row([column], 0, feat_ref.shape[0]), feat_ref[...])
        out_ref[start // slots : (start + step) // slots] = picked.astype(bf16).reshape(step // slots, slots, width)


def chain_kernel(*refs):
    out_ref = refs[-1]
    count = refs[0].shape[0]
    for place, ref in enumerate(refs[:-1]):
        out_ref[place * count : (place + 1) * count, :] = ref[...]


def hub_place(hub, row, col, rows, cols, hub_rows):
    owner = lax.div(hub, jnp.int32(hub_rows))
    owner_row = lax.div(owner, jnp.int32(cols))
    down = row - owner_row
    along = col - (owner - owner_row * cols)
    down = jnp.where(down < 0, down + rows, down)
    along = jnp.where(along < 0, along + cols, along)
    return (down * cols + along) * hub_rows + (hub - owner * hub_rows)


def local_kernel(
    rows, cols, hub_rows, row_ref, col_ref, local_ref, hub_ref, remote_ref, feat_ref, sum_ref, by_row_ref, by_col_ref
):
    nodes = feat_ref.shape[0]
    columns = [along_rows(row) for row in index_rows(local_ref, 0, TILE)]
    total = None
    for first in range(0, nodes, TILE):
        part = dot(hits_by_row(columns, first, TILE), feat_ref[first : first + TILE, :])
        total = part if total is None else total + part
    sum_ref[...] = total
    hub_index = [hub_place(hub, row_ref[0], col_ref[0], rows, cols, hub_rows) for hub in index_rows(hub_ref, 0, TILE)]
    split = rows * cols * hub_rows
    for index, low, high in (
        (hub_index, 0, split),
        (index_rows(remote_ref, 0, TILE), split, by_row_ref.shape[1]),
    ):
        columns = [along_rows(row) for row in index]
        for first in range(low, high, TILE):
            by_row_ref[:, first : first + TILE] = hits_by_row(columns, first - low, TILE)
            by_col_ref[first : first + TILE, :] = hits_by_column(index, first - low, TILE)


def middle_kernel(rows, cols, fanout, row_ref, *refs):
    hub_refs, refs = refs[:rows], refs[rows:]
    (feat_hbm, sum_hbm, by_row_hbm, by_col_hbm, cot_hbm, bound_ref, ws_ref, wn_ref, bias_ref) = refs[:9]
    (act_hbm, grad_hbm, bound_out, own_out) = refs[9:13]
    sends = refs[13 : 12 + rows]
    (feat, sums, by_row, by_col, cot, act, grad_all, mean_all, terms, sem, col_sem, out_sem) = refs[12 + rows :]
    nodes, width = feat.shape
    parts, slots, _ = bound_ref.shape
    hub_count = hub_refs[0].shape[0] * rows
    hub_rows = hub_count // parts
    slab = hub_rows + 16
    copy_rows = 2 * TILE
    loads = []
    for part in range(nodes // copy_rows):
        here = slice(part * copy_rows, (part + 1) * copy_rows)
        group = []
        for which, (source, target) in enumerate(
            ((by_row_hbm, by_row), (sum_hbm, sums), (feat_hbm, feat), (cot_hbm, cot))
        ):
            load = pltpu.make_async_copy(source.at[here, :], target.at[here, :], sem.at[which, part])
            load.start()
            group.append(load)
        loads.append(group)
    col_load = pltpu.make_async_copy(by_col_hbm, by_col, col_sem)
    col_load.start()
    hubs = jnp.concatenate([ref[...] for ref in hub_refs], axis=0)
    bound = bound_ref[...].reshape(parts * slots, width)
    stores = []
    bias_total = jnp.zeros((1, width), f32)
    for block in range(nodes // TILE):
        here = slice(block * TILE, (block + 1) * TILE)
        if block * TILE % copy_rows == 0:
            for load in loads[block * TILE // copy_rows]:
                load.wait()
        total = sums[here, :] + dot(by_row[here, :hub_count], hubs) + dot(by_row[here, hub_count:], bound)
        mean = (total / fanout).astype(bf16)
        mean_all[here, :] = mean
        pre = dot(feat[here, :], ws_ref[...]) + dot(mean, wn_ref[...]) + bias_ref[...]
        sig = jax.nn.sigmoid(pre)
        act[here, :] = (pre * sig).astype(bf16)
        grad = (cot[here, :].astype(f32) * sig * (1.0 + pre * (1.0 - sig))).astype(bf16)
        grad_all[here, :] = grad
        bias_total = bias_total + jnp.sum(grad.astype(f32), axis=0, keepdims=True)
        for which, (source, target) in enumerate(((act, act_hbm), (grad_all, grad_hbm))):
            store = pltpu.make_async_copy(source.at[here, :], target.at[here, :], out_sem.at[which, block])
            store.start()
            stores.append(store)
    grad = grad_all[...]
    col_load.wait()
    hub_terms = dot(by_col[:hub_count, :], grad)
    terms[:, :hub_rows, :] = hub_terms.reshape(parts, hub_rows, width)
    per = width // 16
    terms[:per, hub_rows:, :] = dot(feat[...], grad, TN).reshape(per, 16, width)
    terms[per : 2 * per, hub_rows:, :] = dot(mean_all[...], grad, TN).reshape(per, 16, width)
    if parts > 2 * per:
        terms[2 * per :, hub_rows:, :] = jnp.zeros((parts - 2 * per, 16, width), f32)
    bias_rows = high_low(bias_total)
    row = row_ref[0]
    for step, out in enumerate((own_out,) + tuple(sends)):
        target = row + step
        target = jnp.where(target >= rows, target - rows, target)
        place = (rows - step) % rows * cols
        chunk = jnp.concatenate(
            [terms[place : place + cols, :hub_rows, :], terms[pl.ds(target * cols, cols), hub_rows:, :]], axis=1
        )
        out[: cols * slab, :] = chunk.reshape(cols * slab, width).astype(out.dtype)
        out[cols * slab :, :] = bias_rows.astype(out.dtype)
    bound_out[...] = dot(by_col[hub_count:, :], grad).astype(bf16).reshape(parts, slots, width)
    for store in stores:
        store.wait()


def high_low(row):
    high = row.astype(bf16).astype(f32)
    place = lax.broadcasted_iota(jnp.int32, (16, row.shape[1]), 0)
    return jnp.where(place == 0, high, jnp.where(place == 1, row - high, 0.0))


def row_join_kernel(cols, slab, col_ref, own_ref, *refs):
    got, outs, total = refs[: -cols - 1], refs[-cols - 1 : -1], refs[-1]
    width = own_ref.shape[1]
    count = cols * slab
    whole = own_ref[...]
    for ref in got:
        whole = whole + ref[...].astype(f32)
    total[...] = whole[:count].reshape(cols, slab, width)
    bias_rows = high_low(jnp.sum(whole[count:], axis=0, keepdims=True))
    for step, out in enumerate(outs):
        target = col_ref[0] + step
        target = jnp.where(target >= cols, target - cols, target)
        out[: slab - 16, :] = total[(cols - step) % cols, : slab - 16, :].astype(out.dtype)
        out[slab - 16 : slab, :] = total[target, slab - 16 :, :].astype(out.dtype)
        out[slab:, :] = bias_rows.astype(out.dtype)


def col_join_kernel(fanout, hub_rows, own_ref, *refs):
    got, (wn_ref, weight_ref, hub_ref, bias_ref) = refs[:-4], refs[-4:]
    whole = own_ref[...]
    for ref in got:
        whole = whole + ref[...].astype(f32)
    hub = whole[:hub_rows]
    high = hub.astype(bf16)
    low = (hub - high.astype(f32)).astype(bf16)
    hub_ref[...] = (dot(high, wn_ref[...], NT) + dot(low, wn_ref[...], NT)) / fanout
    weight_ref[...] = whole[hub_rows : hub_rows + 16].astype(bf16)
    bias_ref[...] = jnp.sum(whole[hub_rows + 16 :], axis=0, keepdims=True)


def place_kernel(count, at_ref, *refs):
    out_ref = refs[-1]
    size = out_ref.shape[0] // count
    for step, ref in enumerate(refs[:-1]):
        source = at_ref[0] - step
        source = jnp.where(source < 0, source + count, source)
        out_ref[pl.ds(pl.multiple_of(source * size, size), size), :] = ref[...]


def weights_kernel(count, at_ref, *refs):
    got, (self_ref, neigh_ref, whole) = refs[:-3], refs[-3:]
    place_kernel(count, at_ref, *(got + (whole,)))
    width = self_ref.shape[0]
    self_ref[...] = whole[:width, :].astype(f32)
    neigh_ref[...] = whole[width : 2 * width, :].astype(f32)


def scatter_kernel(local_ref, grad_ref, out_ref):
    height = out_ref.shape[0]
    first = pl.program_id(0) * height
    total = None
    for start in range(0, grad_ref.shape[0], TILE):
        rows = index_rows(local_ref, start, TILE)
        part = dot(hits_by_column(rows, first, height), grad_ref[start : start + TILE, :])
        total = part if total is None else total + part
    out_ref[...] = total


def final_kernel(fanout, send_ref, bound_ref, scat_ref, grad_ref, ws_ref, wn_ref, out_ref):
    height, width = out_ref.shape
    first = pl.program_id(0) * height
    count = send_ref.shape[1]
    returned = bound_ref[...].reshape(count, width)
    total = scat_ref[...]
    for start in range(0, count, 512):
        stop = min(count, start + 512)
        hits = hits_by_column([send_ref[:, start:stop]], first, height)
        total = total + dot(hits, returned[start:stop])
    out_ref[...] = dot(grad_ref[...], ws_ref[...], NT) + dot((total / fanout).astype(bf16), wn_ref[...], NT)


def call(kernel, ins, in_specs, outs, out_specs, name, grid=(), scratch=(), flops=0, moved=0, limit=LESS_VMEM):
    return pl.pallas_call(
        kernel,
        grid=grid,
        in_specs=in_specs,
        out_specs=out_specs,
        out_shape=outs,
        scratch_shapes=scratch,
        compiler_params=params(limit),
        cost_estimate=cost(flops, moved),
        name=name,
    )(*ins)


def whole_block(shape):
    return pl.BlockSpec(shape, lambda *_: (0,) * len(shape))


def body(
    features,
    hub_features,
    w_self,
    w_neigh,
    out_bias,
    local_edges,
    hub_edges,
    remote_edges,
    send_rows,
    cotangent,
):
    nodes, width = features.shape
    hub_rows = hub_features.shape[0]
    rows, cols = lax.axis_size("row"), lax.axis_size("col")
    parts = rows * cols
    slots = send_rows.shape[1] // parts
    slab = hub_rows + 16
    hubs, bounds = parts * hub_rows, parts * slots
    fanout = float(local_edges.shape[1] + hub_edges.shape[1] + remote_edges.shape[1])
    local_t, hub_t, remote_t = local_edges.T, hub_edges.T, remote_edges.T
    bias = out_bias.reshape(1, width)
    row = lax.axis_index("row").astype(jnp.int32).reshape(1)
    col = lax.axis_index("col").astype(jnp.int32).reshape(1)
    shape = jax.ShapeDtypeStruct

    def exchange(value):
        return lax.all_to_all(value, AXES, split_axis=0, concat_axis=0, tiled=True)

    def shifted(value, axis, step):
        count = lax.axis_size(axis)
        return lax.ppermute(value, axis, [(i, (i + step) % count) for i in range(count)])

    near_hubs = [hub_features] + [shifted(hub_features, "col", step) for step in range(1, cols)]
    bound_send = call(
        pick_kernel,
        (send_rows, features),
        [VMEM, VMEM],
        shape((parts, slots, width), bf16),
        whole_block((parts, slots, width)),
        "pick_rows",
        limit=MOST_VMEM,
        flops=2 * bounds * nodes * width,
        moved=nodes * width * 2,
    )
    bound_send, features = lax.optimization_barrier((bound_send, features))
    bound_all = exchange(bound_send)
    row_hubs = call(
        chain_kernel,
        near_hubs,
        [VMEM] * cols,
        shape((cols * hub_rows, width), bf16),
        whole_block((cols * hub_rows, width)),
        "chain_hubs",
        moved=cols * hub_rows * width * 4,
    )
    all_hubs = [row_hubs] + [shifted(row_hubs, "row", step) for step in range(1, rows)]

    block = TILE
    table = hubs + bounds
    local_sum, by_row, by_col = call(
        functools.partial(local_kernel, rows, cols, hub_rows),
        (row, col, local_t, hub_t, remote_t, features),
        [SMEM, SMEM]
        + [pl.BlockSpec((edges.shape[0], block), lambda i: (0, i)) for edges in (local_t, hub_t, remote_t)]
        + [whole_block((nodes, width))],
        [shape((nodes, width), f32), shape((nodes, table), bf16), shape((table, nodes), bf16)],
        [
            pl.BlockSpec((block, width), lambda i: (i, 0)),
            pl.BlockSpec((block, table), lambda i: (i, 0)),
            pl.BlockSpec((table, block), lambda i: (0, i)),
        ],
        "local_gather",
        limit=MOST_VMEM,
        grid=(nodes // block,),
        flops=8 * nodes * nodes * width,
        moved=nodes * table * 4,
    )

    send_shape = (cols * slab + 16, width)
    copies = nodes // (2 * TILE)
    activated, grad_pre, bound_terms, own, *sends = call(
        functools.partial(middle_kernel, rows, cols, fanout),
        [row] + all_hubs + [features, local_sum, by_row, by_col, cotangent, bound_all, w_self, w_neigh, bias],
        [SMEM] + [VMEM] * rows + [HBM] * 5 + [VMEM] * 4,
        [shape((nodes, width), bf16)] * 2
        + [shape((parts, slots, width), bf16), shape(send_shape, f32)]
        + [shape(send_shape, bf16)] * (rows - 1),
        [HBM] * 2 + [whole_block((parts, slots, width))] + [whole_block(send_shape)] * rows,
        "activate",
        limit=MOST_VMEM,
        scratch=[
            pltpu.VMEM((nodes, width), bf16),
            pltpu.VMEM((nodes, width), f32),
            pltpu.VMEM((nodes, table), bf16),
            pltpu.VMEM((table, nodes), bf16),
            pltpu.VMEM((nodes, width), bf16),
            pltpu.VMEM((nodes, width), bf16),
            pltpu.VMEM((nodes, width), bf16),
            pltpu.VMEM((nodes, width), bf16),
            pltpu.VMEM((parts, slab, width), f32),
            pltpu.SemaphoreType.DMA((4, copies)),
            pltpu.SemaphoreType.DMA,
            pltpu.SemaphoreType.DMA((2, nodes // TILE)),
        ],
        flops=4 * nodes * table * width,
        moved=nodes * table * 4,
    )
    got = [shifted(value, "row", step + 1) for step, value in enumerate(sends)]
    bound_back = exchange(bound_terms)

    own, *sends = call(
        functools.partial(row_join_kernel, cols, slab),
        [col, own] + got,
        [SMEM] + [VMEM] * rows,
        [shape((slab + 16, width), f32)] + [shape((slab + 16, width), bf16)] * (cols - 1),
        [whole_block((slab + 16, width))] * cols,
        "row_join",
        scratch=[pltpu.VMEM((cols, slab, width), f32)],
        moved=rows * send_shape[0] * width * 2,
    )
    got = [shifted(value, "col", step + 1) for step, value in enumerate(sends)]
    weight_rows, grad_hubs, grad_bias = call(
        functools.partial(col_join_kernel, fanout, hub_rows),
        [own] + got + [w_neigh],
        [VMEM] * (cols + 1),
        [shape((16, width), bf16), shape((hub_rows, width), f32), shape((1, width), f32)],
        [whole_block((16, width)), whole_block((hub_rows, width)), whole_block((1, width))],
        "col_join",
        moved=cols * (slab + 16) * width * 2,
    )
    near = [weight_rows] + [shifted(weight_rows, "col", step) for step in range(1, cols)]
    row_weights = call(
        functools.partial(place_kernel, cols),
        [col] + near,
        [SMEM] + [VMEM] * cols,
        shape((cols * 16, width), bf16),
        whole_block((cols * 16, width)),
        "place_weights",
        moved=cols * 16 * width * 4,
    )
    far = [row_weights] + [shifted(row_weights, "row", step) for step in range(1, rows)]
    grad_w_self, grad_w_neigh = call(
        functools.partial(weights_kernel, rows),
        [row] + far,
        [SMEM] + [VMEM] * rows,
        [shape((width, width), f32)] * 2,
        [whole_block((width, width))] * 2,
        "weights",
        scratch=[pltpu.VMEM((parts * 16, width), bf16)],
        moved=4 * width * width * 4,
    )

    scattered = call(
        scatter_kernel,
        (local_t, grad_pre),
        [whole_block(local_t.shape), whole_block((nodes, width))],
        shape((nodes, width), f32),
        pl.BlockSpec((block, width), lambda i: (i, 0)),
        "local_scatter",
        limit=MOST_VMEM,
        grid=(nodes // block,),
        flops=8 * nodes * nodes * width,
        moved=nodes * width * 6,
    )
    height = 2 * TILE
    by_height = pl.BlockSpec((height, width), lambda i: (i, 0))
    grad_features = call(
        functools.partial(final_kernel, fanout),
        (send_rows, bound_back, scattered, grad_pre, w_self, w_neigh),
        [whole_block(send_rows.shape), whole_block((parts, slots, width)), by_height, by_height]
        + [whole_block((width, width))] * 2,
        shape((nodes, width), f32),
        by_height,
        "return_scatter",
        limit=MOST_VMEM,
        grid=(nodes // height,),
        flops=2 * nodes * bounds * width,
        moved=nodes * width * 10,
    )
    return (activated, grad_features, grad_hubs, grad_w_self, grad_w_neigh, grad_bias.reshape(width))


def solution(mesh):
    split = P(AXES, None)
    return jax.shard_map(
        body,
        mesh=mesh,
        in_specs=(split, split, P(), P(), P(), split, split, split, split, split),
        out_specs=(split, split, split, P(), P(), P()),
        check_vma=False,
    )
```

```python
import functools

import jax
import jax.numpy as jnp
from jax import lax
from jax.experimental import pallas as pl
from jax.experimental.pallas import tpu as pltpu
from jax.sharding import PartitionSpec as P

AXES = ("row", "col")
LANES = 128
TILE = 256
MOST_VMEM = 60928 * 1024
LESS_VMEM = 8 * 1024 * 1024
NT = (((1,), (1,)), ((), ()))
TN = (((0,), (0,)), ((), ()))
VMEM = pl.BlockSpec(memory_space=pltpu.VMEM)
SMEM = pl.BlockSpec(memory_space=pltpu.SMEM)
HBM = pl.BlockSpec(memory_space=pltpu.HBM)
bf16, f32 = jnp.bfloat16, jnp.float32


def params(limit):
    return pltpu.CompilerParams(vmem_limit_bytes=limit)


def cost(flops, moved):
    return pl.CostEstimate(flops=int(flops), bytes_accessed=int(moved), transcendentals=0)


def along_rows(index_row):
    count = index_row.shape[1]
    return jnp.transpose(jnp.broadcast_to(index_row, (LANES, count))).astype(jnp.int16)


def hits_by_row(columns, first, width):
    rows = columns[0].shape[0]
    lane = lax.broadcasted_iota(jnp.int32, (rows, LANES), 1).astype(jnp.int16)
    one = jnp.ones((rows, LANES), bf16)
    zero = jnp.zeros((rows, LANES), bf16)
    tiles = []
    for start in range(first, first + width, LANES):
        here = lane + jnp.int16(start)
        total = None
        for column in columns:
            hit = jnp.where(column == here, one, zero)
            total = hit if total is None else total + hit
        tiles.append(total)
    return jnp.concatenate(tiles, axis=1) if len(tiles) > 1 else tiles[0]


def hits_by_column(index_rows, first, height):
    count = index_rows[0].shape[1]
    down = lax.broadcasted_iota(jnp.int32, (height, count), 0).astype(jnp.int16)
    one = jnp.ones((height, count), bf16)
    zero = jnp.zeros((height, count), bf16)
    total = None
    for row in index_rows:
        entry = jnp.broadcast_to(row - first, (16, count)).astype(jnp.int16)
        entry = jnp.broadcast_to(entry[None], (height // 16, 16, count)).reshape(height, count)
        hit = jnp.where(entry == down, one, zero)
        total = hit if total is None else total + hit
    return total


def dot(a, b, dims=(((1,), (0,)), ((), ()))):
    return lax.dot_general(a, b, dims, preferred_element_type=f32)


def index_rows(ref, start, count):
    return [ref[j : j + 1, pl.ds(start, count)] for j in range(ref.shape[0])]


def pick_kernel(send_ref, feat_ref, hub_ref, out_ref):
    parts, slab, width = out_ref.shape
    hub_rows = hub_ref.shape[0]
    slots = slab - hub_rows
    total = send_ref.shape[1]
    step = min(512, total)
    for start in range(0, total, step):
        column = along_rows(send_ref[:, start : start + step])
        picked = dot(hits_by_row([column], 0, feat_ref.shape[0]), feat_ref[...])
        out_ref[start // slots : (start + step) // slots, :slots, :] = (
            picked.astype(bf16).reshape(step // slots, slots, width)
        )
    out_ref[:, slots:, :] = jnp.broadcast_to(hub_ref[...][None], (parts, hub_rows, width))


def local_kernel(split, local_ref, remote_ref, hub_ref, feat_ref, sum_ref, by_row_ref, by_col_ref):
    nodes = feat_ref.shape[0]
    columns = [along_rows(row) for row in index_rows(local_ref, 0, TILE)]
    total = None
    for first in range(0, nodes, TILE):
        part = dot(hits_by_row(columns, first, TILE), feat_ref[first : first + TILE, :])
        total = part if total is None else total + part
    sum_ref[...] = total
    for ref, low, high in ((remote_ref, 0, split), (hub_ref, split, by_row_ref.shape[1])):
        index = index_rows(ref, 0, TILE)
        columns = [along_rows(row) for row in index]
        for first in range(low, high, TILE):
            by_row_ref[:, first : first + TILE] = hits_by_row(columns, first - low, TILE)
            by_col_ref[first : first + TILE, :] = hits_by_column(index, first - low, TILE)


def middle_kernel(
    scale,
    slots,
    feat_hbm,
    sum_hbm,
    by_row_hbm,
    by_col_hbm,
    cot_hbm,
    table_ref,
    ws_ref,
    wn_ref,
    bias_ref,
    act_hbm,
    grad_hbm,
    pay_ref,
    feat,
    sums,
    by_row,
    by_col,
    cot,
    act,
    grad_all,
    mean_all,
    block_sem,
    half_sem,
    col_sem,
    out_sem,
):
    nodes, width = feat.shape
    parts, slab, _ = table_ref.shape
    hub_rows = slab - slots
    bounds, hubs = parts * slots, parts * hub_rows
    blocks = nodes // TILE
    halves = 2

    def here(block):
        return slice(block * TILE, (block + 1) * TILE)

    def loads(block):
        at = here(block)
        copies = [
            pltpu.make_async_copy(by_row_hbm.at[at, :], by_row.at[at, :], block_sem.at[0, block]),
            pltpu.make_async_copy(sum_hbm.at[at, :], sums.at[at, :], block_sem.at[1, block]),
        ]
        if block % (blocks // halves) == 0:
            half = block // (blocks // halves)
            at = slice(half * (nodes // halves), (half + 1) * (nodes // halves))
            copies.append(pltpu.make_async_copy(feat_hbm.at[at, :], feat.at[at, :], half_sem.at[0, half]))
            copies.append(pltpu.make_async_copy(cot_hbm.at[at, :], cot.at[at, :], half_sem.at[1, half]))
        return copies

    coming = [loads(block) for block in range(blocks)]
    for group in coming:
        for copy in group:
            copy.start()
    col_load = pltpu.make_async_copy(by_col_hbm, by_col, col_sem)
    col_load.start()
    table = jnp.concatenate(
        [table_ref[:, :slots, :].reshape(bounds, width), table_ref[:, slots:, :].reshape(hubs, width)], axis=0
    )
    stores = []
    bias_total = jnp.zeros((1, width), f32)
    total = None
    for block in range(blocks + 1):
        following = None
        if block < blocks:
            for copy in coming[block]:
                copy.wait()
            at = here(block)
            following = sums[at, :] + dot(by_row[at, :], table)
        if block > 0:
            at = here(block - 1)
            mean = (total * scale).astype(bf16)
            mean_all[at, :] = mean
            pre = dot(feat[at, :], ws_ref[...]) + dot(mean, wn_ref[...]) + bias_ref[...]
            sig = 0.5 * jnp.tanh(0.5 * pre) + 0.5
            active = pre * sig
            act[at, :] = active.astype(bf16)
            grad = (cot[at, :].astype(f32) * (sig + active * (1.0 - sig))).astype(bf16)
            grad_all[at, :] = grad
            bias_total = bias_total + jnp.sum(grad.astype(f32), axis=0, keepdims=True)
            for which, (source, target) in enumerate(((act, act_hbm), (grad_all, grad_hbm))):
                store = pltpu.make_async_copy(source.at[at, :], target.at[at, :], out_sem.at[which, block - 1])
                store.start()
                stores.append(store)
        total = following
    grad = grad_all[...]
    holders = 2 * width // 16
    per = holders // 2
    for which, source in enumerate((feat, mean_all)):
        pay_ref[which * per : (which + 1) * per, slab : slab + 16, :] = (
            dot(source[...], grad, TN).astype(bf16).reshape(per, 16, width)
        )
    if parts > holders:
        pay_ref[holders:, slab : slab + 16, :] = jnp.zeros((parts - holders, 16, width), bf16)
    pay_ref[:, slab + 16 :, :] = jnp.broadcast_to(high_low(bias_total).astype(bf16)[None], (parts, 8, width))
    col_load.wait()
    pay_ref[:, :slots, :] = dot(by_col[:bounds, :], grad).astype(bf16).reshape(parts, slots, width)
    pay_ref[:, slots:slab, :] = dot(by_col[bounds:, :], grad).astype(bf16).reshape(parts, hub_rows, width)
    for store in stores:
        store.wait()


def high_low(row):
    high = row.astype(bf16).astype(f32)
    place = lax.broadcasted_iota(jnp.int32, (8, row.shape[1]), 0)
    return jnp.where(place == 0, high, jnp.where(place == 1, row - high, 0.0))


def sums_kernel(scale, slots, hub_rows, back_ref, wn_ref, weight_ref, bias_ref, hub_ref):
    slab = slots + hub_rows
    total = jnp.sum(back_ref[:, slots:, :].astype(f32), axis=0)
    weight_ref[...] = jnp.broadcast_to(total[hub_rows : hub_rows + 16].astype(bf16)[None], weight_ref.shape)
    bias_ref[...] = jnp.sum(total[hub_rows + 16 :], axis=0, keepdims=True)
    hub = total[:hub_rows]
    high = hub.astype(bf16)
    low = (hub - high.astype(f32)).astype(bf16)
    hub_ref[...] = (dot(high, wn_ref[...], NT) + dot(low, wn_ref[...], NT)) * scale


def scatter_kernel(local_ref, grad_ref, out_ref):
    height = out_ref.shape[0]
    first = pl.program_id(0) * height
    total = None
    for start in range(0, grad_ref.shape[0], TILE):
        rows = index_rows(local_ref, start, TILE)
        part = dot(hits_by_column(rows, first, height), grad_ref[start : start + TILE, :])
        total = part if total is None else total + part
    out_ref[...] = total


def final_kernel(scale, slots, send_ref, back_ref, scat_ref, grad_ref, ws_ref, wn_ref, out_ref):
    height, width = out_ref.shape
    first = pl.program_id(0) * height
    count = send_ref.shape[1]
    returned = back_ref[:, :slots, :].reshape(count, width)
    total = scat_ref[...]
    for start in range(0, count, 512):
        stop = min(count, start + 512)
        hits = hits_by_column([send_ref[:, start:stop]], first, height)
        total = total + dot(hits, returned[start:stop])
    out_ref[...] = dot(grad_ref[...], ws_ref[...], NT) + dot((total * scale).astype(bf16), wn_ref[...], NT)


def call(
    kernel, ins, in_specs, outs, out_specs, name, grid=(), scratch=(), flops=0, moved=0, limit=LESS_VMEM
):
    return pl.pallas_call(
        kernel,
        grid=grid,
        in_specs=in_specs,
        out_specs=out_specs,
        out_shape=outs,
        scratch_shapes=scratch,
        compiler_params=params(limit),
        cost_estimate=cost(flops, moved),
        name=name,
    )(*ins)


def whole_block(shape):
    return pl.BlockSpec(shape, lambda *_: (0,) * len(shape))


def body(
    features,
    hub_features,
    w_self,
    w_neigh,
    out_bias,
    local_edges,
    hub_edges,
    remote_edges,
    send_rows,
    cotangent,
):
    nodes, width = features.shape
    hub_rows = hub_features.shape[0]
    parts = lax.axis_size(AXES)
    slots = send_rows.shape[1] // parts
    slab = slots + hub_rows
    pay = slab + 24
    table = parts * slab
    scale = 1.0 / (local_edges.shape[1] + hub_edges.shape[1] + remote_edges.shape[1])
    local_t, hub_t, remote_t = local_edges.T, hub_edges.T, remote_edges.T
    bias = out_bias.reshape(1, width)
    shape = jax.ShapeDtypeStruct

    def exchange(value):
        return lax.all_to_all(value, AXES, split_axis=0, concat_axis=0, tiled=True)

    sending = call(
        pick_kernel,
        (send_rows, features, hub_features),
        [VMEM, VMEM, VMEM],
        shape((parts, slab, width), bf16),
        whole_block((parts, slab, width)),
        "pick_rows",
        limit=MOST_VMEM,
        flops=2 * parts * slots * nodes * width,
        moved=nodes * width * 2,
    )
    sending, features = lax.optimization_barrier((sending, features))
    received = exchange(sending)

    block = TILE
    local_sum, by_row, by_col = call(
        functools.partial(local_kernel, parts * slots),
        (local_t, remote_t, hub_t, features),
        [pl.BlockSpec((edges.shape[0], block), lambda i: (0, i)) for edges in (local_t, remote_t, hub_t)]
        + [whole_block((nodes, width))],
        [shape((nodes, width), f32), shape((nodes, table), bf16), shape((table, nodes), bf16)],
        [
            pl.BlockSpec((block, width), lambda i: (i, 0)),
            pl.BlockSpec((block, table), lambda i: (i, 0)),
            pl.BlockSpec((table, block), lambda i: (0, i)),
        ],
        "local_gather",
        limit=MOST_VMEM,
        grid=(nodes // block,),
        flops=8 * nodes * nodes * width,
        moved=nodes * table * 4,
    )

    activated, grad_pre, terms = call(
        functools.partial(middle_kernel, scale, slots),
        [features, local_sum, by_row, by_col, cotangent, received, w_self, w_neigh, bias],
        [HBM] * 5 + [VMEM] * 4,
        [shape((nodes, width), bf16)] * 2 + [shape((parts, pay, width), bf16)],
        [HBM] * 2 + [whole_block((parts, pay, width))],
        "activate",
        limit=MOST_VMEM,
        scratch=[
            pltpu.VMEM((nodes, width), bf16),
            pltpu.VMEM((nodes, width), f32),
            pltpu.VMEM((nodes, table), bf16),
            pltpu.VMEM((table, nodes), bf16),
            pltpu.VMEM((nodes, width), bf16),
            pltpu.VMEM((nodes, width), bf16),
            pltpu.VMEM((nodes, width), bf16),
            pltpu.VMEM((nodes, width), bf16),
            pltpu.SemaphoreType.DMA((2, nodes // TILE)),
            pltpu.SemaphoreType.DMA((2, 2)),
            pltpu.SemaphoreType.DMA,
            pltpu.SemaphoreType.DMA((2, nodes // TILE)),
        ],
        flops=4 * nodes * table * width,
        moved=nodes * table * 4,
    )
    back = exchange(terms)

    scattered = call(
        scatter_kernel,
        (local_t, grad_pre),
        [whole_block(local_t.shape), whole_block((nodes, width))],
        shape((nodes, width), f32),
        pl.BlockSpec((block, width), lambda i: (i, 0)),
        "local_scatter",
        limit=MOST_VMEM,
        grid=(nodes // block,),
        flops=8 * nodes * nodes * width,
        moved=nodes * width * 6,
    )
    weight_rows, grad_bias, grad_hubs = call(
        functools.partial(sums_kernel, scale, slots, hub_rows),
        (back, w_neigh),
        [VMEM, VMEM],
        [shape((parts, 16, width), bf16), shape((1, width), f32), shape((hub_rows, width), f32)],
        [whole_block((parts, 16, width)), whole_block((1, width)), whole_block((hub_rows, width))],
        "sums",
        limit=MOST_VMEM,
        moved=parts * (pay + 16) * width * 2,
    )
    weights = exchange(weight_rows)

    height = 2 * TILE
    by_height = pl.BlockSpec((height, width), lambda i: (i, 0))
    grad_features = call(
        functools.partial(final_kernel, scale, slots),
        (send_rows, back, scattered, grad_pre, w_self, w_neigh),
        [whole_block(send_rows.shape), whole_block((parts, pay, width)), by_height, by_height]
        + [whole_block((width, width))] * 2,
        shape((nodes, width), f32),
        by_height,
        "return_scatter",
        limit=MOST_VMEM,
        grid=(nodes // height,),
        flops=2 * nodes * parts * slots * width,
        moved=nodes * width * 10,
    )
    weights = weights[: 2 * width // 16].reshape(2, width, width).astype(f32)
    return (activated, grad_features, grad_hubs, weights[0], weights[1], grad_bias.reshape(width))


def solution(mesh):
    split = P(AXES, None)
    return jax.shard_map(
        body,
        mesh=mesh,
        in_specs=(split, split, P(), P(), P(), split, split, split, split, split),
        out_specs=(split, split, split, P(), P(), P()),
        check_vma=False,
    )
```

```python
import functools

import jax
import jax.numpy as jnp
from jax import lax
from jax.experimental import pallas as pl
from jax.experimental.pallas import tpu as pltpu
from jax.sharding import PartitionSpec as P

AXES = ("row", "col")
LANES = 128
TILE = 256
MOST_VMEM = 61952 * 1024
SOME_VMEM = 44 * 1024 * 1024
NT = (((1,), (1,)), ((), ()))
TN = (((0,), (0,)), ((), ()))
VMEM = pl.BlockSpec(memory_space=pltpu.VMEM)
SMEM = pl.BlockSpec(memory_space=pltpu.SMEM)
HBM = pl.BlockSpec(memory_space=pltpu.HBM)
bf16, f32 = jnp.bfloat16, jnp.float32


def params(limit):
    return pltpu.CompilerParams(vmem_limit_bytes=limit)


def cost(flops, moved):
    return pl.CostEstimate(flops=int(flops), bytes_accessed=int(moved), transcendentals=0)


def along_rows(index_row):
    count = index_row.shape[1]
    return jnp.transpose(jnp.broadcast_to(index_row, (LANES, count))).astype(jnp.int16)


def stack_rows(value, height):
    count = value.shape[1]
    return jnp.broadcast_to(value[None], (height // 16, 16, count)).reshape(height, count)


def count_hits(entries, here):
    one, zero = jnp.ones(here.shape, bf16), jnp.zeros(here.shape, bf16)
    total = None
    for entry in entries:
        hit = jnp.where(entry == here, one, zero)
        total = hit if total is None else total + hit
    return total


def hits_by_row(columns, first, width):
    rows = columns[0].shape[0]
    lane = lax.broadcasted_iota(jnp.int32, (16, LANES), 1).astype(jnp.int16)
    tiles = [
        count_hits(columns, stack_rows(lane + jnp.int16(start), rows)) for start in range(first, first + width, LANES)
    ]
    return jnp.concatenate(tiles, axis=1) if len(tiles) > 1 else tiles[0]


def hits_by_column(index_rows, first, height):
    count = index_rows[0].shape[1]
    group = 64
    down = lax.broadcasted_iota(jnp.int32, (group, count), 0).astype(jnp.int16)
    entries = [
        stack_rows(jnp.broadcast_to(row - first, (16, count)).astype(jnp.int16), group) for row in index_rows
    ]
    return jnp.concatenate(
        [count_hits(entries, down + jnp.int16(start)) for start in range(0, height, group)], axis=0
    )


def dot(a, b, dims=(((1,), (0,)), ((), ()))):
    return lax.dot_general(a, b, dims, preferred_element_type=f32)


def index_rows(ref, start, count):
    return [ref[j : j + 1, pl.ds(start, count)] for j in range(ref.shape[0])]


def pick_kernel(send_ref, feat_ref, hub_ref, out_ref):
    parts, slab, width = out_ref.shape
    hub_rows = hub_ref.shape[0]
    slots = slab - hub_rows
    total = send_ref.shape[1]
    step = min(512, total)
    for start in range(0, total, step):
        column = along_rows(send_ref[:, start : start + step])
        picked = dot(hits_by_row([column], 0, feat_ref.shape[0]), feat_ref[...])
        out_ref[start // slots : (start + step) // slots, :slots, :] = (
            picked.astype(bf16).reshape(step // slots, slots, width)
        )
    out_ref[:, slots:, :] = jnp.broadcast_to(hub_ref[...][None], (parts, hub_rows, width))


def local_kernel(local_ref, feat_ref, sum_ref):
    columns = [along_rows(row) for row in index_rows(local_ref, 0, TILE)]
    total = None
    for first in range(0, feat_ref.shape[0], TILE):
        part = dot(hits_by_row(columns, first, TILE), feat_ref[first : first + TILE, :])
        total = part if total is None else total + part
    sum_ref[...] = total


def middle_kernel(
    scale,
    remote_ref,
    hub_ref,
    feat_hbm,
    sum_hbm,
    cot_hbm,
    table_hbm,
    ws_ref,
    wn_ref,
    bias_ref,
    act_hbm,
    grad_hbm,
    pay_ref,
    feat,
    sums,
    cot,
    bound_part,
    hub_part,
    by_col,
    act,
    grad_all,
    mean_all,
    sum_sem,
    half_sem,
    table_sem,
    out_sem,
):
    nodes, width = feat.shape
    parts, slots, _ = bound_part.shape
    hub_rows = hub_part.shape[1]
    slab = slots + hub_rows
    bounds, hubs = parts * slots, parts * hub_rows
    blocks = nodes // TILE
    halves = 2

    def here(block):
        return slice(block * TILE, (block + 1) * TILE)

    table_loads = [
        pltpu.make_async_copy(table_hbm.at[:, :slots, :], bound_part, table_sem.at[0]),
        pltpu.make_async_copy(table_hbm.at[:, slots:, :], hub_part, table_sem.at[1]),
    ]
    for copy in table_loads:
        copy.start()

    def loads(block):
        at = here(block)
        copies = [pltpu.make_async_copy(sum_hbm.at[at, :], sums.at[at, :], sum_sem.at[block])]
        if block % (blocks // halves) == 0:
            half = block // (blocks // halves)
            at = slice(half * (nodes // halves), (half + 1) * (nodes // halves))
            copies.append(pltpu.make_async_copy(feat_hbm.at[at, :], feat.at[at, :], half_sem.at[0, half]))
            copies.append(pltpu.make_async_copy(cot_hbm.at[at, :], cot.at[at, :], half_sem.at[1, half]))
        return copies

    coming = [loads(block) for block in range(blocks)]
    for group in coming:
        for copy in group:
            copy.start()

    def counts(block):
        start = block * TILE
        hits = jnp.concatenate(
            [
                hits_by_column(index_rows(remote_ref, start, TILE), 0, bounds),
                hits_by_column(index_rows(hub_ref, start, TILE), 0, hubs),
            ],
            axis=0,
        )
        by_col[:, here(block)] = hits
        return hits

    hits = counts(0)
    for copy in table_loads:
        copy.wait()
    table = jnp.concatenate([bound_part[...].reshape(bounds, width), hub_part[...].reshape(hubs, width)], axis=0)
    stores = []
    bias_total = jnp.zeros((1, width), f32)
    total = None
    for block in range(blocks + 1):
        following = None
        if block < blocks:
            for copy in coming[block]:
                copy.wait()
            following = sums[here(block), :] + dot(hits, table, TN)
            if block + 1 < blocks:
                hits = counts(block + 1)
        if block > 0:
            at = here(block - 1)
            mean = (total * scale).astype(bf16)
            mean_all[at, :] = mean
            pre = dot(feat[at, :], ws_ref[...]) + dot(mean, wn_ref[...]) + bias_ref[...]
            sig = 0.5 * jnp.tanh(0.5 * pre) + 0.5
            active = pre * sig
            act[at, :] = active.astype(bf16)
            grad = (cot[at, :].astype(f32) * (sig + active * (1.0 - sig))).astype(bf16)
            grad_all[at, :] = grad
            bias_total = bias_total + jnp.sum(grad.astype(f32), axis=0, keepdims=True)
            for which, (source, target) in enumerate(((act, act_hbm), (grad_all, grad_hbm))):
                store = pltpu.make_async_copy(source.at[at, :], target.at[at, :], out_sem.at[which, block - 1])
                store.start()
                stores.append(store)
        total = following
    grad = grad_all[...]
    holders = 2 * width // 16
    per = holders // 2
    for which, source in enumerate((feat, mean_all)):
        pay_ref[which * per : (which + 1) * per, slab : slab + 16, :] = (
            dot(source[...], grad, TN).astype(bf16).reshape(per, 16, width)
        )
    if parts > holders:
        pay_ref[holders:, slab : slab + 16, :] = jnp.zeros((parts - holders, 16, width), bf16)
    pay_ref[:, slab + 16 :, :] = jnp.broadcast_to(high_low(bias_total).astype(bf16)[None], (parts, 8, width))
    pay_ref[:, :slots, :] = dot(by_col[:bounds, :], grad).astype(bf16).reshape(parts, slots, width)
    pay_ref[:, slots:slab, :] = dot(by_col[bounds:, :], grad).astype(bf16).reshape(parts, hub_rows, width)
    for store in stores:
        store.wait()


def high_low(row):
    high = row.astype(bf16).astype(f32)
    place = lax.broadcasted_iota(jnp.int32, (8, row.shape[1]), 0)
    return jnp.where(place == 0, high, jnp.where(place == 1, row - high, 0.0))


def sums_kernel(scale, slots, hub_rows, back_ref, wn_ref, weight_ref, bias_ref, hub_ref):
    slab = slots + hub_rows
    total = jnp.sum(back_ref[:, slots:, :].astype(f32), axis=0)
    weight_ref[...] = jnp.broadcast_to(total[hub_rows : hub_rows + 16].astype(bf16)[None], weight_ref.shape)
    bias_ref[...] = jnp.sum(total[hub_rows + 16 :], axis=0, keepdims=True)
    hub = total[:hub_rows]
    high = hub.astype(bf16)
    low = (hub - high.astype(f32)).astype(bf16)
    hub_ref[...] = (dot(high, wn_ref[...], NT) + dot(low, wn_ref[...], NT)) * scale


def scatter_kernel(local_ref, grad_ref, out_ref):
    height = out_ref.shape[0]
    first = pl.program_id(0) * height
    total = None
    for start in range(0, grad_ref.shape[0], TILE):
        rows = index_rows(local_ref, start, TILE)
        part = dot(hits_by_column(rows, first, height), grad_ref[start : start + TILE, :])
        total = part if total is None else total + part
    out_ref[...] = total


def final_kernel(scale, slots, send_ref, back_ref, scat_ref, grad_ref, ws_ref, wn_ref, out_ref):
    height, width = out_ref.shape
    first = pl.program_id(0) * height
    count = send_ref.shape[1]
    returned = back_ref[:, :slots, :].reshape(count, width)
    total = scat_ref[...]
    for start in range(0, count, 512):
        stop = min(count, start + 512)
        hits = hits_by_column([send_ref[:, start:stop]], first, height)
        total = total + dot(hits, returned[start:stop])
    out_ref[...] = dot(grad_ref[...], ws_ref[...], NT) + dot((total * scale).astype(bf16), wn_ref[...], NT)


def call(
    kernel, ins, in_specs, outs, out_specs, name, grid=(), scratch=(), flops=0, moved=0, limit=SOME_VMEM
):
    return pl.pallas_call(
        kernel,
        grid=grid,
        in_specs=in_specs,
        out_specs=out_specs,
        out_shape=outs,
        scratch_shapes=scratch,
        compiler_params=params(limit),
        cost_estimate=cost(flops, moved),
        name=name,
    )(*ins)


def whole_block(shape):
    return pl.BlockSpec(shape, lambda *_: (0,) * len(shape))


def body(
    features,
    hub_features,
    w_self,
    w_neigh,
    out_bias,
    local_edges,
    hub_edges,
    remote_edges,
    send_rows,
    cotangent,
):
    nodes, width = features.shape
    hub_rows = hub_features.shape[0]
    parts = lax.axis_size(AXES)
    slots = send_rows.shape[1] // parts
    slab = slots + hub_rows
    pay = slab + 24
    table = parts * slab
    scale = 1.0 / (local_edges.shape[1] + hub_edges.shape[1] + remote_edges.shape[1])
    local_t, hub_t, remote_t = local_edges.T, hub_edges.T, remote_edges.T
    bias = out_bias.reshape(1, width)
    shape = jax.ShapeDtypeStruct

    def exchange(value):
        return lax.all_to_all(value, AXES, split_axis=0, concat_axis=0, tiled=True)

    sending = call(
        pick_kernel,
        (send_rows, features, hub_features),
        [VMEM, VMEM, VMEM],
        shape((parts, slab, width), bf16),
        whole_block((parts, slab, width)),
        "pick_rows",
        limit=MOST_VMEM,
        flops=2 * parts * slots * nodes * width,
        moved=nodes * width * 2,
    )
    sending, features = lax.optimization_barrier((sending, features))
    received = exchange(sending)

    block = TILE
    local_sum = call(
        local_kernel,
        (local_t, features),
        [pl.BlockSpec((local_t.shape[0], block), lambda i: (0, i)), whole_block((nodes, width))],
        shape((nodes, width), f32),
        pl.BlockSpec((block, width), lambda i: (i, 0)),
        "local_gather",
        limit=MOST_VMEM,
        grid=(nodes // block,),
        flops=8 * nodes * nodes * width,
        moved=nodes * width * 6,
    )

    activated, grad_pre, terms = call(
        functools.partial(middle_kernel, scale),
        [remote_t, hub_t, features, local_sum, cotangent, received, w_self, w_neigh, bias],
        [VMEM] * 2 + [HBM] * 4 + [VMEM] * 3,
        [shape((nodes, width), bf16)] * 2 + [shape((parts, pay, width), bf16)],
        [HBM] * 2 + [whole_block((parts, pay, width))],
        "activate",
        limit=MOST_VMEM,
        scratch=[
            pltpu.VMEM((nodes, width), bf16),
            pltpu.VMEM((nodes, width), f32),
            pltpu.VMEM((nodes, width), bf16),
            pltpu.VMEM((parts, slots, width), bf16),
            pltpu.VMEM((parts, hub_rows, width), bf16),
            pltpu.VMEM((table, nodes), bf16),
            pltpu.VMEM((nodes, width), bf16),
            pltpu.VMEM((nodes, width), bf16),
            pltpu.VMEM((nodes, width), bf16),
            pltpu.SemaphoreType.DMA((nodes // TILE,)),
            pltpu.SemaphoreType.DMA((2, 2)),
            pltpu.SemaphoreType.DMA((2,)),
            pltpu.SemaphoreType.DMA((2, nodes // TILE)),
        ],
        flops=4 * nodes * table * width,
        moved=nodes * width * 8,
    )
    back = exchange(terms)

    scattered = call(
        scatter_kernel,
        (local_t, grad_pre),
        [whole_block(local_t.shape), whole_block((nodes, width))],
        shape((nodes, width), f32),
        pl.BlockSpec((block, width), lambda i: (i, 0)),
        "local_scatter",
        grid=(nodes // block,),
        flops=8 * nodes * nodes * width,
        moved=nodes * width * 6,
    )
    weight_rows, grad_bias, grad_hubs = call(
        functools.partial(sums_kernel, scale, slots, hub_rows),
        (back, w_neigh),
        [VMEM, VMEM],
        [shape((parts, 16, width), bf16), shape((1, width), f32), shape((hub_rows, width), f32)],
        [whole_block((parts, 16, width)), whole_block((1, width)), whole_block((hub_rows, width))],
        "sums",
        moved=parts * (pay + 16) * width * 2,
    )
    weights = exchange(weight_rows)

    height = 2 * TILE
    by_height = pl.BlockSpec((height, width), lambda i: (i, 0))
    grad_features = call(
        functools.partial(final_kernel, scale, slots),
        (send_rows, back, scattered, grad_pre, w_self, w_neigh),
        [whole_block(send_rows.shape), whole_block((parts, pay, width)), by_height, by_height]
        + [whole_block((width, width))] * 2,
        shape((nodes, width), f32),
        by_height,
        "return_scatter",
        grid=(nodes // height,),
        flops=2 * nodes * parts * slots * width,
        moved=nodes * width * 10,
    )
    weights = weights[: 2 * width // 16].reshape(2, width, width).astype(f32)
    return (activated, grad_features, grad_hubs, weights[0], weights[1], grad_bias.reshape(width))


def solution(mesh):
    split = P(AXES, None)
    return jax.shard_map(
        body,
        mesh=mesh,
        in_specs=(split, split, P(), P(), P(), split, split, split, split, split),
        out_specs=(split, split, split, P(), P(), P()),
        check_vma=False,
    )
```

```python
import functools

import jax
import jax.numpy as jnp
from jax import lax
from jax.experimental import pallas as pl
from jax.experimental.pallas import tpu as pltpu
from jax.sharding import PartitionSpec as P

AXES = ("row", "col")
LANES = 128
TILE = 256
MOST_VMEM = 61952 * 1024
SOME_VMEM = 44 * 1024 * 1024
NT = (((1,), (1,)), ((), ()))
TN = (((0,), (0,)), ((), ()))
VMEM = pl.BlockSpec(memory_space=pltpu.VMEM)
SMEM = pl.BlockSpec(memory_space=pltpu.SMEM)
HBM = pl.BlockSpec(memory_space=pltpu.HBM)
bf16, f32 = jnp.bfloat16, jnp.float32


def params(limit):
    return pltpu.CompilerParams(vmem_limit_bytes=limit)


def cost(flops, moved):
    return pl.CostEstimate(flops=int(flops), bytes_accessed=int(moved), transcendentals=0)


def along_rows(index_row):
    count = index_row.shape[1]
    return jnp.transpose(jnp.broadcast_to(index_row, (LANES, count))).astype(jnp.int16)


def stack_rows(value, height):
    count = value.shape[1]
    return jnp.broadcast_to(value[None], (height // 16, 16, count)).reshape(height, count)


def count_hits(entries, here):
    one, zero = jnp.ones(here.shape, bf16), jnp.zeros(here.shape, bf16)
    total = None
    for entry in entries:
        hit = jnp.where(entry == here, one, zero)
        total = hit if total is None else total + hit
    return total


def hits_by_row(columns, first, width):
    rows = columns[0].shape[0]
    lane = lax.broadcasted_iota(jnp.int32, (16, LANES), 1).astype(jnp.int16)
    tiles = [
        count_hits(columns, stack_rows(lane + jnp.int16(start), rows)) for start in range(first, first + width, LANES)
    ]
    return jnp.concatenate(tiles, axis=1) if len(tiles) > 1 else tiles[0]


def hits_by_column(index_rows, first, height):
    count = index_rows[0].shape[1]
    group = 64
    down = lax.broadcasted_iota(jnp.int32, (group, count), 0).astype(jnp.int16)
    entries = [
        stack_rows(jnp.broadcast_to(row - first, (16, count)).astype(jnp.int16), group) for row in index_rows
    ]
    return jnp.concatenate(
        [count_hits(entries, down + jnp.int16(start)) for start in range(0, height, group)], axis=0
    )


def dot(a, b, dims=(((1,), (0,)), ((), ()))):
    return lax.dot_general(a, b, dims, preferred_element_type=f32)


def index_rows(ref, start, count):
    return [ref[j : j + 1, pl.ds(start, count)] for j in range(ref.shape[0])]


def pick_kernel(send_hbm, feat_hbm, hub_hbm, out_ref, send_ref, feat_ref, hub_ref, small_sem, feat_sem):
    parts, slab, width = out_ref.shape
    nodes = feat_ref.shape[0]
    hub_rows = hub_ref.shape[0]
    slots = slab - hub_rows
    total = send_ref.shape[1]
    step = min(512, total)
    chunk = nodes // 4
    small = [
        pltpu.make_async_copy(send_hbm, send_ref, small_sem.at[0]),
        pltpu.make_async_copy(hub_hbm, hub_ref, small_sem.at[1]),
    ]
    chunks = [slice(k * chunk, (k + 1) * chunk) for k in range(4)]
    loads = [
        pltpu.make_async_copy(feat_hbm.at[at, :], feat_ref.at[at, :], feat_sem.at[k]) for k, at in enumerate(chunks)
    ]
    small[0].start()
    for load in loads:
        load.start()
    small[1].start()
    small[0].wait()
    starts = range(0, total, step)
    hits = [hits_by_row([along_rows(send_ref[:, start : start + step])], 0, nodes) for start in starts]
    small[1].wait()
    out_ref[:, slots:, :] = jnp.broadcast_to(hub_ref[...][None], (parts, hub_rows, width))
    picked = [None] * len(hits)
    for load, at in zip(loads, chunks):
        load.wait()
        for k, hit in enumerate(hits):
            part = dot(hit[:, at], feat_ref[at, :])
            picked[k] = part if picked[k] is None else picked[k] + part
    for start, rows in zip(starts, picked):
        out_ref[start // slots : (start + step) // slots, :slots, :] = (
            rows.astype(bf16).reshape(step // slots, slots, width)
        )


def local_kernel(local_ref, feat_ref, sum_ref):
    columns = [along_rows(row) for row in index_rows(local_ref, 0, TILE)]
    total = None
    for first in range(0, feat_ref.shape[0], TILE):
        part = dot(hits_by_row(columns, first, TILE), feat_ref[first : first + TILE, :])
        total = part if total is None else total + part
    sum_ref[...] = total


def middle_kernel(
    scale,
    remote_hbm,
    hub_hbm,
    feat_hbm,
    sum_hbm,
    cot_hbm,
    table_hbm,
    ws_hbm,
    wn_hbm,
    bias_hbm,
    act_hbm,
    grad_hbm,
    pay_hbm,
    remote_ref,
    hub_ref,
    feat,
    sums,
    cot,
    bound_part,
    hub_part,
    ws_ref,
    wn_ref,
    bias_ref,
    by_col,
    act,
    grad_all,
    mean_all,
    bound_pay,
    hub_pay,
    weight_pay,
    small_sem,
    block_sem,
    out_sem,
    pay_sem,
):
    nodes, width = feat.shape
    parts, slots, _ = bound_part.shape
    hub_rows = hub_part.shape[1]
    slab = slots + hub_rows
    bounds, hubs = parts * slots, parts * hub_rows
    size = 2 * TILE
    blocks = nodes // size

    def here(block):
        return slice(block * size, (block + 1) * size)

    def loads(block):
        at = here(block)
        return [
            pltpu.make_async_copy(source.at[at, :], target.at[at, :], block_sem.at[which, block])
            for which, (source, target) in enumerate(((sum_hbm, sums), (feat_hbm, feat), (cot_hbm, cot)))
        ]

    small = [
        pltpu.make_async_copy(source, target, small_sem.at[which])
        for which, (source, target) in enumerate(
            (
                (remote_hbm, remote_ref),
                (hub_hbm, hub_ref),
                (table_hbm.at[:, :slots, :], bound_part),
                (table_hbm.at[:, slots:, :], hub_part),
                (ws_hbm, ws_ref),
                (wn_hbm, wn_ref),
                (bias_hbm, bias_ref),
            )
        )
    ]
    for copy in small:
        copy.start()
    coming = [loads(block) for block in range(blocks)]
    for group in coming:
        for copy in group:
            copy.start()

    def counts(block):
        start = block * size
        hits = jnp.concatenate(
            [
                hits_by_column(index_rows(remote_ref, start, size), 0, bounds),
                hits_by_column(index_rows(hub_ref, start, size), 0, hubs),
            ],
            axis=0,
        )
        by_col[:, here(block)] = hits
        return hits

    small[0].wait()
    small[1].wait()
    hits = counts(0)
    for copy in small[2:]:
        copy.wait()
    table = jnp.concatenate(
        [jnp.transpose(bound_part[...].reshape(bounds, width)), jnp.transpose(hub_part[...].reshape(hubs, width))],
        axis=1,
    )
    stores = []
    bias_total = jnp.zeros((1, width), f32)
    total = None
    for block in range(blocks + 1):
        following = None
        if block < blocks:
            for copy in coming[block]:
                copy.wait()
            following = sums[here(block), :] + jnp.transpose(dot(table, hits))
            if block + 1 < blocks:
                hits = counts(block + 1)
        if block > 0:
            at = here(block - 1)
            mean = (total * scale).astype(bf16)
            mean_all[at, :] = mean
            pre = dot(feat[at, :], ws_ref[...]) + dot(mean, wn_ref[...]) + bias_ref[...]
            sig = 0.5 * jnp.tanh(0.5 * pre) + 0.5
            active = pre * sig
            act[at, :] = active.astype(bf16)
            grad = (cot[at, :].astype(f32) * (sig + active * (1.0 - sig))).astype(bf16)
            grad_all[at, :] = grad
            bias_total = bias_total + jnp.sum(grad.astype(f32), axis=0, keepdims=True)
            for which, (source, target) in enumerate(((act, act_hbm), (grad_all, grad_hbm))):
                store = pltpu.make_async_copy(source.at[at, :], target.at[at, :], out_sem.at[which, block - 1])
                store.start()
                stores.append(store)
        total = following
    grad = grad_all[...]

    def send(source, first, which):
        store = pltpu.make_async_copy(source, pay_hbm.at[:, first : first + source.shape[1], :], pay_sem.at[which])
        store.start()
        stores.append(store)

    bound_pay[...] = dot(by_col[:bounds, :], grad).astype(bf16).reshape(parts, slots, width)
    send(bound_pay, 0, 0)
    hub_pay[...] = dot(by_col[bounds:, :], grad).astype(bf16).reshape(parts, hub_rows, width)
    send(hub_pay, slots, 1)
    holders = 2 * width // 16
    per = holders // 2
    weight_pay[:, 16:, :] = jnp.broadcast_to(high_low(bias_total).astype(bf16)[None], (parts, 8, width))
    for which, source in enumerate((feat, mean_all)):
        weight_pay[which * per : (which + 1) * per, :16, :] = (
            dot(source[...], grad, TN).astype(bf16).reshape(per, 16, width)
        )
    if parts > holders:
        weight_pay[holders:, :16, :] = jnp.zeros((parts - holders, 16, width), bf16)
    send(weight_pay, slab, 2)
    for store in stores:
        store.wait()


def high_low(row):
    high = row.astype(bf16).astype(f32)
    place = lax.broadcasted_iota(jnp.int32, (8, row.shape[1]), 0)
    return jnp.where(place == 0, high, jnp.where(place == 1, row - high, 0.0))


def sums_kernel(scale, slots, hub_rows, back_ref, wn_ref, weight_ref, bias_ref, hub_ref):
    slab = slots + hub_rows
    total = jnp.sum(back_ref[:, slots:, :].astype(f32), axis=0)
    weight_ref[...] = jnp.broadcast_to(total[hub_rows : hub_rows + 16].astype(bf16)[None], weight_ref.shape)
    bias_ref[...] = jnp.sum(total[hub_rows + 16 :], axis=0, keepdims=True)
    hub = total[:hub_rows]
    high = hub.astype(bf16)
    low = (hub - high.astype(f32)).astype(bf16)
    hub_ref[...] = (dot(high, wn_ref[...], NT) + dot(low, wn_ref[...], NT)) * scale


def spread_kernel(in_ref, out_ref):
    out_ref[...] = jnp.broadcast_to(in_ref[...][None], out_ref.shape)


def scatter_kernel(local_ref, grad_ref, out_ref):
    height = out_ref.shape[0]
    first = pl.program_id(0) * height
    total = None
    for start in range(0, grad_ref.shape[0], TILE):
        rows = index_rows(local_ref, start, TILE)
        part = dot(hits_by_column(rows, first, height), grad_ref[start : start + TILE, :])
        total = part if total is None else total + part
    out_ref[...] = total


def final_kernel(scale, slots, send_ref, back_ref, scat_ref, grad_ref, ws_ref, wn_ref, out_ref):
    height, width = out_ref.shape
    first = pl.program_id(0) * height
    count = send_ref.shape[1]
    returned = back_ref[:, :slots, :].reshape(count, width)
    total = scat_ref[...]
    for start in range(0, count, 512):
        stop = min(count, start + 512)
        hits = hits_by_column([send_ref[:, start:stop]], first, height)
        total = total + dot(hits, returned[start:stop])
    out_ref[...] = dot(grad_ref[...], ws_ref[...], NT) + dot((total * scale).astype(bf16), wn_ref[...], NT)


def call(
    kernel, ins, in_specs, outs, out_specs, name, grid=(), scratch=(), flops=0, moved=0, limit=SOME_VMEM
):
    return pl.pallas_call(
        kernel,
        grid=grid,
        in_specs=in_specs,
        out_specs=out_specs,
        out_shape=outs,
        scratch_shapes=scratch,
        compiler_params=params(limit),
        cost_estimate=cost(flops, moved),
        name=name,
    )(*ins)


def whole_block(shape):
    return pl.BlockSpec(shape, lambda *_: (0,) * len(shape))


def body(
    features,
    hub_features,
    w_self,
    w_neigh,
    out_bias,
    local_edges,
    hub_edges,
    remote_edges,
    send_rows,
    cotangent,
):
    nodes, width = features.shape
    hub_rows = hub_features.shape[0]
    rows, cols = lax.axis_size("row"), lax.axis_size("col")
    parts = rows * cols
    slots = send_rows.shape[1] // parts
    slab = slots + hub_rows
    pay = slab + 24
    table = parts * slab
    scale = 1.0 / (local_edges.shape[1] + hub_edges.shape[1] + remote_edges.shape[1])
    local_t, hub_t, remote_t = local_edges.T, hub_edges.T, remote_edges.T
    bias = out_bias.reshape(1, width)
    shape = jax.ShapeDtypeStruct

    def exchange(value, axes=AXES):
        return lax.all_to_all(value, axes, split_axis=0, concat_axis=0, tiled=True)

    sending = call(
        pick_kernel,
        (send_rows, features, hub_features),
        [HBM] * 3,
        shape((parts, slab, width), bf16),
        whole_block((parts, slab, width)),
        "pick_rows",
        limit=MOST_VMEM,
        scratch=[
            pltpu.VMEM(send_rows.shape, jnp.int32),
            pltpu.VMEM((nodes, width), bf16),
            pltpu.VMEM((hub_rows, width), bf16),
            pltpu.SemaphoreType.DMA((2,)),
            pltpu.SemaphoreType.DMA((4,)),
        ],
        flops=2 * parts * slots * nodes * width,
        moved=nodes * width * 2,
    )
    sending, features = lax.optimization_barrier((sending, features))
    received = exchange(sending)

    block = TILE
    local_sum = call(
        local_kernel,
        (local_t, features),
        [pl.BlockSpec((local_t.shape[0], block), lambda i: (0, i)), whole_block((nodes, width))],
        shape((nodes, width), f32),
        pl.BlockSpec((block, width), lambda i: (i, 0)),
        "local_gather",
        limit=MOST_VMEM,
        grid=(nodes // block,),
        flops=8 * nodes * nodes * width,
        moved=nodes * width * 6,
    )

    activated, grad_pre, terms = call(
        functools.partial(middle_kernel, scale),
        [remote_t, hub_t, features, local_sum, cotangent, received, w_self, w_neigh, bias],
        [HBM] * 9,
        [shape((nodes, width), bf16)] * 2 + [shape((parts, pay, width), bf16)],
        [HBM] * 3,
        "activate",
        limit=MOST_VMEM,
        scratch=[
            pltpu.VMEM(remote_t.shape, jnp.int32),
            pltpu.VMEM(hub_t.shape, jnp.int32),
            pltpu.VMEM((nodes, width), bf16),
            pltpu.VMEM((nodes, width), f32),
            pltpu.VMEM((nodes, width), bf16),
            pltpu.VMEM((parts, slots, width), bf16),
            pltpu.VMEM((parts, hub_rows, width), bf16),
            pltpu.VMEM((width, width), bf16),
            pltpu.VMEM((width, width), bf16),
            pltpu.VMEM((1, width), f32),
            pltpu.VMEM((table, nodes), bf16),
            pltpu.VMEM((nodes, width), bf16),
            pltpu.VMEM((nodes, width), bf16),
            pltpu.VMEM((nodes, width), bf16),
            pltpu.VMEM((parts, slots, width), bf16),
            pltpu.VMEM((parts, hub_rows, width), bf16),
            pltpu.VMEM((parts, 24, width), bf16),
            pltpu.SemaphoreType.DMA((7,)),
            pltpu.SemaphoreType.DMA((3, nodes // (2 * TILE))),
            pltpu.SemaphoreType.DMA((2, nodes // (2 * TILE))),
            pltpu.SemaphoreType.DMA((3,)),
        ],
        flops=4 * nodes * table * width,
        moved=nodes * width * 8,
    )
    back = exchange(terms)

    scattered = call(
        scatter_kernel,
        (local_t, grad_pre),
        [whole_block(local_t.shape), whole_block((nodes, width))],
        shape((nodes, width), f32),
        pl.BlockSpec((block, width), lambda i: (i, 0)),
        "local_scatter",
        grid=(nodes // block,),
        flops=8 * nodes * nodes * width,
        moved=nodes * width * 6,
    )
    weight_rows, grad_bias, grad_hubs = call(
        functools.partial(sums_kernel, scale, slots, hub_rows),
        (back, w_neigh),
        [VMEM, VMEM],
        [shape((cols, 16, width), bf16), shape((1, width), f32), shape((hub_rows, width), f32)],
        [whole_block((cols, 16, width)), whole_block((1, width)), whole_block((hub_rows, width))],
        "sums",
        moved=parts * (pay + 16) * width * 2,
    )
    weight_rows = exchange(weight_rows, "col").reshape(cols * 16, width)
    weight_rows = call(
        spread_kernel,
        (weight_rows,),
        [VMEM],
        shape((rows, cols * 16, width), bf16),
        whole_block((rows, cols * 16, width)),
        "spread_weights",
        moved=parts * 16 * width * 2,
    )
    weights = exchange(weight_rows, "row").reshape(parts, 16, width)

    height = 2 * TILE
    by_height = pl.BlockSpec((height, width), lambda i: (i, 0))
    grad_features = call(
        functools.partial(final_kernel, scale, slots),
        (send_rows, back, scattered, grad_pre, w_self, w_neigh),
        [whole_block(send_rows.shape), whole_block((parts, pay, width)), by_height, by_height]
        + [whole_block((width, width))] * 2,
        shape((nodes, width), f32),
        by_height,
        "return_scatter",
        grid=(nodes // height,),
        flops=2 * nodes * parts * slots * width,
        moved=nodes * width * 10,
    )
    weights = weights[: 2 * width // 16].reshape(2, width, width).astype(f32)
    return (activated, grad_features, grad_hubs, weights[0], weights[1], grad_bias.reshape(width))


def solution(mesh):
    split = P(AXES, None)
    return jax.shard_map(
        body,
        mesh=mesh,
        in_specs=(split, split, P(), P(), P(), split, split, split, split, split),
        out_specs=(split, split, split, P(), P(), P()),
        check_vma=False,
    )
```

```python
import functools

import jax
import jax.numpy as jnp
from jax import lax
from jax.experimental import pallas as pl
from jax.experimental.pallas import tpu as pltpu
from jax.sharding import PartitionSpec as P

AXES = ("row", "col")
LANES = 128
TILE = 256
MOST_VMEM = 61952 * 1024
MUCH_VMEM = 60500 * 1024
SOME_VMEM = 44 * 1024 * 1024
NT = (((1,), (1,)), ((), ()))
TN = (((0,), (0,)), ((), ()))
VMEM = pl.BlockSpec(memory_space=pltpu.VMEM)
SMEM = pl.BlockSpec(memory_space=pltpu.SMEM)
HBM = pl.BlockSpec(memory_space=pltpu.HBM)
bf16, f32 = jnp.bfloat16, jnp.float32


def params(limit):
    return pltpu.CompilerParams(vmem_limit_bytes=limit)


def cost(flops, moved):
    return pl.CostEstimate(flops=int(flops), bytes_accessed=int(moved), transcendentals=0)


def along_rows(index_row):
    count = index_row.shape[1]
    return jnp.transpose(jnp.broadcast_to(index_row, (LANES, count))).astype(jnp.int16)


def stack_rows(value, height):
    count = value.shape[1]
    return jnp.broadcast_to(value[None], (height // 16, 16, count)).reshape(height, count)


def count_hits(entries, here):
    one, zero = jnp.ones(here.shape, bf16), jnp.zeros(here.shape, bf16)
    total = None
    for entry in entries:
        hit = jnp.where(entry == here, one, zero)
        total = hit if total is None else total + hit
    return total


def hits_by_row(columns, first, width):
    rows = columns[0].shape[0]
    lane = lax.broadcasted_iota(jnp.int32, (16, LANES), 1).astype(jnp.int16)
    tiles = [
        count_hits(columns, stack_rows(lane + jnp.int16(start), rows)) for start in range(first, first + width, LANES)
    ]
    return jnp.concatenate(tiles, axis=1) if len(tiles) > 1 else tiles[0]


def hits_by_column(index_rows, first, height):
    count = index_rows[0].shape[1]
    group = 64
    down = lax.broadcasted_iota(jnp.int32, (group, count), 0).astype(jnp.int16)
    entries = [
        stack_rows(jnp.broadcast_to(row - first, (16, count)).astype(jnp.int16), group) for row in index_rows
    ]
    return jnp.concatenate(
        [count_hits(entries, down + jnp.int16(start)) for start in range(0, height, group)], axis=0
    )


def dot(a, b, dims=(((1,), (0,)), ((), ()))):
    return lax.dot_general(a, b, dims, preferred_element_type=f32)


def index_rows(ref, start, count):
    return [ref[j : j + 1, pl.ds(start, count)] for j in range(ref.shape[0])]


def pick_kernel(send_ref, feat_ref, hub_ref, out_ref):
    parts, slab, width = out_ref.shape
    hub_rows = hub_ref.shape[0]
    slots = slab - hub_rows
    total = send_ref.shape[1]
    step = min(512, total)
    for start in range(0, total, step):
        column = along_rows(send_ref[:, start : start + step])
        picked = dot(hits_by_row([column], 0, feat_ref.shape[0]), feat_ref[...])
        out_ref[start // slots : (start + step) // slots, :slots, :] = (
            picked.astype(bf16).reshape(step // slots, slots, width)
        )
    out_ref[:, slots:, :] = jnp.broadcast_to(hub_ref[...][None], (parts, hub_rows, width))


def local_kernel(split, local_ref, remote_ref, hub_ref, feat_ref, own_ref, cot_ref, sum_ref, pack_ref):
    nodes, width = feat_ref.shape
    columns = [along_rows(row) for row in index_rows(local_ref, 0, TILE)]
    total = None
    for first in range(0, nodes, TILE):
        part = dot(hits_by_row(columns, first, TILE), feat_ref[first : first + TILE, :])
        total = part if total is None else total + part
    sum_ref[...] = total
    pack_ref[:, :width] = own_ref[...]
    pack_ref[:, width : 2 * width] = cot_ref[...]
    place = 2 * width
    counts = pack_ref.shape[1] - place
    for ref, share in ((remote_ref, split), (hub_ref, counts - split)):
        columns = [along_rows(row) for row in index_rows(ref, 0, TILE)]
        for first in range(0, share, TILE):
            pack_ref[:, place + first : place + first + TILE] = hits_by_row(columns, first, TILE)
        place += share


def middle_kernel(
    scale,
    slots,
    remote_ref,
    hub_ref,
    table_ref,
    ws_ref,
    wn_ref,
    bias_ref,
    sum_hbm,
    pack_hbm,
    act_hbm,
    grad_hbm,
    pay_hbm,
    sums,
    pack,
    by_col,
    act,
    grad_all,
    mean_all,
    bound_pay,
    hub_pay,
    weight_pay,
    block_sem,
    out_sem,
    pay_sem,
):
    nodes, width = sums.shape
    parts, slab, _ = table_ref.shape
    hub_rows = slab - slots
    bounds, hubs = parts * slots, parts * hub_rows
    size = 2 * TILE
    blocks = nodes // size

    def here(block):
        return slice(block * size, (block + 1) * size)

    def loads(block):
        at = here(block)
        return [
            pltpu.make_async_copy(source.at[at, :], target.at[at, :], block_sem.at[which, block])
            for which, (source, target) in enumerate(((pack_hbm, pack), (sum_hbm, sums)))
        ]

    coming = [loads(block) for block in range(blocks)]
    for group in coming:
        for copy in group:
            copy.start()

    def counts(block):
        start = block * size
        by_col[:bounds, here(block)] = hits_by_column(index_rows(remote_ref, start, size), 0, bounds)
        by_col[bounds:, here(block)] = hits_by_column(index_rows(hub_ref, start, size), 0, hubs)

    counts(0)
    table = jnp.concatenate(
        [table_ref[:, :slots, :].reshape(bounds, width), table_ref[:, slots:, :].reshape(hubs, width)], axis=0
    )
    stores = []
    bias_total = jnp.zeros((1, width), f32)
    total = None
    for block in range(blocks + 1):
        following = None
        if block < blocks:
            for copy in coming[block]:
                copy.wait()
            following = sums[here(block), :] + dot(pack[here(block), 2 * width :], table)
            if block > 0:
                counts(block)
        if block > 0:
            at = here(block - 1)
            mean = (total * scale).astype(bf16)
            mean_all[at, :] = mean
            pre = dot(pack[at, :width], ws_ref[...]) + dot(mean, wn_ref[...]) + bias_ref[...]
            sig = 0.5 * jnp.tanh(0.5 * pre) + 0.5
            active = pre * sig
            act[at, :] = active.astype(bf16)
            grad = (pack[at, width : 2 * width].astype(f32) * (sig + active * (1.0 - sig))).astype(bf16)
            grad_all[at, :] = grad
            bias_total = bias_total + jnp.sum(grad.astype(f32), axis=0, keepdims=True)
            for which, (source, target) in enumerate(((act, act_hbm), (grad_all, grad_hbm))):
                store = pltpu.make_async_copy(source.at[at, :], target.at[at, :], out_sem.at[which, block - 1])
                store.start()
                stores.append(store)
        total = following
    grad = grad_all[...]

    def send(source, first, which):
        store = pltpu.make_async_copy(source, pay_hbm.at[:, first : first + source.shape[1], :], pay_sem.at[which])
        store.start()
        stores.append(store)

    bound_pay[...] = dot(by_col[:bounds, :], grad).astype(bf16).reshape(parts, slots, width)
    send(bound_pay, 0, 0)
    hub_pay[...] = dot(by_col[bounds:, :], grad).astype(bf16).reshape(parts, hub_rows, width)
    send(hub_pay, slots, 1)
    holders = 2 * width // 16
    per = holders // 2
    weight_pay[:, 16:, :] = jnp.broadcast_to(high_low(bias_total).astype(bf16)[None], (parts, 8, width))
    for which, source in enumerate((pack[:, :width], mean_all[...])):
        weight_pay[which * per : (which + 1) * per, :16, :] = dot(source, grad, TN).astype(bf16).reshape(per, 16, width)
    if parts > holders:
        weight_pay[holders:, :16, :] = jnp.zeros((parts - holders, 16, width), bf16)
    send(weight_pay, slab, 2)
    for store in stores:
        store.wait()


def high_low(row):
    high = row.astype(bf16).astype(f32)
    place = lax.broadcasted_iota(jnp.int32, (8, row.shape[1]), 0)
    return jnp.where(place == 0, high, jnp.where(place == 1, row - high, 0.0))


def sums_kernel(scale, slots, hub_rows, back_ref, wn_ref, weight_ref, bias_ref, hub_ref):
    slab = slots + hub_rows
    total = jnp.sum(back_ref[:, slots:, :].astype(f32), axis=0)
    weight_ref[...] = jnp.broadcast_to(total[hub_rows : hub_rows + 16].astype(bf16)[None], weight_ref.shape)
    bias_ref[...] = jnp.sum(total[hub_rows + 16 :], axis=0, keepdims=True)
    hub = total[:hub_rows]
    high = hub.astype(bf16)
    low = (hub - high.astype(f32)).astype(bf16)
    hub_ref[...] = (dot(high, wn_ref[...], NT) + dot(low, wn_ref[...], NT)) * scale


def scatter_kernel(local_ref, grad_ref, out_ref):
    height = out_ref.shape[0]
    first = pl.program_id(0) * height
    total = None
    for start in range(0, grad_ref.shape[0], TILE):
        rows = index_rows(local_ref, start, TILE)
        part = dot(hits_by_column(rows, first, height), grad_ref[start : start + TILE, :])
        total = part if total is None else total + part
    out_ref[...] = total


def final_kernel(scale, slots, send_ref, back_ref, scat_ref, grad_ref, ws_ref, wn_ref, out_ref):
    height, width = out_ref.shape
    first = pl.program_id(0) * height
    count = send_ref.shape[1]
    returned = back_ref[:, :slots, :].reshape(count, width)
    total = scat_ref[...]
    for start in range(0, count, 512):
        stop = min(count, start + 512)
        hits = hits_by_column([send_ref[:, start:stop]], first, height)
        total = total + dot(hits, returned[start:stop])
    out_ref[...] = dot(grad_ref[...], ws_ref[...], NT) + dot((total * scale).astype(bf16), wn_ref[...], NT)


def call(
    kernel, ins, in_specs, outs, out_specs, name, grid=(), scratch=(), flops=0, moved=0, limit=SOME_VMEM
):
    return pl.pallas_call(
        kernel,
        grid=grid,
        in_specs=in_specs,
        out_specs=out_specs,
        out_shape=outs,
        scratch_shapes=scratch,
        compiler_params=params(limit),
        cost_estimate=cost(flops, moved),
        name=name,
    )(*ins)


def whole_block(shape):
    return pl.BlockSpec(shape, lambda *_: (0,) * len(shape))


def body(
    features,
    hub_features,
    w_self,
    w_neigh,
    out_bias,
    local_edges,
    hub_edges,
    remote_edges,
    send_rows,
    cotangent,
):
    nodes, width = features.shape
    hub_rows = hub_features.shape[0]
    parts = lax.axis_size(AXES)
    slots = send_rows.shape[1] // parts
    slab = slots + hub_rows
    pay = slab + 24
    table = parts * slab
    scale = 1.0 / (local_edges.shape[1] + hub_edges.shape[1] + remote_edges.shape[1])
    local_t, hub_t, remote_t = local_edges.T, hub_edges.T, remote_edges.T
    bias = out_bias.reshape(1, width)
    shape = jax.ShapeDtypeStruct

    def exchange(value):
        return lax.all_to_all(value, AXES, split_axis=0, concat_axis=0, tiled=True)

    sending = call(
        pick_kernel,
        (send_rows, features, hub_features),
        [VMEM, VMEM, VMEM],
        shape((parts, slab, width), bf16),
        whole_block((parts, slab, width)),
        "pick_rows",
        limit=MOST_VMEM,
        flops=2 * parts * slots * nodes * width,
        moved=nodes * width * 2,
    )
    sending, features = lax.optimization_barrier((sending, features))
    received = exchange(sending)

    block = TILE
    by_block = pl.BlockSpec((block, width), lambda i: (i, 0))
    packed = 2 * width + table
    local_sum, pack = call(
        functools.partial(local_kernel, parts * slots),
        (local_t, remote_t, hub_t, features, features, cotangent),
        [pl.BlockSpec((edges.shape[0], block), lambda i: (0, i)) for edges in (local_t, remote_t, hub_t)]
        + [whole_block((nodes, width)), by_block, by_block],
        [shape((nodes, width), f32), shape((nodes, packed), bf16)],
        [by_block, pl.BlockSpec((block, packed), lambda i: (i, 0))],
        "local_gather",
        limit=MOST_VMEM,
        grid=(nodes // block,),
        flops=8 * nodes * nodes * width,
        moved=nodes * packed * 2,
    )

    activated, grad_pre, terms = call(
        functools.partial(middle_kernel, scale, slots),
        [remote_t, hub_t, received, w_self, w_neigh, bias, local_sum, pack],
        [VMEM] * 6 + [HBM] * 2,
        [shape((nodes, width), bf16)] * 2 + [shape((parts, pay, width), bf16)],
        [HBM] * 3,
        "activate",
        limit=MUCH_VMEM,
        scratch=[
            pltpu.VMEM((nodes, width), f32),
            pltpu.VMEM((nodes, packed), bf16),
            pltpu.VMEM((table, nodes), bf16),
            pltpu.VMEM((nodes, width), bf16),
            pltpu.VMEM((nodes, width), bf16),
            pltpu.VMEM((nodes, width), bf16),
            pltpu.VMEM((parts, slots, width), bf16),
            pltpu.VMEM((parts, hub_rows, width), bf16),
            pltpu.VMEM((parts, 24, width), bf16),
            pltpu.SemaphoreType.DMA((2, nodes // (2 * TILE))),
            pltpu.SemaphoreType.DMA((2, nodes // (2 * TILE))),
            pltpu.SemaphoreType.DMA((3,)),
        ],
        flops=4 * nodes * table * width,
        moved=nodes * packed * 2,
    )
    back = exchange(terms)

    scattered = call(
        scatter_kernel,
        (local_t, grad_pre),
        [whole_block(local_t.shape), whole_block((nodes, width))],
        shape((nodes, width), f32),
        pl.BlockSpec((block, width), lambda i: (i, 0)),
        "local_scatter",
        grid=(nodes // block,),
        flops=8 * nodes * nodes * width,
        moved=nodes * width * 6,
    )
    weight_rows, grad_bias, grad_hubs = call(
        functools.partial(sums_kernel, scale, slots, hub_rows),
        (back, w_neigh),
        [VMEM, VMEM],
        [shape((parts, 16, width), bf16), shape((1, width), f32), shape((hub_rows, width), f32)],
        [whole_block((parts, 16, width)), whole_block((1, width)), whole_block((hub_rows, width))],
        "sums",
        moved=parts * (pay + 16) * width * 2,
    )
    weights = exchange(weight_rows)

    height = 2 * TILE
    by_height = pl.BlockSpec((height, width), lambda i: (i, 0))
    grad_features = call(
        functools.partial(final_kernel, scale, slots),
        (send_rows, back, scattered, grad_pre, w_self, w_neigh),
        [whole_block(send_rows.shape), whole_block((parts, pay, width)), by_height, by_height]
        + [whole_block((width, width))] * 2,
        shape((nodes, width), f32),
        by_height,
        "return_scatter",
        grid=(nodes // height,),
        flops=2 * nodes * parts * slots * width,
        moved=nodes * width * 10,
    )
    weights = weights[: 2 * width // 16].reshape(2, width, width).astype(f32)
    return (activated, grad_features, grad_hubs, weights[0], weights[1], grad_bias.reshape(width))


def solution(mesh):
    split = P(AXES, None)
    return jax.shard_map(
        body,
        mesh=mesh,
        in_specs=(split, split, P(), P(), P(), split, split, split, split, split),
        out_specs=(split, split, split, P(), P(), P()),
        check_vma=False,
    )
```

```python
import functools

import jax
import jax.numpy as jnp
from jax import lax
from jax.experimental import pallas as pl
from jax.experimental.pallas import tpu as pltpu
from jax.sharding import PartitionSpec as P

AXES = ("row", "col")
LANES = 128
TILE = 256
MOST_VMEM = 61952 * 1024
SOME_VMEM = 44 * 1024 * 1024
NT = (((1,), (1,)), ((), ()))
TN = (((0,), (0,)), ((), ()))
VMEM = pl.BlockSpec(memory_space=pltpu.VMEM)
SMEM = pl.BlockSpec(memory_space=pltpu.SMEM)
HBM = pl.BlockSpec(memory_space=pltpu.HBM)
bf16, f32 = jnp.bfloat16, jnp.float32


def params(limit):
    return pltpu.CompilerParams(vmem_limit_bytes=limit)


def cost(flops, moved):
    return pl.CostEstimate(flops=int(flops), bytes_accessed=int(moved), transcendentals=0)


def along_rows(index_row):
    count = index_row.shape[1]
    return jnp.transpose(jnp.broadcast_to(index_row, (LANES, count))).astype(jnp.int16)


def stack_rows(value, height):
    count = value.shape[1]
    return jnp.broadcast_to(value[None], (height // 16, 16, count)).reshape(height, count)


def count_hits(entries, here):
    one, zero = jnp.ones(here.shape, bf16), jnp.zeros(here.shape, bf16)
    total = None
    for entry in entries:
        hit = jnp.where(entry == here, one, zero)
        total = hit if total is None else total + hit
    return total


def hits_by_row(columns, first, width):
    rows = columns[0].shape[0]
    lane = lax.broadcasted_iota(jnp.int32, (16, LANES), 1).astype(jnp.int16)
    tiles = [
        count_hits(columns, stack_rows(lane + jnp.int16(start), rows)) for start in range(first, first + width, LANES)
    ]
    return jnp.concatenate(tiles, axis=1) if len(tiles) > 1 else tiles[0]


def hits_by_column(index_rows, first, height):
    count = index_rows[0].shape[1]
    group = 64
    down = lax.broadcasted_iota(jnp.int32, (group, count), 0).astype(jnp.int16)
    entries = [
        stack_rows(jnp.broadcast_to(row - first, (16, count)).astype(jnp.int16), group) for row in index_rows
    ]
    return jnp.concatenate(
        [count_hits(entries, down + jnp.int16(start)) for start in range(0, height, group)], axis=0
    )


def dot(a, b, dims=(((1,), (0,)), ((), ()))):
    return lax.dot_general(a, b, dims, preferred_element_type=f32)


def index_rows(ref, start, count):
    return [ref[j : j + 1, pl.ds(start, count)] for j in range(ref.shape[0])]


def pick_kernel(send_ref, feat_ref, hub_ref, out_ref):
    parts, slab, width = out_ref.shape
    hub_rows = hub_ref.shape[0]
    slots = slab - hub_rows
    total = send_ref.shape[1]
    step = min(512, total)
    for start in range(0, total, step):
        column = along_rows(send_ref[:, start : start + step])
        picked = dot(hits_by_row([column], 0, feat_ref.shape[0]), feat_ref[...])
        out_ref[start // slots : (start + step) // slots, :slots, :] = (
            picked.astype(bf16).reshape(step // slots, slots, width)
        )
    out_ref[:, slots:, :] = jnp.broadcast_to(hub_ref[...][None], (parts, hub_rows, width))


def local_kernel(split, local_ref, remote_ref, hub_ref, feat_ref, own_ref, cot_ref, sum_ref, pack_ref):
    nodes, width = feat_ref.shape
    columns = [along_rows(row) for row in index_rows(local_ref, 0, TILE)]
    total = None
    for first in range(0, nodes, TILE):
        part = dot(hits_by_row(columns, first, TILE), feat_ref[first : first + TILE, :])
        total = part if total is None else total + part
    sum_ref[...] = total
    pack_ref[:, :width] = cot_ref[...]
    pack_ref[:, width : 2 * width] = own_ref[...]
    place = 2 * width
    counts = pack_ref.shape[1] - place
    for ref, share in ((remote_ref, split), (hub_ref, counts - split)):
        columns = [along_rows(row) for row in index_rows(ref, 0, TILE)]
        for first in range(0, share, TILE):
            pack_ref[:, place + first : place + first + TILE] = hits_by_row(columns, first, TILE)
        place += share


def middle_kernel(
    scale,
    slots,
    table_ref,
    ws_ref,
    wn_ref,
    bias_ref,
    sum_ref,
    pack_hbm,
    act_hbm,
    grad_hbm,
    pay_ref,
    pack,
    act,
    grad_all,
    grad_t,
    in_sem,
    out_sem,
):
    nodes, width = sum_ref.shape
    parts, slab, _ = table_ref.shape
    hub_rows = slab - slots
    bounds, hubs = parts * slots, parts * hub_rows
    size = 2 * TILE
    blocks = nodes // size
    features, counts = slice(width, 2 * width), 3 * width

    def here(block):
        return slice(block * size, (block + 1) * size)

    def loads(block):
        at = here(block)
        return [
            pltpu.make_async_copy(pack_hbm.at[at, : 2 * width], pack.at[at, : 2 * width], in_sem.at[0, block]),
            pltpu.make_async_copy(pack_hbm.at[at, 2 * width :], pack.at[at, counts:], in_sem.at[1, block]),
        ]

    coming = [loads(block) for block in range(blocks)]
    for group in coming:
        for copy in group:
            copy.start()
    table = jnp.concatenate(
        [table_ref[:, :slots, :].reshape(bounds, width), table_ref[:, slots:, :].reshape(hubs, width)], axis=0
    )
    half_weights = jnp.concatenate([ws_ref[...], wn_ref[...]], axis=0) * jnp.bfloat16(0.5)
    half_bias = 0.5 * bias_ref[...]
    stores = []
    total = None
    for block in range(blocks + 1):
        following = None
        if block < blocks:
            for copy in coming[block]:
                copy.wait()
            following = sum_ref[here(block), :] + dot(pack[here(block), counts:], table)
        if block > 0:
            at = here(block - 1)
            pack[at, 2 * width : counts] = (total * scale).astype(bf16)
            half = dot(pack[at, width:counts], half_weights) + half_bias
            tanh = jnp.tanh(half)
            above = 1.0 + tanh
            act[at, :] = (half * above).astype(bf16)
            slope = above * (0.5 + (0.5 * half) * (1.0 - tanh))
            grad = (pack[at, :width].astype(f32) * slope).astype(bf16)
            grad_all[at, :] = grad
            grad_t[:, at] = jnp.transpose(grad)
            for which, (source, target) in enumerate(((act, act_hbm), (grad_all, grad_hbm))):
                store = pltpu.make_async_copy(source.at[at, :], target.at[at, :], out_sem.at[which, block - 1])
                store.start()
                stores.append(store)
        total = following

    def terms(first, count):
        return jnp.transpose(dot(grad_t[...], pack[:, first : first + count])).astype(bf16).reshape(-1, 16, width)

    holders = 2 * width // 16
    pay_ref[:holders, slab : slab + 16, :] = terms(width, 2 * width)
    if parts > holders:
        pay_ref[holders:, slab : slab + 16, :] = jnp.zeros((parts - holders, 16, width), bf16)
    bias_total = dot(jnp.ones((16, nodes), bf16), grad_all[...])[:1]
    pay_ref[:, slab + 16 :, :] = jnp.broadcast_to(high_low(bias_total).astype(bf16)[None], (parts, 8, width))
    step = 2 * width
    for low, total_rows, place, rows in ((0, bounds, 0, slots), (bounds, hubs, slots, hub_rows)):
        for first in range(0, total_rows, step):
            part = terms(counts + low + first, step).reshape(step // rows, rows, width)
            pay_ref[first // rows : (first + step) // rows, place : place + rows, :] = part
    for store in stores:
        store.wait()


def high_low(row):
    high = row.astype(bf16).astype(f32)
    place = lax.broadcasted_iota(jnp.int32, (8, row.shape[1]), 0)
    return jnp.where(place == 0, high, jnp.where(place == 1, row - high, 0.0))


def sums_kernel(scale, slots, hub_rows, back_ref, wn_ref, weight_ref, bias_ref, hub_ref):
    slab = slots + hub_rows
    total = jnp.sum(back_ref[:, slots:, :].astype(f32), axis=0)
    weight_ref[...] = jnp.broadcast_to(total[hub_rows : hub_rows + 16].astype(bf16)[None], weight_ref.shape)
    bias_ref[...] = jnp.sum(total[hub_rows + 16 :], axis=0, keepdims=True)
    hub = total[:hub_rows]
    high = hub.astype(bf16)
    low = (hub - high.astype(f32)).astype(bf16)
    hub_ref[...] = (dot(high, wn_ref[...], NT) + dot(low, wn_ref[...], NT)) * scale


def scatter_kernel(local_ref, grad_ref, out_ref):
    height = out_ref.shape[0]
    first = pl.program_id(0) * height
    total = None
    for start in range(0, grad_ref.shape[0], TILE):
        rows = index_rows(local_ref, start, TILE)
        part = dot(hits_by_column(rows, first, height), grad_ref[start : start + TILE, :])
        total = part if total is None else total + part
    out_ref[...] = total


def final_kernel(scale, slots, send_ref, back_ref, scat_ref, grad_ref, ws_ref, wn_ref, out_ref):
    height, width = out_ref.shape
    first = pl.program_id(0) * height
    count = send_ref.shape[1]
    returned = back_ref[:, :slots, :].reshape(count, width)
    total = scat_ref[...]
    for start in range(0, count, 512):
        stop = min(count, start + 512)
        hits = hits_by_column([send_ref[:, start:stop]], first, height)
        total = total + dot(hits, returned[start:stop])
    out_ref[...] = dot(grad_ref[...], ws_ref[...], NT) + dot((total * scale).astype(bf16), wn_ref[...], NT)


def call(
    kernel, ins, in_specs, outs, out_specs, name, grid=(), scratch=(), flops=0, moved=0, limit=SOME_VMEM
):
    return pl.pallas_call(
        kernel,
        grid=grid,
        in_specs=in_specs,
        out_specs=out_specs,
        out_shape=outs,
        scratch_shapes=scratch,
        compiler_params=params(limit),
        cost_estimate=cost(flops, moved),
        name=name,
    )(*ins)


def whole_block(shape):
    return pl.BlockSpec(shape, lambda *_: (0,) * len(shape))


def body(
    features,
    hub_features,
    w_self,
    w_neigh,
    out_bias,
    local_edges,
    hub_edges,
    remote_edges,
    send_rows,
    cotangent,
):
    nodes, width = features.shape
    hub_rows = hub_features.shape[0]
    parts = lax.axis_size(AXES)
    slots = send_rows.shape[1] // parts
    slab = slots + hub_rows
    pay = slab + 24
    table = parts * slab
    scale = 1.0 / (local_edges.shape[1] + hub_edges.shape[1] + remote_edges.shape[1])
    local_t, hub_t, remote_t = local_edges.T, hub_edges.T, remote_edges.T
    bias = out_bias.reshape(1, width)
    shape = jax.ShapeDtypeStruct

    def exchange(value):
        return lax.all_to_all(value, AXES, split_axis=0, concat_axis=0, tiled=True)

    sending = call(
        pick_kernel,
        (send_rows, features, hub_features),
        [VMEM, VMEM, VMEM],
        shape((parts, slab, width), bf16),
        whole_block((parts, slab, width)),
        "pick_rows",
        limit=MOST_VMEM,
        flops=2 * parts * slots * nodes * width,
        moved=nodes * width * 2,
    )
    sending, features = lax.optimization_barrier((sending, features))
    received = exchange(sending)

    block = TILE
    by_block = pl.BlockSpec((block, width), lambda i: (i, 0))
    packed = 2 * width + table
    local_sum, pack = call(
        functools.partial(local_kernel, parts * slots),
        (local_t, remote_t, hub_t, features, features, cotangent),
        [pl.BlockSpec((edges.shape[0], block), lambda i: (0, i)) for edges in (local_t, remote_t, hub_t)]
        + [whole_block((nodes, width)), by_block, by_block],
        [shape((nodes, width), f32), pltpu.HBM((nodes, packed), bf16)],
        [by_block, pl.BlockSpec((block, packed), lambda i: (i, 0))],
        "local_gather",
        grid=(nodes // block,),
        flops=8 * nodes * nodes * width,
        moved=nodes * packed * 2,
    )

    activated, grad_pre, terms = call(
        functools.partial(middle_kernel, scale, slots),
        [received, w_self, w_neigh, bias, local_sum, pack],
        [VMEM] * 5 + [HBM],
        [shape((nodes, width), bf16)] * 2 + [shape((parts, pay, width), bf16)],
        [HBM] * 2 + [VMEM],
        "activate",
        scratch=[
            pltpu.VMEM((nodes, packed + width), bf16),
            pltpu.VMEM((nodes, width), bf16),
            pltpu.VMEM((nodes, width), bf16),
            pltpu.VMEM((width, nodes), bf16),
            pltpu.SemaphoreType.DMA((2, nodes // (2 * TILE))),
            pltpu.SemaphoreType.DMA((2, nodes // (2 * TILE))),
        ],
        flops=4 * nodes * table * width,
        moved=nodes * packed * 2,
    )
    back = exchange(terms)

    scattered = call(
        scatter_kernel,
        (local_t, grad_pre),
        [whole_block(local_t.shape), whole_block((nodes, width))],
        shape((nodes, width), f32),
        pl.BlockSpec((block, width), lambda i: (i, 0)),
        "local_scatter",
        grid=(nodes // block,),
        flops=8 * nodes * nodes * width,
        moved=nodes * width * 6,
    )
    weight_rows, grad_bias, grad_hubs = call(
        functools.partial(sums_kernel, scale, slots, hub_rows),
        (back, w_neigh),
        [VMEM, VMEM],
        [shape((parts, 16, width), bf16), shape((1, width), f32), shape((hub_rows, width), f32)],
        [whole_block((parts, 16, width)), whole_block((1, width)), whole_block((hub_rows, width))],
        "sums",
        moved=parts * (pay + 16) * width * 2,
    )
    weights = exchange(weight_rows)

    height = 2 * TILE
    by_height = pl.BlockSpec((height, width), lambda i: (i, 0))
    grad_features = call(
        functools.partial(final_kernel, scale, slots),
        (send_rows, back, scattered, grad_pre, w_self, w_neigh),
        [whole_block(send_rows.shape), whole_block((parts, pay, width)), by_height, by_height]
        + [whole_block((width, width))] * 2,
        shape((nodes, width), f32),
        by_height,
        "return_scatter",
        grid=(nodes // height,),
        flops=2 * nodes * parts * slots * width,
        moved=nodes * width * 10,
    )
    weights = weights[: 2 * width // 16].reshape(2, width, width).astype(f32)
    return (activated, grad_features, grad_hubs, weights[0], weights[1], grad_bias.reshape(width))


def solution(mesh):
    split = P(AXES, None)
    return jax.shard_map(
        body,
        mesh=mesh,
        in_specs=(split, split, P(), P(), P(), split, split, split, split, split),
        out_specs=(split, split, split, P(), P(), P()),
        check_vma=False,
    )
```

```python
import functools

import jax
import jax.numpy as jnp
from jax import lax
from jax.experimental import pallas as pl
from jax.experimental.pallas import tpu as pltpu
from jax.sharding import PartitionSpec as P

AXES = ("row", "col")
LANES = 128
TILE = 256
MOST_VMEM = 61952 * 1024
SOME_VMEM = 44 * 1024 * 1024
NT = (((1,), (1,)), ((), ()))
TN = (((0,), (0,)), ((), ()))
VMEM = pl.BlockSpec(memory_space=pltpu.VMEM)
SMEM = pl.BlockSpec(memory_space=pltpu.SMEM)
HBM = pl.BlockSpec(memory_space=pltpu.HBM)
bf16, f32 = jnp.bfloat16, jnp.float32


def params(limit):
    return pltpu.CompilerParams(vmem_limit_bytes=limit)


def cost(flops, moved):
    return pl.CostEstimate(flops=int(flops), bytes_accessed=int(moved), transcendentals=0)


def along_rows(index_row):
    count = index_row.shape[1]
    return jnp.transpose(jnp.broadcast_to(index_row, (LANES, count))).astype(jnp.int16)


def stack_rows(value, height):
    count = value.shape[1]
    return jnp.broadcast_to(value[None], (height // 16, 16, count)).reshape(height, count)


def count_hits(entries, here):
    one, zero = jnp.ones(here.shape, bf16), jnp.zeros(here.shape, bf16)
    total = None
    for entry in entries:
        hit = jnp.where(entry == here, one, zero)
        total = hit if total is None else total + hit
    return total


def hits_by_row(columns, first, width):
    rows = columns[0].shape[0]
    lane = lax.broadcasted_iota(jnp.int32, (16, LANES), 1).astype(jnp.int16)
    tiles = [
        count_hits(columns, stack_rows(lane + jnp.int16(start), rows)) for start in range(first, first + width, LANES)
    ]
    return jnp.concatenate(tiles, axis=1) if len(tiles) > 1 else tiles[0]


def hits_by_column(index_rows, first, height):
    count = index_rows[0].shape[1]
    group = 64
    down = lax.broadcasted_iota(jnp.int32, (group, count), 0).astype(jnp.int16)
    entries = [
        stack_rows(jnp.broadcast_to(row - first, (16, count)).astype(jnp.int16), group) for row in index_rows
    ]
    return jnp.concatenate(
        [count_hits(entries, down + jnp.int16(start)) for start in range(0, height, group)], axis=0
    )


def dot(a, b, dims=(((1,), (0,)), ((), ()))):
    return lax.dot_general(a, b, dims, preferred_element_type=f32)


def index_rows(ref, start, count):
    return [ref[j : j + 1, pl.ds(start, count)] for j in range(ref.shape[0])]


def pick_kernel(send_ref, feat_ref, hub_ref, out_ref):
    parts, slab, width = out_ref.shape
    hub_rows = hub_ref.shape[0]
    slots = slab - hub_rows
    total = send_ref.shape[1]
    step = min(512, total)
    for start in range(0, total, step):
        column = along_rows(send_ref[:, start : start + step])
        picked = dot(hits_by_row([column], 0, feat_ref.shape[0]), feat_ref[...])
        out_ref[start // slots : (start + step) // slots, :slots, :] = (
            picked.astype(bf16).reshape(step // slots, slots, width)
        )
    out_ref[:, slots:, :] = jnp.broadcast_to(hub_ref[...][None], (parts, hub_rows, width))


def local_kernel(split, local_ref, remote_ref, hub_ref, feat_ref, own_ref, cot_ref, sum_ref, pack_ref):
    nodes, width = feat_ref.shape
    columns = [along_rows(row) for row in index_rows(local_ref, 0, TILE)]
    total = None
    for first in range(0, nodes, TILE):
        part = dot(hits_by_row(columns, first, TILE), feat_ref[first : first + TILE, :])
        total = part if total is None else total + part
    sum_ref[...] = total
    pack_ref[:, :width] = cot_ref[...]
    pack_ref[:, width : 2 * width] = own_ref[...]
    place = 2 * width
    counts = pack_ref.shape[1] - place
    for ref, share in ((remote_ref, split), (hub_ref, counts - split)):
        columns = [along_rows(row) for row in index_rows(ref, 0, TILE)]
        for first in range(0, share, TILE):
            pack_ref[:, place + first : place + first + TILE] = hits_by_row(columns, first, TILE)
        place += share


def middle_kernel(
    scale,
    slots,
    table_ref,
    ws_ref,
    wn_ref,
    bias_ref,
    sum_ref,
    pack_hbm,
    act_hbm,
    grad_hbm,
    pay_ref,
    pack,
    act,
    grad_all,
    terms,
    in_sem,
    out_sem,
):
    nodes, width = sum_ref.shape
    parts, slab, _ = table_ref.shape
    hub_rows = slab - slots
    bounds, hubs = parts * slots, parts * hub_rows
    size = 2 * TILE
    blocks = nodes // size
    features, counts = slice(width, 2 * width), 3 * width

    def here(block):
        return slice(block * size, (block + 1) * size)

    def loads(block):
        at = here(block)
        return [
            pltpu.make_async_copy(pack_hbm.at[at, : 2 * width], pack.at[at, : 2 * width], in_sem.at[0, block]),
            pltpu.make_async_copy(pack_hbm.at[at, 2 * width :], pack.at[at, counts:], in_sem.at[1, block]),
        ]

    coming = [loads(block) for block in range(blocks)]
    for group in coming:
        for copy in group:
            copy.start()
    table = jnp.concatenate(
        [table_ref[:, :slots, :].reshape(bounds, width), table_ref[:, slots:, :].reshape(hubs, width)], axis=0
    )
    half_weights = jnp.concatenate([ws_ref[...], wn_ref[...]], axis=0) * jnp.bfloat16(0.5)
    half_bias = 0.5 * bias_ref[...]
    stores = []
    total = None
    turned = None
    for block in range(blocks + 2):
        following = None
        if block < blocks:
            for copy in coming[block]:
                copy.wait()
            following = sum_ref[here(block), :] + dot(pack[here(block), counts:], table)
        if block > 1:
            part = dot(turned, pack[here(block - 2), width:])
            terms[...] = part if block == 2 else terms[...] + part
        if 0 < block <= blocks:
            at = here(block - 1)
            pack[at, 2 * width : counts] = (total * scale).astype(bf16)
            half = dot(pack[at, width:counts], half_weights) + half_bias
            tanh = jnp.tanh(half)
            above = 1.0 + tanh
            act[at, :] = (half * above).astype(bf16)
            slope = above * (0.5 + (0.5 * half) * (1.0 - tanh))
            grad = (pack[at, :width].astype(f32) * slope).astype(bf16)
            grad_all[at, :] = grad
            turned = jnp.transpose(grad)
            for which, (source, target) in enumerate(((act, act_hbm), (grad_all, grad_hbm))):
                store = pltpu.make_async_copy(source.at[at, :], target.at[at, :], out_sem.at[which, block - 1])
                store.start()
                stores.append(store)
        total = following

    pieces = width // LANES
    tall = slab + 16

    def put(low, high, place, rows, value):
        value = value.astype(bf16).reshape(high - low, rows, width)
        for piece in range(pieces):
            at = piece * tall + place
            pay_ref[low:high, at : at + rows, :] = value[:, :, piece * LANES : (piece + 1) * LANES]

    def term_rows(first, count):
        return jnp.transpose(terms[:, first : first + count])

    holders = 2 * width // 16
    put(0, holders, slab, 16, term_rows(0, 2 * width))
    if parts > holders:
        put(holders, parts, slab, 16, jnp.zeros(((parts - holders) * 16, width), f32))
    step = 2 * width
    for low, total_rows, place, rows in ((0, bounds, 0, slots), (bounds, hubs, slots, hub_rows)):
        for first in range(0, total_rows, step):
            put(first // rows, (first + step) // rows, place, rows, term_rows(2 * width + low + first, step))
    bias_total = dot(jnp.ones((16, nodes), bf16), grad_all[...])[:1]
    high = bias_total.astype(bf16).astype(f32)
    line = lax.broadcasted_iota(jnp.int32, (8, LANES), 0)
    rows = jnp.zeros((8, LANES), f32)
    for piece in range(pieces):
        lanes = slice(piece * LANES, (piece + 1) * LANES)
        rows = jnp.where(line == piece, high[:, lanes], rows)
        rows = jnp.where(line == pieces + piece, (bias_total - high)[:, lanes], rows)
    pay_ref[:, pieces * tall :, :] = jnp.broadcast_to(rows.astype(bf16)[None], (parts, 8, LANES))
    for store in stores:
        store.wait()


def sums_kernel(scale, slots, hub_rows, back_ref, wn_ref, weight_ref, bias_ref, hub_ref):
    tall = slots + hub_rows + 16
    pieces = back_ref.shape[1] // tall
    sums = [
        jnp.sum(back_ref[:, piece * tall + slots : (piece + 1) * tall, :].astype(f32), axis=0)
        for piece in range(pieces)
    ]
    total = jnp.concatenate(sums, axis=1)
    weight_ref[...] = jnp.broadcast_to(total[hub_rows:].astype(bf16)[None], weight_ref.shape)
    tail = jnp.sum(back_ref[:, pieces * tall :, :].astype(f32), axis=0)
    bias_ref[...] = jnp.concatenate(
        [tail[piece : piece + 1] + tail[pieces + piece : pieces + piece + 1] for piece in range(pieces)], axis=1
    )
    hub = total[:hub_rows]
    high = hub.astype(bf16)
    low = (hub - high.astype(f32)).astype(bf16)
    hub_ref[...] = (dot(high, wn_ref[...], NT) + dot(low, wn_ref[...], NT)) * scale


def scatter_kernel(local_ref, grad_ref, out_ref):
    height = out_ref.shape[0]
    first = pl.program_id(0) * height
    total = None
    for start in range(0, grad_ref.shape[0], TILE):
        rows = index_rows(local_ref, start, TILE)
        part = dot(hits_by_column(rows, first, height), grad_ref[start : start + TILE, :])
        total = part if total is None else total + part
    out_ref[...] = total


def final_kernel(scale, slots, send_ref, back_ref, scat_ref, grad_ref, ws_ref, wn_ref, out_ref):
    height, width = out_ref.shape
    first = pl.program_id(0) * height
    count = send_ref.shape[1]
    pieces = width // LANES
    tall = back_ref.shape[1] // pieces // 16 * 16
    returned = jnp.concatenate(
        [back_ref[:, piece * tall : piece * tall + slots, :].reshape(count, LANES) for piece in range(pieces)], axis=1
    )
    total = scat_ref[...]
    for start in range(0, count, 512):
        stop = min(count, start + 512)
        hits = hits_by_column([send_ref[:, start:stop]], first, height)
        total = total + dot(hits, returned[start:stop])
    out_ref[...] = dot(grad_ref[...], ws_ref[...], NT) + dot((total * scale).astype(bf16), wn_ref[...], NT)


def call(
    kernel, ins, in_specs, outs, out_specs, name, grid=(), scratch=(), flops=0, moved=0, limit=SOME_VMEM
):
    return pl.pallas_call(
        kernel,
        grid=grid,
        in_specs=in_specs,
        out_specs=out_specs,
        out_shape=outs,
        scratch_shapes=scratch,
        compiler_params=params(limit),
        cost_estimate=cost(flops, moved),
        name=name,
    )(*ins)


def whole_block(shape):
    return pl.BlockSpec(shape, lambda *_: (0,) * len(shape))


def body(
    features,
    hub_features,
    w_self,
    w_neigh,
    out_bias,
    local_edges,
    hub_edges,
    remote_edges,
    send_rows,
    cotangent,
):
    nodes, width = features.shape
    hub_rows = hub_features.shape[0]
    parts = lax.axis_size(AXES)
    slots = send_rows.shape[1] // parts
    slab = slots + hub_rows
    pieces = width // LANES
    pay = pieces * (slab + 16) + 8
    table = parts * slab
    scale = 1.0 / (local_edges.shape[1] + hub_edges.shape[1] + remote_edges.shape[1])
    local_t, hub_t, remote_t = local_edges.T, hub_edges.T, remote_edges.T
    bias = out_bias.reshape(1, width)
    shape = jax.ShapeDtypeStruct

    def exchange(value):
        return lax.all_to_all(value, AXES, split_axis=0, concat_axis=0, tiled=True)

    sending = call(
        pick_kernel,
        (send_rows, features, hub_features),
        [VMEM, VMEM, VMEM],
        shape((parts, slab, width), bf16),
        whole_block((parts, slab, width)),
        "pick_rows",
        limit=MOST_VMEM,
        flops=2 * parts * slots * nodes * width,
        moved=nodes * width * 2,
    )
    sending, features = lax.optimization_barrier((sending, features))
    received = exchange(sending)

    block = TILE
    by_block = pl.BlockSpec((block, width), lambda i: (i, 0))
    packed = 2 * width + table
    local_sum, pack = call(
        functools.partial(local_kernel, parts * slots),
        (local_t, remote_t, hub_t, features, features, cotangent),
        [pl.BlockSpec((edges.shape[0], block), lambda i: (0, i)) for edges in (local_t, remote_t, hub_t)]
        + [whole_block((nodes, width)), by_block, by_block],
        [shape((nodes, width), f32), pltpu.HBM((nodes, packed), bf16)],
        [by_block, pl.BlockSpec((block, packed), lambda i: (i, 0))],
        "local_gather",
        grid=(nodes // block,),
        flops=8 * nodes * nodes * width,
        moved=nodes * packed * 2,
    )

    activated, grad_pre, terms = call(
        functools.partial(middle_kernel, scale, slots),
        [received, w_self, w_neigh, bias, local_sum, pack],
        [VMEM] * 5 + [HBM],
        [pltpu.HBM((nodes, width), bf16)] * 2 + [shape((parts, pay, LANES), bf16)],
        [HBM] * 2 + [VMEM],
        "activate",
        scratch=[
            pltpu.VMEM((nodes, packed + width), bf16),
            pltpu.VMEM((nodes, width), bf16),
            pltpu.VMEM((nodes, width), bf16),
            pltpu.VMEM((width, 2 * width + table), f32),
            pltpu.SemaphoreType.DMA((2, nodes // (2 * TILE))),
            pltpu.SemaphoreType.DMA((2, nodes // (2 * TILE))),
        ],
        flops=4 * nodes * table * width,
        moved=nodes * packed * 2,
    )
    back = exchange(terms)

    scattered = call(
        scatter_kernel,
        (local_t, grad_pre),
        [whole_block(local_t.shape), whole_block((nodes, width))],
        shape((nodes, width), f32),
        pl.BlockSpec((block, width), lambda i: (i, 0)),
        "local_scatter",
        grid=(nodes // block,),
        flops=8 * nodes * nodes * width,
        moved=nodes * width * 6,
    )
    weight_rows, grad_bias, grad_hubs = call(
        functools.partial(sums_kernel, scale, slots, hub_rows),
        (back, w_neigh),
        [VMEM, VMEM],
        [shape((parts, 16, width), bf16), shape((1, width), f32), shape((hub_rows, width), f32)],
        [whole_block((parts, 16, width)), whole_block((1, width)), whole_block((hub_rows, width))],
        "sums",
        moved=parts * pay * width * 2,
    )
    weights = exchange(weight_rows)

    height = 2 * TILE
    by_height = pl.BlockSpec((height, width), lambda i: (i, 0))
    grad_features = call(
        functools.partial(final_kernel, scale, slots),
        (send_rows, back, scattered, grad_pre, w_self, w_neigh),
        [whole_block(send_rows.shape), whole_block((parts, pay, LANES)), by_height, by_height]
        + [whole_block((width, width))] * 2,
        shape((nodes, width), f32),
        by_height,
        "return_scatter",
        grid=(nodes // height,),
        flops=2 * nodes * parts * slots * width,
        moved=nodes * width * 10,
    )
    weights = weights[: 2 * width // 16].reshape(2, width, width).astype(f32)
    return (activated, grad_features, grad_hubs, weights[0], weights[1], grad_bias.reshape(width))


def solution(mesh):
    split = P(AXES, None)
    return jax.shard_map(
        body,
        mesh=mesh,
        in_specs=(split, split, P(), P(), P(), split, split, split, split, split),
        out_specs=(split, split, split, P(), P(), P()),
        check_vma=False,
    )
```

```python
import functools

import jax
import jax.numpy as jnp
from jax import lax
from jax.experimental import pallas as pl
from jax.experimental.pallas import tpu as pltpu
from jax.sharding import PartitionSpec as P

AXES = ("row", "col")
LANES = 128
TILE = 256
MOST_VMEM = 61952 * 1024
SOME_VMEM = 44 * 1024 * 1024
MUCH_VMEM = 50 * 1024 * 1024
NT = (((1,), (1,)), ((), ()))
TN = (((0,), (0,)), ((), ()))
VMEM = pl.BlockSpec(memory_space=pltpu.VMEM)
SMEM = pl.BlockSpec(memory_space=pltpu.SMEM)
HBM = pl.BlockSpec(memory_space=pltpu.HBM)
bf16, f32 = jnp.bfloat16, jnp.float32


def params(limit):
    return pltpu.CompilerParams(vmem_limit_bytes=limit)


def cost(flops, moved):
    return pl.CostEstimate(flops=int(flops), bytes_accessed=int(moved), transcendentals=0)


def along_rows(index_row):
    count = index_row.shape[1]
    return jnp.transpose(jnp.broadcast_to(index_row, (LANES, count))).astype(jnp.int16)


def stack_rows(value, height):
    count = value.shape[1]
    return jnp.broadcast_to(value[None], (height // 16, 16, count)).reshape(height, count)


def count_hits(entries, here):
    one, zero = jnp.ones(here.shape, bf16), jnp.zeros(here.shape, bf16)
    total = None
    for entry in entries:
        hit = jnp.where(entry == here, one, zero)
        total = hit if total is None else total + hit
    return total


def hits_by_row(columns, first, width):
    rows = columns[0].shape[0]
    lane = lax.broadcasted_iota(jnp.int32, (16, LANES), 1).astype(jnp.int16)
    tiles = [
        count_hits(columns, stack_rows(lane + jnp.int16(start), rows)) for start in range(first, first + width, LANES)
    ]
    return jnp.concatenate(tiles, axis=1) if len(tiles) > 1 else tiles[0]


def hits_by_column(index_rows, first, height):
    count = index_rows[0].shape[1]
    group = 64
    down = lax.broadcasted_iota(jnp.int32, (group, count), 0).astype(jnp.int16)
    entries = [
        stack_rows(jnp.broadcast_to(row - first, (16, count)).astype(jnp.int16), group) for row in index_rows
    ]
    return jnp.concatenate(
        [count_hits(entries, down + jnp.int16(start)) for start in range(0, height, group)], axis=0
    )


def dot(a, b, dims=(((1,), (0,)), ((), ()))):
    return lax.dot_general(a, b, dims, preferred_element_type=f32)


def index_rows(ref, start, count):
    return [ref[j : j + 1, pl.ds(start, count)] for j in range(ref.shape[0])]


def pick_kernel(send_ref, feat_ref, hub_ref, out_ref):
    parts, slab, width = out_ref.shape
    hub_rows = hub_ref.shape[0]
    slots = slab - hub_rows
    total = send_ref.shape[1]
    step = min(512, total)
    for start in range(0, total, step):
        column = along_rows(send_ref[:, start : start + step])
        picked = dot(hits_by_row([column], 0, feat_ref.shape[0]), feat_ref[...])
        out_ref[start // slots : (start + step) // slots, :slots, :] = (
            picked.astype(bf16).reshape(step // slots, slots, width)
        )
    out_ref[:, slots:, :] = jnp.broadcast_to(hub_ref[...][None], (parts, hub_rows, width))


def local_kernel(split, local_ref, remote_ref, hub_ref, feat_ref, own_ref, cot_ref, sum_ref, pack_ref):
    nodes, width = feat_ref.shape
    columns = [along_rows(row) for row in index_rows(local_ref, 0, TILE)]
    total = None
    for first in range(0, nodes, TILE):
        part = dot(hits_by_row(columns, first, TILE), feat_ref[first : first + TILE, :])
        total = part if total is None else total + part
    sum_ref[...] = total
    pack_ref[:, :width] = cot_ref[...]
    pack_ref[:, width : 2 * width] = own_ref[...]
    place = 2 * width
    counts = pack_ref.shape[1] - place
    for ref, share in ((remote_ref, split), (hub_ref, counts - split)):
        columns = [along_rows(row) for row in index_rows(ref, 0, TILE)]
        for first in range(0, share, TILE):
            pack_ref[:, place + first : place + first + TILE] = hits_by_row(columns, first, TILE)
        place += share


def middle_kernel(
    scale,
    slots,
    table_ref,
    ws_ref,
    wn_ref,
    bias_ref,
    sum_ref,
    pack_hbm,
    act_hbm,
    grad_hbm,
    pay_ref,
    pack,
    act,
    grad_all,
    terms,
    in_sem,
    out_sem,
):
    nodes, width = sum_ref.shape
    parts, slab, _ = table_ref.shape
    hub_rows = slab - slots
    bounds, hubs = parts * slots, parts * hub_rows
    size = 2 * TILE
    blocks = nodes // size
    features, counts = slice(width, 2 * width), 3 * width

    def here(block):
        return slice(block * size, (block + 1) * size)

    def loads(block):
        at = here(block)
        return [
            pltpu.make_async_copy(pack_hbm.at[at, : 2 * width], pack.at[at, : 2 * width], in_sem.at[0, block]),
            pltpu.make_async_copy(pack_hbm.at[at, 2 * width :], pack.at[at, counts:], in_sem.at[1, block]),
        ]

    coming = [loads(block) for block in range(blocks)]
    for group in coming:
        for copy in group:
            copy.start()
    table = jnp.concatenate(
        [table_ref[:, :slots, :].reshape(bounds, width), table_ref[:, slots:, :].reshape(hubs, width)], axis=0
    )
    half_weights = jnp.concatenate([ws_ref[...], wn_ref[...]], axis=0) * jnp.bfloat16(0.5)
    half_bias = 0.5 * bias_ref[...]
    stores = []
    total = None
    turned = None
    for block in range(blocks + 2):
        following = None
        if block < blocks:
            for copy in coming[block]:
                copy.wait()
            following = sum_ref[here(block), :] + dot(pack[here(block), counts:], table)
        if block > 1:
            part = dot(turned, pack[here(block - 2), width:])
            terms[...] = part if block == 2 else terms[...] + part
        if 0 < block <= blocks:
            at = here(block - 1)
            pack[at, 2 * width : counts] = (total * scale).astype(bf16)
            half = dot(pack[at, width:counts], half_weights) + half_bias
            tanh = jnp.tanh(half)
            above = 1.0 + tanh
            act[at, :] = (half * above).astype(bf16)
            slope = above * (0.5 + (0.5 * half) * (1.0 - tanh))
            grad = (pack[at, :width].astype(f32) * slope).astype(bf16)
            grad_all[at, :] = grad
            turned = jnp.transpose(grad)
            for which, (source, target) in enumerate(((act, act_hbm), (grad_all, grad_hbm))):
                store = pltpu.make_async_copy(source.at[at, :], target.at[at, :], out_sem.at[which, block - 1])
                store.start()
                stores.append(store)
        total = following

    pieces = width // LANES
    tall = slab + 16

    def put(low, high, place, rows, value):
        value = value.astype(bf16).reshape(high - low, rows, width)
        for piece in range(pieces):
            at = piece * tall + place
            pay_ref[low:high, at : at + rows, :] = value[:, :, piece * LANES : (piece + 1) * LANES]

    def term_rows(first, count):
        return jnp.transpose(terms[:, first : first + count])

    holders = 2 * width // 16
    put(0, holders, slab, 16, term_rows(0, 2 * width))
    if parts > holders:
        put(holders, parts, slab, 16, jnp.zeros(((parts - holders) * 16, width), f32))
    step = 2 * width
    for low, total_rows, place, rows in ((0, bounds, 0, slots), (bounds, hubs, slots, hub_rows)):
        for first in range(0, total_rows, step):
            put(first // rows, (first + step) // rows, place, rows, term_rows(2 * width + low + first, step))
    bias_total = dot(jnp.ones((16, nodes), bf16), grad_all[...])[:1]
    high = bias_total.astype(bf16).astype(f32)
    line = lax.broadcasted_iota(jnp.int32, (8, LANES), 0)
    rows = jnp.zeros((8, LANES), f32)
    for piece in range(pieces):
        lanes = slice(piece * LANES, (piece + 1) * LANES)
        rows = jnp.where(line == piece, high[:, lanes], rows)
        rows = jnp.where(line == pieces + piece, (bias_total - high)[:, lanes], rows)
    pay_ref[:, pieces * tall :, :] = jnp.broadcast_to(rows.astype(bf16)[None], (parts, 8, LANES))
    for store in stores:
        store.wait()


def sums_kernel(scale, slots, hub_rows, back_ref, wn_ref, weight_ref, bias_ref, hub_ref):
    tall = slots + hub_rows + 16
    pieces = back_ref.shape[1] // tall
    sums = [
        jnp.sum(back_ref[:, piece * tall + slots : (piece + 1) * tall, :].astype(f32), axis=0)
        for piece in range(pieces)
    ]
    total = jnp.concatenate(sums, axis=1)
    weight_ref[...] = jnp.broadcast_to(total[hub_rows:].astype(bf16)[None], weight_ref.shape)
    tail = jnp.sum(back_ref[:, pieces * tall :, :].astype(f32), axis=0)
    bias_ref[...] = jnp.concatenate(
        [tail[piece : piece + 1] + tail[pieces + piece : pieces + piece + 1] for piece in range(pieces)], axis=1
    )
    hub = total[:hub_rows]
    high = hub.astype(bf16)
    low = (hub - high.astype(f32)).astype(bf16)
    hub_ref[...] = (dot(high, wn_ref[...], NT) + dot(low, wn_ref[...], NT)) * scale


def scatter_kernel(local_ref, grad_ref, out_ref):
    height = out_ref.shape[0]
    first = pl.program_id(0) * height
    total = None
    for start in range(0, grad_ref.shape[0], TILE):
        rows = index_rows(local_ref, start, TILE)
        part = dot(hits_by_column(rows, first, height), grad_ref[start : start + TILE, :])
        total = part if total is None else total + part
    out_ref[...] = total


def final_kernel(scale, slots, send_ref, back_ref, scat_ref, grad_ref, ws_ref, wn_ref, out_ref):
    height, width = out_ref.shape
    first = pl.program_id(0) * height
    count = send_ref.shape[1]
    pieces = width // LANES
    tall = back_ref.shape[1] // pieces // 16 * 16
    returned = jnp.concatenate(
        [back_ref[:, piece * tall : piece * tall + slots, :].reshape(count, LANES) for piece in range(pieces)], axis=1
    )
    total = scat_ref[...]
    for start in range(0, count, 512):
        stop = min(count, start + 512)
        hits = hits_by_column([send_ref[:, start:stop]], first, height)
        total = total + dot(hits, returned[start:stop])
    out_ref[...] = dot(grad_ref[...], ws_ref[...], NT) + dot((total * scale).astype(bf16), wn_ref[...], NT)


def call(
    kernel, ins, in_specs, outs, out_specs, name, grid=(), scratch=(), flops=0, moved=0, limit=SOME_VMEM
):
    return pl.pallas_call(
        kernel,
        grid=grid,
        in_specs=in_specs,
        out_specs=out_specs,
        out_shape=outs,
        scratch_shapes=scratch,
        compiler_params=params(limit),
        cost_estimate=cost(flops, moved),
        name=name,
    )(*ins)


def whole_block(shape):
    return pl.BlockSpec(shape, lambda *_: (0,) * len(shape))


def body(
    features,
    hub_features,
    w_self,
    w_neigh,
    out_bias,
    local_edges,
    hub_edges,
    remote_edges,
    send_rows,
    cotangent,
):
    nodes, width = features.shape
    hub_rows = hub_features.shape[0]
    parts = lax.axis_size(AXES)
    slots = send_rows.shape[1] // parts
    slab = slots + hub_rows
    pieces = width // LANES
    pay = pieces * (slab + 16) + 8
    table = parts * slab
    scale = 1.0 / (local_edges.shape[1] + hub_edges.shape[1] + remote_edges.shape[1])
    local_t, hub_t, remote_t = local_edges.T, hub_edges.T, remote_edges.T
    bias = out_bias.reshape(1, width)
    shape = jax.ShapeDtypeStruct

    def exchange(value):
        return lax.all_to_all(value, AXES, split_axis=0, concat_axis=0, tiled=True)

    sending = call(
        pick_kernel,
        (send_rows, features, hub_features),
        [VMEM, VMEM, VMEM],
        shape((parts, slab, width), bf16),
        whole_block((parts, slab, width)),
        "pick_rows",
        limit=MOST_VMEM,
        flops=2 * parts * slots * nodes * width,
        moved=nodes * width * 2,
    )
    sending, features = lax.optimization_barrier((sending, features))
    received = exchange(sending)

    block = TILE
    by_block = pl.BlockSpec((block, width), lambda i: (i, 0))
    packed = 2 * width + table
    local_sum, pack = call(
        functools.partial(local_kernel, parts * slots),
        (local_t, remote_t, hub_t, features, features, cotangent),
        [pl.BlockSpec((edges.shape[0], block), lambda i: (0, i)) for edges in (local_t, remote_t, hub_t)]
        + [whole_block((nodes, width)), by_block, by_block],
        [shape((nodes, width), f32), pltpu.HBM((nodes, packed), bf16)],
        [by_block, pl.BlockSpec((block, packed), lambda i: (i, 0))],
        "local_gather",
        grid=(nodes // block,),
        flops=8 * nodes * nodes * width,
        moved=nodes * packed * 2,
    )

    activated, grad_pre, terms = call(
        functools.partial(middle_kernel, scale, slots),
        [received, w_self, w_neigh, bias, local_sum, pack],
        [VMEM] * 5 + [HBM],
        [pltpu.HBM((nodes, width), bf16)] * 2 + [shape((parts, pay, LANES), bf16)],
        [HBM] * 2 + [VMEM],
        "activate",
        limit=MUCH_VMEM,
        scratch=[
            pltpu.VMEM((nodes, packed + width), bf16),
            pltpu.VMEM((nodes, width), bf16),
            pltpu.VMEM((nodes, width), bf16),
            pltpu.VMEM((width, 2 * width + table), f32),
            pltpu.SemaphoreType.DMA((2, nodes // (2 * TILE))),
            pltpu.SemaphoreType.DMA((2, nodes // (2 * TILE))),
        ],
        flops=4 * nodes * table * width,
        moved=nodes * packed * 2,
    )
    back = exchange(terms)

    scattered = call(
        scatter_kernel,
        (local_t, grad_pre),
        [whole_block(local_t.shape), whole_block((nodes, width))],
        shape((nodes, width), f32),
        pl.BlockSpec((block, width), lambda i: (i, 0)),
        "local_scatter",
        grid=(nodes // block,),
        flops=8 * nodes * nodes * width,
        moved=nodes * width * 6,
    )
    weight_rows, grad_bias, grad_hubs = call(
        functools.partial(sums_kernel, scale, slots, hub_rows),
        (back, w_neigh),
        [VMEM, VMEM],
        [shape((parts, 16, width), bf16), shape((1, width), f32), shape((hub_rows, width), f32)],
        [whole_block((parts, 16, width)), whole_block((1, width)), whole_block((hub_rows, width))],
        "sums",
        moved=parts * pay * width * 2,
    )
    weights = exchange(weight_rows)

    height = 2 * TILE
    by_height = pl.BlockSpec((height, width), lambda i: (i, 0))
    grad_features = call(
        functools.partial(final_kernel, scale, slots),
        (send_rows, back, scattered, grad_pre, w_self, w_neigh),
        [whole_block(send_rows.shape), whole_block((parts, pay, LANES)), by_height, by_height]
        + [whole_block((width, width))] * 2,
        shape((nodes, width), f32),
        by_height,
        "return_scatter",
        grid=(nodes // height,),
        flops=2 * nodes * parts * slots * width,
        moved=nodes * width * 10,
    )
    weights = weights[: 2 * width // 16].reshape(2, width, width).astype(f32)
    return (activated, grad_features, grad_hubs, weights[0], weights[1], grad_bias.reshape(width))


def solution(mesh):
    split = P(AXES, None)
    return jax.shard_map(
        body,
        mesh=mesh,
        in_specs=(split, split, P(), P(), P(), split, split, split, split, split),
        out_specs=(split, split, split, P(), P(), P()),
        check_vma=False,
    )
```

```python
import functools

import jax
import jax.numpy as jnp
from jax import lax
from jax.experimental import pallas as pl
from jax.experimental.pallas import tpu as pltpu
from jax.sharding import PartitionSpec as P

AXES = ("row", "col")
LANES = 128
TILE = 256
MOST_VMEM = 61952 * 1024
SOME_VMEM = 44 * 1024 * 1024
MUCH_VMEM = 47 * 1024 * 1024
NT = (((1,), (1,)), ((), ()))
TN = (((0,), (0,)), ((), ()))
VMEM = pl.BlockSpec(memory_space=pltpu.VMEM)
SMEM = pl.BlockSpec(memory_space=pltpu.SMEM)
HBM = pl.BlockSpec(memory_space=pltpu.HBM)
bf16, f32 = jnp.bfloat16, jnp.float32


def params(limit):
    return pltpu.CompilerParams(vmem_limit_bytes=limit)


def cost(flops, moved):
    return pl.CostEstimate(flops=int(flops), bytes_accessed=int(moved), transcendentals=0)


def along_rows(index_row):
    count = index_row.shape[1]
    return jnp.transpose(jnp.broadcast_to(index_row, (LANES, count))).astype(jnp.int16)


def stack_rows(value, height):
    count = value.shape[1]
    return jnp.broadcast_to(value[None], (height // 16, 16, count)).reshape(height, count)


def count_hits(entries, here):
    one, zero = jnp.ones(here.shape, bf16), jnp.zeros(here.shape, bf16)
    total = None
    for entry in entries:
        hit = jnp.where(entry == here, one, zero)
        total = hit if total is None else total + hit
    return total


def hits_by_row(columns, first, width):
    rows = columns[0].shape[0]
    lane = lax.broadcasted_iota(jnp.int32, (16, LANES), 1).astype(jnp.int16)
    tiles = [
        count_hits(columns, stack_rows(lane + jnp.int16(start), rows)) for start in range(first, first + width, LANES)
    ]
    return jnp.concatenate(tiles, axis=1) if len(tiles) > 1 else tiles[0]


def hits_by_column(index_rows, first, height):
    count = index_rows[0].shape[1]
    group = 64
    down = lax.broadcasted_iota(jnp.int32, (group, count), 0).astype(jnp.int16)
    entries = [
        stack_rows(jnp.broadcast_to(row - first, (16, count)).astype(jnp.int16), group) for row in index_rows
    ]
    return jnp.concatenate(
        [count_hits(entries, down + jnp.int16(start)) for start in range(0, height, group)], axis=0
    )


def dot(a, b, dims=(((1,), (0,)), ((), ()))):
    return lax.dot_general(a, b, dims, preferred_element_type=f32)


def index_rows(ref, start, count):
    return [ref[j : j + 1, pl.ds(start, count)] for j in range(ref.shape[0])]


def pick_kernel(send_ref, feat_ref, hub_ref, out_ref):
    parts, slab, width = out_ref.shape
    hub_rows = hub_ref.shape[0]
    slots = slab - hub_rows
    total = send_ref.shape[1]
    step = min(512, total)
    for start in range(0, total, step):
        column = along_rows(send_ref[:, start : start + step])
        picked = dot(hits_by_row([column], 0, feat_ref.shape[0]), feat_ref[...])
        out_ref[start // slots : (start + step) // slots, :slots, :] = (
            picked.astype(bf16).reshape(step // slots, slots, width)
        )
    out_ref[:, slots:, :] = jnp.broadcast_to(hub_ref[...][None], (parts, hub_rows, width))


def local_kernel(split, local_ref, remote_ref, hub_ref, feat_ref, own_ref, cot_ref, sum_ref, pack_ref):
    nodes, width = feat_ref.shape
    columns = [along_rows(row) for row in index_rows(local_ref, 0, TILE)]
    total = None
    for first in range(0, nodes, TILE):
        part = dot(hits_by_row(columns, first, TILE), feat_ref[first : first + TILE, :])
        total = part if total is None else total + part
    sum_ref[...] = total
    pack_ref[:, :width] = cot_ref[...]
    pack_ref[:, width : 2 * width] = own_ref[...]
    place = 2 * width
    counts = pack_ref.shape[1] - place
    for ref, share in ((remote_ref, split), (hub_ref, counts - split)):
        columns = [along_rows(row) for row in index_rows(ref, 0, TILE)]
        for first in range(0, share, TILE):
            pack_ref[:, place + first : place + first + TILE] = hits_by_row(columns, first, TILE)
        place += share


def middle_kernel(
    scale,
    slots,
    core_ref,
    table_ref,
    ws_ref,
    wn_ref,
    bias_ref,
    sum_ref,
    pack_hbm,
    act_hbm,
    grad_hbm,
    bound_ref,
    keep_ref,
    give_ref,
    pack,
    act,
    grad_all,
    terms,
    in_sem,
    out_sem,
):
    nodes, width = sum_ref.shape
    parts, slab, _ = table_ref.shape
    hub_rows = slab - slots
    bounds, hubs = parts * slots, parts * hub_rows
    size = 2 * TILE
    blocks = nodes // size
    features, counts = slice(width, 2 * width), 3 * width

    def here(block):
        return slice(block * size, (block + 1) * size)

    def loads(block):
        at = here(block)
        return [
            pltpu.make_async_copy(pack_hbm.at[at, : 2 * width], pack.at[at, : 2 * width], in_sem.at[0, block]),
            pltpu.make_async_copy(pack_hbm.at[at, 2 * width :], pack.at[at, counts:], in_sem.at[1, block]),
        ]

    coming = [loads(block) for block in range(blocks)]
    for group in coming:
        for copy in group:
            copy.start()
    table = jnp.concatenate(
        [table_ref[:, :slots, :].reshape(bounds, width), table_ref[:, slots:, :].reshape(hubs, width)], axis=0
    )
    half_weights = jnp.concatenate([ws_ref[...], wn_ref[...]], axis=0) * jnp.bfloat16(0.5)
    half_bias = 0.5 * bias_ref[...]
    stores = []
    total = None
    turned = None
    for block in range(blocks + 2):
        following = None
        if block < blocks:
            for copy in coming[block]:
                copy.wait()
            following = sum_ref[here(block), :] + dot(pack[here(block), counts:], table)
        if block > 1:
            part = dot(turned, pack[here(block - 2), width:])
            terms[...] = part if block == 2 else terms[...] + part
        if 0 < block <= blocks:
            at = here(block - 1)
            pack[at, 2 * width : counts] = (total * scale).astype(bf16)
            half = dot(pack[at, width:counts], half_weights) + half_bias
            tanh = jnp.tanh(half)
            above = 1.0 + tanh
            act[at, :] = (half * above).astype(bf16)
            slope = above * (0.5 + (0.5 * half) * (1.0 - tanh))
            grad = (pack[at, :width].astype(f32) * slope).astype(bf16)
            grad_all[at, :] = grad
            turned = jnp.transpose(grad)
            for which, (source, target) in enumerate(((act, act_hbm), (grad_all, grad_hbm))):
                store = pltpu.make_async_copy(source.at[at, :], target.at[at, :], out_sem.at[which, block - 1])
                store.start()
                stores.append(store)
        total = following

    pieces = width // LANES
    step = 2 * width

    def term_rows(first, rows):
        return jnp.transpose(terms[:, first : first + step]).reshape(step // rows, rows, width)

    def lanes(piece):
        return slice(piece * LANES, (piece + 1) * LANES)

    first_core = core_ref[0] == 0
    half = hub_rows // 2
    weights = term_rows(0, hub_rows)
    for low in range(0, hubs, step):
        hub_terms = term_rows(step + bounds + low, hub_rows)
        if low > 0:
            weights = jnp.zeros_like(weights)
        front = jnp.concatenate([hub_terms[:, :half], weights[:, :half]], axis=1)
        back = jnp.concatenate([hub_terms[:, half:], weights[:, half:]], axis=1)
        keep, give = jnp.where(first_core, front, back), jnp.where(first_core, back, front).astype(bf16)
        at = slice(low // hub_rows, (low + step) // hub_rows)
        for piece in range(pieces):
            there = slice(piece * hub_rows, (piece + 1) * hub_rows)
            keep_ref[at, there, :] = keep[:, :, lanes(piece)]
            give_ref[at, there, :] = give[:, :, lanes(piece)]
    bias_total = dot(jnp.ones((16, nodes), bf16), grad_all[...])[:1]
    rows = bias_rows([bias_total[:, lanes(piece)] for piece in range(pieces)])
    keep_ref[:, pieces * hub_rows :, :] = jnp.broadcast_to(rows[None], (parts, 8, LANES))
    give_ref[:, pieces * hub_rows :, :] = jnp.broadcast_to(rows.astype(bf16)[None], (parts, 8, LANES))
    for low in range(0, bounds, step):
        bound_terms = term_rows(step + low, slots).astype(bf16)
        for piece in range(pieces):
            bound_ref[low // slots : (low + step) // slots, piece * slots : (piece + 1) * slots, :] = (
                bound_terms[:, :, lanes(piece)]
            )
    for store in stores:
        store.wait()


def bias_rows(parts):
    line = lax.broadcasted_iota(jnp.int32, (8, LANES), 0)
    rows = jnp.zeros((8, LANES), f32)
    for piece, value in enumerate(parts):
        high = value.astype(bf16).astype(f32)
        rows = jnp.where(line == piece, high, rows)
        rows = jnp.where(line == len(parts) + piece, value - high, rows)
    return rows


def join_kernel(bound_ref, keep_ref, got_ref, out_ref):
    parts, tall, _ = keep_ref.shape
    place = bound_ref.shape[1]
    pieces = (tall - 8) // 16
    out_ref[:, :place, :] = bound_ref[...]
    both = keep_ref[:, : tall - 8, :] + got_ref[:, : tall - 8, :].astype(f32)
    out_ref[:, place : place + tall - 8, :] = both.astype(bf16)
    tail = keep_ref[0, tall - 8 :, :] + got_ref[0, tall - 8 :, :].astype(f32)
    rows = bias_rows([tail[piece : piece + 1] + tail[pieces + piece : pieces + piece + 1] for piece in range(pieces)])
    out_ref[:, place + tall - 8 :, :] = jnp.broadcast_to(rows.astype(bf16)[None], (parts, 8, LANES))


def sums_kernel(scale, slots, hub_rows, rows, back_ref, wn_ref, weight_ref, bias_ref, hub_ref):
    parts, tall, _ = back_ref.shape
    pieces = (tall - 8) // (slots + hub_rows)
    half = hub_rows // 2
    whole = back_ref[:, pieces * slots :, :].astype(f32)
    count = whole.shape[1]
    whole = whole.reshape(rows // 2, 2, parts // rows, count, LANES)
    total = jnp.sum(jnp.sum(whole, axis=2), axis=0)

    def table(first):
        return jnp.concatenate(
            [
                jnp.concatenate([total[core, piece * hub_rows + first : piece * hub_rows + first + half] for core in (0, 1)], axis=0)
                for piece in range(pieces)
            ],
            axis=1,
        )

    weight_ref[...] = jnp.broadcast_to(table(half).astype(bf16)[None], weight_ref.shape)
    tail = 0.5 * (total[0, count - 8 :] + total[1, count - 8 :])
    bias_ref[...] = jnp.concatenate(
        [tail[piece : piece + 1] + tail[pieces + piece : pieces + piece + 1] for piece in range(pieces)], axis=1
    )
    hub = table(0)
    high = hub.astype(bf16)
    low = (hub - high.astype(f32)).astype(bf16)
    hub_ref[...] = (dot(high, wn_ref[...], NT) + dot(low, wn_ref[...], NT)) * scale


def scatter_kernel(local_ref, grad_ref, out_ref):
    height = out_ref.shape[0]
    first = pl.program_id(0) * height
    total = None
    for start in range(0, grad_ref.shape[0], TILE):
        rows = index_rows(local_ref, start, TILE)
        part = dot(hits_by_column(rows, first, height), grad_ref[start : start + TILE, :])
        total = part if total is None else total + part
    out_ref[...] = total


def final_kernel(scale, slots, send_ref, back_ref, scat_ref, grad_ref, ws_ref, wn_ref, out_ref):
    height, width = out_ref.shape
    first = pl.program_id(0) * height
    count = send_ref.shape[1]
    returned = jnp.concatenate(
        [
            back_ref[:, piece * slots : (piece + 1) * slots, :].reshape(count, LANES)
            for piece in range(width // LANES)
        ],
        axis=1,
    )
    total = scat_ref[...]
    for start in range(0, count, 512):
        stop = min(count, start + 512)
        hits = hits_by_column([send_ref[:, start:stop]], first, height)
        total = total + dot(hits, returned[start:stop])
    out_ref[...] = dot(grad_ref[...], ws_ref[...], NT) + dot((total * scale).astype(bf16), wn_ref[...], NT)


def call(
    kernel, ins, in_specs, outs, out_specs, name, grid=(), scratch=(), flops=0, moved=0, limit=SOME_VMEM
):
    return pl.pallas_call(
        kernel,
        grid=grid,
        in_specs=in_specs,
        out_specs=out_specs,
        out_shape=outs,
        scratch_shapes=scratch,
        compiler_params=params(limit),
        cost_estimate=cost(flops, moved),
        name=name,
    )(*ins)


def whole_block(shape):
    return pl.BlockSpec(shape, lambda *_: (0,) * len(shape))


def body(
    features,
    hub_features,
    w_self,
    w_neigh,
    out_bias,
    local_edges,
    hub_edges,
    remote_edges,
    send_rows,
    cotangent,
):
    nodes, width = features.shape
    hub_rows = hub_features.shape[0]
    parts = lax.axis_size(AXES)
    slots = send_rows.shape[1] // parts
    slab = slots + hub_rows
    pieces = width // LANES
    pay = pieces * slab + 8
    core = (lax.axis_index("row") % 2).astype(jnp.int32).reshape(1)
    rows = lax.axis_size("row")
    table = parts * slab
    scale = 1.0 / (local_edges.shape[1] + hub_edges.shape[1] + remote_edges.shape[1])
    local_t, hub_t, remote_t = local_edges.T, hub_edges.T, remote_edges.T
    bias = out_bias.reshape(1, width)
    shape = jax.ShapeDtypeStruct

    def exchange(value):
        return lax.all_to_all(value, AXES, split_axis=0, concat_axis=0, tiled=True)

    sending = call(
        pick_kernel,
        (send_rows, features, hub_features),
        [VMEM, VMEM, VMEM],
        shape((parts, slab, width), bf16),
        whole_block((parts, slab, width)),
        "pick_rows",
        limit=MOST_VMEM,
        flops=2 * parts * slots * nodes * width,
        moved=nodes * width * 2,
    )
    sending, features = lax.optimization_barrier((sending, features))
    received = exchange(sending)

    block = TILE
    by_block = pl.BlockSpec((block, width), lambda i: (i, 0))
    packed = 2 * width + table
    local_sum, pack = call(
        functools.partial(local_kernel, parts * slots),
        (local_t, remote_t, hub_t, features, features, cotangent),
        [pl.BlockSpec((edges.shape[0], block), lambda i: (0, i)) for edges in (local_t, remote_t, hub_t)]
        + [whole_block((nodes, width)), by_block, by_block],
        [shape((nodes, width), f32), pltpu.HBM((nodes, packed), bf16)],
        [by_block, pl.BlockSpec((block, packed), lambda i: (i, 0))],
        "local_gather",
        grid=(nodes // block,),
        flops=8 * nodes * nodes * width,
        moved=nodes * packed * 2,
    )

    activated, grad_pre, bound_terms, keep, give = call(
        functools.partial(middle_kernel, scale, slots),
        [core, received, w_self, w_neigh, bias, local_sum, pack],
        [SMEM] + [VMEM] * 5 + [HBM],
        [pltpu.HBM((nodes, width), bf16)] * 2
        + [
            shape((parts, pieces * slots, LANES), bf16),
            shape((parts, pieces * hub_rows + 8, LANES), f32),
            shape((parts, pieces * hub_rows + 8, LANES), bf16),
        ],
        [HBM] * 2 + [VMEM] * 3,
        "activate",
        limit=MUCH_VMEM,
        scratch=[
            pltpu.VMEM((nodes, packed + width), bf16),
            pltpu.VMEM((nodes, width), bf16),
            pltpu.VMEM((nodes, width), bf16),
            pltpu.VMEM((width, 2 * width + table), f32),
            pltpu.SemaphoreType.DMA((2, nodes // (2 * TILE))),
            pltpu.SemaphoreType.DMA((2, nodes // (2 * TILE))),
        ],
        flops=4 * nodes * table * width,
        moved=nodes * packed * 2,
    )
    got = lax.ppermute(give, "row", [(r, r ^ 1) for r in range(rows)])
    back = exchange(
        call(
            join_kernel,
            [bound_terms, keep, got],
            [VMEM] * 3,
            shape((parts, pay, LANES), bf16),
            VMEM,
            "join_siblings",
            moved=parts * pay * LANES * 6,
        )
    )

    scattered = call(
        scatter_kernel,
        (local_t, grad_pre),
        [whole_block(local_t.shape), whole_block((nodes, width))],
        shape((nodes, width), f32),
        pl.BlockSpec((block, width), lambda i: (i, 0)),
        "local_scatter",
        grid=(nodes // block,),
        flops=8 * nodes * nodes * width,
        moved=nodes * width * 6,
    )
    weight_rows, grad_bias, grad_hubs = call(
        functools.partial(sums_kernel, scale, slots, hub_rows, rows),
        (back, w_neigh),
        [VMEM, VMEM],
        [shape((parts, 16, width), bf16), shape((1, width), f32), shape((hub_rows, width), f32)],
        [whole_block((parts, 16, width)), whole_block((1, width)), whole_block((hub_rows, width))],
        "sums",
        moved=parts * pay * width * 2,
    )
    weights = exchange(weight_rows)

    height = 2 * TILE
    by_height = pl.BlockSpec((height, width), lambda i: (i, 0))
    grad_features = call(
        functools.partial(final_kernel, scale, slots),
        (send_rows, back, scattered, grad_pre, w_self, w_neigh),
        [whole_block(send_rows.shape), whole_block((parts, pay, LANES)), by_height, by_height]
        + [whole_block((width, width))] * 2,
        shape((nodes, width), f32),
        by_height,
        "return_scatter",
        grid=(nodes // height,),
        flops=2 * nodes * parts * slots * width,
        moved=nodes * width * 10,
    )
    weights = weights[: 2 * width // 16].reshape(2, width, width).astype(f32)
    return (activated, grad_features, grad_hubs, weights[0], weights[1], grad_bias.reshape(width))


def solution(mesh):
    split = P(AXES, None)
    return jax.shard_map(
        body,
        mesh=mesh,
        in_specs=(split, split, P(), P(), P(), split, split, split, split, split),
        out_specs=(split, split, split, P(), P(), P()),
        check_vma=False,
    )
```

```python
import functools

import jax
import jax.numpy as jnp
from jax import lax
from jax.experimental import pallas as pl
from jax.experimental.pallas import tpu as pltpu
from jax.sharding import PartitionSpec as P

AXES = ("row", "col")
LANES = 128
TILE = 256
MOST_VMEM = 61952 * 1024
SOME_VMEM = 44 * 1024 * 1024
MUCH_VMEM = 47 * 1024 * 1024
NT = (((1,), (1,)), ((), ()))
TN = (((0,), (0,)), ((), ()))
VMEM = pl.BlockSpec(memory_space=pltpu.VMEM)
SMEM = pl.BlockSpec(memory_space=pltpu.SMEM)
HBM = pl.BlockSpec(memory_space=pltpu.HBM)
bf16, f32 = jnp.bfloat16, jnp.float32


def params(limit):
    return pltpu.CompilerParams(vmem_limit_bytes=limit)


def cost(flops, moved):
    return pl.CostEstimate(flops=int(flops), bytes_accessed=int(moved), transcendentals=0)


def along_rows(index_row):
    count = index_row.shape[1]
    return jnp.transpose(jnp.broadcast_to(index_row, (LANES, count))).astype(jnp.int16)


def stack_rows(value, height):
    count = value.shape[1]
    return jnp.broadcast_to(value[None], (height // 16, 16, count)).reshape(height, count)


def count_hits(entries, here):
    one, zero = jnp.ones(here.shape, bf16), jnp.zeros(here.shape, bf16)
    total = None
    for entry in entries:
        hit = jnp.where(entry == here, one, zero)
        total = hit if total is None else total + hit
    return total


def hits_by_row(columns, first, width):
    rows = columns[0].shape[0]
    lane = lax.broadcasted_iota(jnp.int32, (16, LANES), 1).astype(jnp.int16)
    tiles = [
        count_hits(columns, stack_rows(lane + jnp.int16(start), rows)) for start in range(first, first + width, LANES)
    ]
    return jnp.concatenate(tiles, axis=1) if len(tiles) > 1 else tiles[0]


def hits_by_column(index_rows, first, height):
    count = index_rows[0].shape[1]
    group = 64
    down = lax.broadcasted_iota(jnp.int32, (group, count), 0).astype(jnp.int16)
    entries = [
        stack_rows(jnp.broadcast_to(row - first, (16, count)).astype(jnp.int16), group) for row in index_rows
    ]
    return jnp.concatenate(
        [count_hits(entries, down + jnp.int16(start)) for start in range(0, height, group)], axis=0
    )


def dot(a, b, dims=(((1,), (0,)), ((), ()))):
    return lax.dot_general(a, b, dims, preferred_element_type=f32)


def index_rows(ref, start, count):
    return [ref[j : j + 1, pl.ds(start, count)] for j in range(ref.shape[0])]


def by_core(value, rows, cols):
    half = value.shape[0] // 2
    value = value.astype(f32)
    halves = [value[core * half : (core + 1) * half] for core in (0, 1)]
    blocks = [jnp.broadcast_to(halves[row % 2][None], (cols,) + halves[0].shape) for row in range(rows)]
    return jnp.concatenate(blocks, axis=0).astype(bf16)


def pick_kernel(rows, send_ref, feat_ref, hub_ref, out_ref):
    parts, slab, width = out_ref.shape
    slots = slab - hub_ref.shape[0] // 2
    total = send_ref.shape[1]
    step = min(512, total)
    for start in range(0, total, step):
        column = along_rows(send_ref[:, start : start + step])
        picked = dot(hits_by_row([column], 0, feat_ref.shape[0]), feat_ref[...])
        out_ref[start // slots : (start + step) // slots, :slots, :] = (
            picked.astype(bf16).reshape(step // slots, slots, width)
        )
    out_ref[:, slots:, :] = by_core(hub_ref[...], rows, parts // rows)


def half_kernel(slots, table_ref, out_ref):
    out_ref[...] = table_ref[:, slots:, :].astype(f32).reshape(out_ref.shape).astype(bf16)


def local_kernel(split, hub_rows, core_ref, local_ref, remote_ref, hub_ref, feat_ref, own_ref, cot_ref, sum_ref, pack_ref):
    nodes, width = feat_ref.shape
    columns = [along_rows(row) for row in index_rows(local_ref, 0, TILE)]
    total = None
    for first in range(0, nodes, TILE):
        part = dot(hits_by_row(columns, first, TILE), feat_ref[first : first + TILE, :])
        total = part if total is None else total + part
    sum_ref[...] = total
    pack_ref[:, :width] = cot_ref[...]
    pack_ref[:, width : 2 * width] = own_ref[...]
    place = 2 * width
    counts = pack_ref.shape[1] - place
    half = hub_rows // 2
    hubs = []
    for hub in index_rows(hub_ref, 0, TILE):
        owner = lax.div(hub, jnp.int32(hub_rows))
        within = hub - owner * hub_rows
        other = (within >= half) != (core_ref[0] == 1)
        within = jnp.where(within >= half, within - half, within)
        hubs.append(owner * half + within + jnp.where(other, (counts - split) // 2, 0))
    for index, share in ((index_rows(remote_ref, 0, TILE), split), (hubs, counts - split)):
        columns = [along_rows(row) for row in index]
        for first in range(0, share, TILE):
            pack_ref[:, place + first : place + first + TILE] = hits_by_row(columns, first, TILE)
        place += share


def middle_kernel(
    scale,
    slots,
    core_ref,
    table_ref,
    near_ref,
    far_ref,
    ws_ref,
    wn_ref,
    bias_ref,
    sum_ref,
    pack_hbm,
    act_hbm,
    grad_hbm,
    bound_ref,
    keep_ref,
    give_ref,
    pack,
    act,
    grad_all,
    terms,
    in_sem,
    out_sem,
):
    nodes, width = sum_ref.shape
    parts, slab, _ = table_ref.shape
    half = slab - slots
    hub_rows = 2 * half
    bounds, hubs = parts * slots, parts * hub_rows
    size = 2 * TILE
    blocks = nodes // size
    features, counts = slice(width, 2 * width), 3 * width

    def here(block):
        return slice(block * size, (block + 1) * size)

    def loads(block):
        at = here(block)
        return [
            pltpu.make_async_copy(pack_hbm.at[at, : 2 * width], pack.at[at, : 2 * width], in_sem.at[0, block]),
            pltpu.make_async_copy(pack_hbm.at[at, 2 * width :], pack.at[at, counts:], in_sem.at[1, block]),
        ]

    coming = [loads(block) for block in range(blocks)]
    for group in coming:
        for copy in group:
            copy.start()
    table = jnp.concatenate(
        [table_ref[:, :slots, :].reshape(bounds, width), near_ref[...], far_ref[...]], axis=0
    )
    half_weights = jnp.concatenate([ws_ref[...], wn_ref[...]], axis=0) * jnp.bfloat16(0.5)
    half_bias = 0.5 * bias_ref[...]
    stores = []
    total = None
    turned = None
    for block in range(blocks + 2):
        following = None
        if block < blocks:
            for copy in coming[block]:
                copy.wait()
            following = sum_ref[here(block), :] + dot(pack[here(block), counts:], table)
        if block > 1:
            part = dot(turned, pack[here(block - 2), width:])
            terms[...] = part if block == 2 else terms[...] + part
        if 0 < block <= blocks:
            at = here(block - 1)
            pack[at, 2 * width : counts] = (total * scale).astype(bf16)
            arg = dot(pack[at, width:counts], half_weights) + half_bias
            tanh = jnp.tanh(arg)
            above = 1.0 + tanh
            act[at, :] = (arg * above).astype(bf16)
            slope = above * (0.5 + (0.5 * arg) * (1.0 - tanh))
            grad = (pack[at, :width].astype(f32) * slope).astype(bf16)
            grad_all[at, :] = grad
            turned = jnp.transpose(grad)
            for which, (source, target) in enumerate(((act, act_hbm), (grad_all, grad_hbm))):
                store = pltpu.make_async_copy(source.at[at, :], target.at[at, :], out_sem.at[which, block - 1])
                store.start()
                stores.append(store)
        total = following

    pieces = width // LANES
    step = 2 * width

    def term_rows(first, count, rows):
        return jnp.transpose(terms[:, first : first + count]).reshape(count // rows, rows, width)

    def lanes(piece):
        return slice(piece * LANES, (piece + 1) * LANES)

    first_core = core_ref[0] == 0
    weights = term_rows(0, step, hub_rows)
    own = jnp.where(first_core, weights[:, :half], weights[:, half:])
    other = jnp.where(first_core, weights[:, half:], weights[:, :half])
    count = step // hub_rows
    for low in range(0, parts, count):
        if low > 0:
            own = other = jnp.zeros_like(own)
        first = step + bounds + low * half
        keep = jnp.concatenate([term_rows(first, count * half, half), own], axis=1)
        give = jnp.concatenate([term_rows(first + hubs // 2, count * half, half), other], axis=1).astype(bf16)
        at = slice(low, low + count)
        for piece in range(pieces):
            there = slice(piece * hub_rows, (piece + 1) * hub_rows)
            keep_ref[at, there, :] = keep[:, :, lanes(piece)]
            give_ref[at, there, :] = give[:, :, lanes(piece)]
    bias_total = dot(jnp.ones((16, nodes), bf16), grad_all[...])[:1]
    rows = bias_rows([bias_total[:, lanes(piece)] for piece in range(pieces)])
    keep_ref[:, pieces * hub_rows :, :] = jnp.broadcast_to(rows[None], (parts, 8, LANES))
    give_ref[:, pieces * hub_rows :, :] = jnp.broadcast_to(rows.astype(bf16)[None], (parts, 8, LANES))
    for low in range(0, bounds, step):
        bound_terms = term_rows(step + low, step, slots).astype(bf16)
        for piece in range(pieces):
            bound_ref[low // slots : (low + step) // slots, piece * slots : (piece + 1) * slots, :] = (
                bound_terms[:, :, lanes(piece)]
            )
    for store in stores:
        store.wait()


def bias_rows(parts):
    line = lax.broadcasted_iota(jnp.int32, (8, LANES), 0)
    rows = jnp.zeros((8, LANES), f32)
    for piece, value in enumerate(parts):
        high = value.astype(bf16).astype(f32)
        rows = jnp.where(line == piece, high, rows)
        rows = jnp.where(line == len(parts) + piece, value - high, rows)
    return rows


def join_kernel(bound_ref, keep_ref, got_ref, out_ref):
    parts, tall, _ = keep_ref.shape
    place = bound_ref.shape[1]
    pieces = (tall - 8) // 16
    out_ref[:, :place, :] = bound_ref[...]
    both = keep_ref[:, : tall - 8, :] + got_ref[:, : tall - 8, :].astype(f32)
    out_ref[:, place : place + tall - 8, :] = both.astype(bf16)
    tail = keep_ref[0, tall - 8 :, :] + got_ref[0, tall - 8 :, :].astype(f32)
    rows = bias_rows([tail[piece : piece + 1] + tail[pieces + piece : pieces + piece + 1] for piece in range(pieces)])
    out_ref[:, place + tall - 8 :, :] = jnp.broadcast_to(rows.astype(bf16)[None], (parts, 8, LANES))


def chip_sums(slots, hub_rows, rows, back_ref):
    parts, tall, _ = back_ref.shape
    pieces = (tall - 8) // (slots + hub_rows)
    whole = back_ref[:, pieces * slots :, :].astype(f32)
    count = whole.shape[1]
    whole = whole.reshape(rows // 2, 2, parts // rows, count, LANES)
    return jnp.sum(jnp.sum(whole, axis=2), axis=0), pieces


def both_halves(total, pieces, hub_rows, first):
    half = hub_rows // 2
    columns = []
    for piece in range(pieces):
        place = piece * hub_rows + first
        columns.append(jnp.concatenate([total[0, place : place + half], total[1, place : place + half]], axis=0))
    return jnp.concatenate(columns, axis=1)


def weight_sum_kernel(slots, hub_rows, rows, back_ref, out_ref):
    total, pieces = chip_sums(slots, hub_rows, rows, back_ref)
    weight = both_halves(total, pieces, hub_rows, hub_rows // 2)
    out_ref[...] = by_core(weight.astype(bf16), rows, out_ref.shape[0] // rows)


def other_sums_kernel(scale, slots, hub_rows, rows, back_ref, wn_ref, bias_ref, hub_ref):
    total, pieces = chip_sums(slots, hub_rows, rows, back_ref)
    tail = 0.5 * (total[0, pieces * hub_rows :] + total[1, pieces * hub_rows :])
    bias_ref[...] = jnp.concatenate(
        [tail[piece : piece + 1] + tail[pieces + piece : pieces + piece + 1] for piece in range(pieces)], axis=1
    )
    hub = both_halves(total, pieces, hub_rows, 0)
    high = hub.astype(bf16)
    low = (hub - high.astype(f32)).astype(bf16)
    hub_ref[...] = (dot(high, wn_ref[...], NT) + dot(low, wn_ref[...], NT)) * scale


def weights_kernel(core_ref, near_ref, far_ref, self_ref, neigh_ref):
    width = self_ref.shape[0]
    count = 2 * width // 16
    near, far = near_ref[:count].astype(f32), far_ref[:count].astype(f32)
    first_core = core_ref[0] == 0
    whole = jnp.concatenate([jnp.where(first_core, near, far), jnp.where(first_core, far, near)], axis=1)
    whole = whole.reshape(2 * width, width)
    self_ref[...] = whole[:width]
    neigh_ref[...] = whole[width:]


def scatter_kernel(local_ref, grad_ref, out_ref):
    height = out_ref.shape[0]
    first = pl.program_id(0) * height
    total = None
    for start in range(0, grad_ref.shape[0], TILE):
        rows = index_rows(local_ref, start, TILE)
        part = dot(hits_by_column(rows, first, height), grad_ref[start : start + TILE, :])
        total = part if total is None else total + part
    out_ref[...] = total


def final_kernel(scale, slots, send_ref, back_ref, scat_ref, grad_ref, ws_ref, wn_ref, out_ref):
    height, width = out_ref.shape
    first = pl.program_id(0) * height
    count = send_ref.shape[1]
    returned = jnp.concatenate(
        [
            back_ref[:, piece * slots : (piece + 1) * slots, :].reshape(count, LANES)
            for piece in range(width // LANES)
        ],
        axis=1,
    )
    total = scat_ref[...]
    for start in range(0, count, 512):
        stop = min(count, start + 512)
        hits = hits_by_column([send_ref[:, start:stop]], first, height)
        total = total + dot(hits, returned[start:stop])
    out_ref[...] = dot(grad_ref[...], ws_ref[...], NT) + dot((total * scale).astype(bf16), wn_ref[...], NT)


def call(
    kernel, ins, in_specs, outs, out_specs, name, grid=(), scratch=(), flops=0, moved=0, limit=SOME_VMEM
):
    return pl.pallas_call(
        kernel,
        grid=grid,
        in_specs=in_specs,
        out_specs=out_specs,
        out_shape=outs,
        scratch_shapes=scratch,
        compiler_params=params(limit),
        cost_estimate=cost(flops, moved),
        name=name,
    )(*ins)


def whole_block(shape):
    return pl.BlockSpec(shape, lambda *_: (0,) * len(shape))


def body(
    features,
    hub_features,
    w_self,
    w_neigh,
    out_bias,
    local_edges,
    hub_edges,
    remote_edges,
    send_rows,
    cotangent,
):
    nodes, width = features.shape
    hub_rows = hub_features.shape[0]
    parts = lax.axis_size(AXES)
    slots = send_rows.shape[1] // parts
    slab = slots + hub_rows
    pieces = width // LANES
    pay = pieces * slab + 8
    core = (lax.axis_index("row") % 2).astype(jnp.int32).reshape(1)
    rows = lax.axis_size("row")
    half = hub_rows // 2
    table = parts * slab
    scale = 1.0 / (local_edges.shape[1] + hub_edges.shape[1] + remote_edges.shape[1])
    local_t, hub_t, remote_t = local_edges.T, hub_edges.T, remote_edges.T
    bias = out_bias.reshape(1, width)
    shape = jax.ShapeDtypeStruct

    def sibling(value):
        return lax.ppermute(value, "row", [(r, r ^ 1) for r in range(rows)])

    def exchange(value):
        return lax.all_to_all(value, AXES, split_axis=0, concat_axis=0, tiled=True)

    sending = call(
        functools.partial(pick_kernel, rows),
        (send_rows, features, hub_features),
        [VMEM, VMEM, VMEM],
        shape((parts, slots + half, width), bf16),
        whole_block((parts, slots + half, width)),
        "pick_rows",
        limit=MOST_VMEM,
        flops=2 * parts * slots * nodes * width,
        moved=nodes * width * 2,
    )
    sending, features = lax.optimization_barrier((sending, features))
    received = exchange(sending)

    block = TILE
    by_block = pl.BlockSpec((block, width), lambda i: (i, 0))
    packed = 2 * width + table
    local_sum, pack = call(
        functools.partial(local_kernel, parts * slots, hub_rows),
        (core, local_t, remote_t, hub_t, features, features, cotangent),
        [SMEM]
        + [pl.BlockSpec((edges.shape[0], block), lambda i: (0, i)) for edges in (local_t, remote_t, hub_t)]
        + [whole_block((nodes, width)), by_block, by_block],
        [shape((nodes, width), f32), pltpu.HBM((nodes, packed), bf16)],
        [by_block, pl.BlockSpec((block, packed), lambda i: (i, 0))],
        "local_gather",
        grid=(nodes // block,),
        flops=8 * nodes * nodes * width,
        moved=nodes * packed * 2,
    )

    received, local_sum, pack = lax.optimization_barrier((received, local_sum, pack))
    near_hubs = call(
        functools.partial(half_kernel, slots),
        [received],
        [VMEM],
        shape((parts * half, width), bf16),
        VMEM,
        "take_hubs",
        moved=parts * half * width * 4,
    )
    far_hubs = sibling(near_hubs)

    activated, grad_pre, bound_terms, keep, give = call(
        functools.partial(middle_kernel, scale, slots),
        [core, received, near_hubs, far_hubs, w_self, w_neigh, bias, local_sum, pack],
        [SMEM] + [VMEM] * 7 + [HBM],
        [pltpu.HBM((nodes, width), bf16)] * 2
        + [
            shape((parts, pieces * slots, LANES), bf16),
            shape((parts, pieces * hub_rows + 8, LANES), f32),
            shape((parts, pieces * hub_rows + 8, LANES), bf16),
        ],
        [HBM] * 2 + [VMEM] * 3,
        "activate",
        limit=MUCH_VMEM,
        scratch=[
            pltpu.VMEM((nodes, packed + width), bf16),
            pltpu.VMEM((nodes, width), bf16),
            pltpu.VMEM((nodes, width), bf16),
            pltpu.VMEM((width, 2 * width + table), f32),
            pltpu.SemaphoreType.DMA((2, nodes // (2 * TILE))),
            pltpu.SemaphoreType.DMA((2, nodes // (2 * TILE))),
        ],
        flops=4 * nodes * table * width,
        moved=nodes * packed * 2,
    )
    got = sibling(give)
    back = exchange(
        call(
            join_kernel,
            [bound_terms, keep, got],
            [VMEM] * 3,
            shape((parts, pay, LANES), bf16),
            VMEM,
            "join_siblings",
            moved=parts * pay * LANES * 6,
        )
    )

    scattered = call(
        scatter_kernel,
        (local_t, grad_pre),
        [whole_block(local_t.shape), whole_block((nodes, width))],
        shape((nodes, width), f32),
        pl.BlockSpec((block, width), lambda i: (i, 0)),
        "local_scatter",
        grid=(nodes // block,),
        flops=8 * nodes * nodes * width,
        moved=nodes * width * 6,
    )
    back, scattered = lax.optimization_barrier((back, scattered))
    weight_rows = call(
        functools.partial(weight_sum_kernel, slots, hub_rows, rows),
        (back,),
        [VMEM],
        shape((parts, 8, width), bf16),
        VMEM,
        "weight_sums",
        moved=parts * pay * width * 2,
    )
    near_weights = exchange(weight_rows)
    grad_bias, grad_hubs = call(
        functools.partial(other_sums_kernel, scale, slots, hub_rows, rows),
        (back, w_neigh),
        [VMEM, VMEM],
        [shape((1, width), f32), shape((hub_rows, width), f32)],
        [whole_block((1, width)), whole_block((hub_rows, width))],
        "hub_sums",
        moved=parts * pay * width * 2,
    )

    height = 2 * TILE
    by_height = pl.BlockSpec((height, width), lambda i: (i, 0))
    grad_features = call(
        functools.partial(final_kernel, scale, slots),
        (send_rows, back, scattered, grad_pre, w_self, w_neigh),
        [whole_block(send_rows.shape), whole_block((parts, pay, LANES)), by_height, by_height]
        + [whole_block((width, width))] * 2,
        shape((nodes, width), f32),
        by_height,
        "return_scatter",
        grid=(nodes // height,),
        flops=2 * nodes * parts * slots * width,
        moved=nodes * width * 10,
    )
    near_weights, grad_features = lax.optimization_barrier((near_weights, grad_features))
    grad_w_self, grad_w_neigh = call(
        weights_kernel,
        [core, near_weights, sibling(near_weights)],
        [SMEM, VMEM, VMEM],
        [shape((width, width), f32)] * 2,
        [whole_block((width, width))] * 2,
        "weights",
        moved=width * width * 12,
    )
    return (activated, grad_features, grad_hubs, grad_w_self, grad_w_neigh, grad_bias.reshape(width))


def solution(mesh):
    split = P(AXES, None)
    return jax.shard_map(
        body,
        mesh=mesh,
        in_specs=(split, split, P(), P(), P(), split, split, split, split, split),
        out_specs=(split, split, split, P(), P(), P()),
        check_vma=False,
    )
```

```python
import functools

import jax
import jax.numpy as jnp
from jax import lax
from jax.experimental import pallas as pl
from jax.experimental.pallas import tpu as pltpu
from jax.sharding import PartitionSpec as P

AXES = ("row", "col")
LANES = 128
TILE = 256
MOST_VMEM = 61952 * 1024
SOME_VMEM = 44 * 1024 * 1024
MUCH_VMEM = 47 * 1024 * 1024
NT = (((1,), (1,)), ((), ()))
TN = (((0,), (0,)), ((), ()))
VMEM = pl.BlockSpec(memory_space=pltpu.VMEM)
SMEM = pl.BlockSpec(memory_space=pltpu.SMEM)
HBM = pl.BlockSpec(memory_space=pltpu.HBM)
bf16, f32 = jnp.bfloat16, jnp.float32


def params(limit):
    return pltpu.CompilerParams(vmem_limit_bytes=limit)


def cost(flops, moved):
    return pl.CostEstimate(flops=int(flops), bytes_accessed=int(moved), transcendentals=0)


def along_rows(index_row):
    count = index_row.shape[1]
    return jnp.transpose(jnp.broadcast_to(index_row, (LANES, count))).astype(jnp.int16)


def stack_rows(value, height):
    count = value.shape[1]
    return jnp.broadcast_to(value[None], (height // 16, 16, count)).reshape(height, count)


def count_hits(entries, here):
    one, zero = jnp.ones(here.shape, bf16), jnp.zeros(here.shape, bf16)
    total = None
    for entry in entries:
        hit = jnp.where(entry == here, one, zero)
        total = hit if total is None else total + hit
    return total


def hits_by_row(columns, first, width):
    rows = columns[0].shape[0]
    lane = lax.broadcasted_iota(jnp.int32, (16, LANES), 1).astype(jnp.int16)
    tiles = [
        count_hits(columns, stack_rows(lane + jnp.int16(start), rows)) for start in range(first, first + width, LANES)
    ]
    return jnp.concatenate(tiles, axis=1) if len(tiles) > 1 else tiles[0]


def hits_by_column(index_rows, first, height):
    count = index_rows[0].shape[1]
    group = 64
    down = lax.broadcasted_iota(jnp.int32, (group, count), 0).astype(jnp.int16)
    entries = [
        stack_rows(jnp.broadcast_to(row - first, (16, count)).astype(jnp.int16), group) for row in index_rows
    ]
    return jnp.concatenate(
        [count_hits(entries, down + jnp.int16(start)) for start in range(0, height, group)], axis=0
    )


def dot(a, b, dims=(((1,), (0,)), ((), ()))):
    return lax.dot_general(a, b, dims, preferred_element_type=f32)


def index_rows(ref, start, count):
    return [ref[j : j + 1, pl.ds(start, count)] for j in range(ref.shape[0])]


def by_core(value, rows, cols):
    half = value.shape[0] // 2
    value = value.astype(f32)
    halves = [value[core * half : (core + 1) * half] for core in (0, 1)]
    blocks = [jnp.broadcast_to(halves[row % 2][None], (cols,) + halves[0].shape) for row in range(rows)]
    return jnp.concatenate(blocks, axis=0).astype(bf16)


def pick_kernel(rows, send_ref, feat_ref, hub_ref, out_ref):
    parts, slab, width = out_ref.shape
    slots = slab - hub_ref.shape[0] // 2
    total = send_ref.shape[1]
    step = min(512, total)
    for start in range(0, total, step):
        column = along_rows(send_ref[:, start : start + step])
        picked = dot(hits_by_row([column], 0, feat_ref.shape[0]), feat_ref[...])
        out_ref[start // slots : (start + step) // slots, :slots, :] = (
            picked.astype(bf16).reshape(step // slots, slots, width)
        )
    out_ref[:, slots:, :] = by_core(hub_ref[...], rows, parts // rows)


def half_kernel(slots, table_ref, out_ref):
    out_ref[...] = table_ref[:, slots:, :].astype(f32).reshape(out_ref.shape).astype(bf16)


def local_kernel(split, hub_rows, core_ref, local_ref, remote_ref, hub_ref, feat_ref, own_ref, cot_ref, sum_ref, pack_ref):
    nodes, width = feat_ref.shape
    columns = [along_rows(row) for row in index_rows(local_ref, 0, TILE)]
    total = None
    for first in range(0, nodes, TILE):
        part = dot(hits_by_row(columns, first, TILE), feat_ref[first : first + TILE, :])
        total = part if total is None else total + part
    sum_ref[...] = total
    pack_ref[:, :width] = cot_ref[...]
    pack_ref[:, width : 2 * width] = own_ref[...]
    place = 2 * width
    counts = pack_ref.shape[1] - place
    half = hub_rows // 2
    hubs = []
    for hub in index_rows(hub_ref, 0, TILE):
        owner = lax.div(hub, jnp.int32(hub_rows))
        within = hub - owner * hub_rows
        other = (within >= half) != (core_ref[0] == 1)
        within = jnp.where(within >= half, within - half, within)
        hubs.append(owner * half + within + jnp.where(other, (counts - split) // 2, 0))
    for index, share in ((index_rows(remote_ref, 0, TILE), split), (hubs, counts - split)):
        columns = [along_rows(row) for row in index]
        for first in range(0, share, TILE):
            pack_ref[:, place + first : place + first + TILE] = hits_by_row(columns, first, TILE)
        place += share


def middle_kernel(
    scale,
    slots,
    core_ref,
    table_ref,
    near_ref,
    far_ref,
    ws_ref,
    wn_ref,
    bias_ref,
    sum_ref,
    pack_hbm,
    act_hbm,
    grad_hbm,
    bound_ref,
    keep_ref,
    give_ref,
    pack,
    act,
    grad_all,
    terms,
    in_sem,
    out_sem,
):
    nodes, width = sum_ref.shape
    parts, slab, _ = table_ref.shape
    half = slab - slots
    hub_rows = 2 * half
    bounds, hubs = parts * slots, parts * hub_rows
    size = 2 * TILE
    blocks = nodes // size
    features, counts = slice(width, 2 * width), 3 * width

    def here(block):
        return slice(block * size, (block + 1) * size)

    def loads(block):
        at = here(block)
        return [
            pltpu.make_async_copy(pack_hbm.at[at, : 2 * width], pack.at[at, : 2 * width], in_sem.at[0, block]),
            pltpu.make_async_copy(pack_hbm.at[at, 2 * width :], pack.at[at, counts:], in_sem.at[1, block]),
        ]

    coming = [loads(block) for block in range(blocks)]
    for group in coming:
        for copy in group:
            copy.start()
    table = jnp.concatenate(
        [table_ref[:, :slots, :].reshape(bounds, width), near_ref[...], far_ref[...]], axis=0
    )
    half_weights = jnp.concatenate([ws_ref[...], wn_ref[...]], axis=0) * jnp.bfloat16(0.5)
    half_bias = 0.5 * bias_ref[...]
    stores = []
    total = None
    turned = None
    for block in range(blocks + 2):
        following = None
        if block < blocks:
            for copy in coming[block]:
                copy.wait()
            following = sum_ref[here(block), :] + dot(pack[here(block), counts:], table)
        if block > 1:
            part = dot(turned, pack[here(block - 2), width:])
            terms[...] = part if block == 2 else terms[...] + part
        if 0 < block <= blocks:
            at = here(block - 1)
            pack[at, 2 * width : counts] = (total * scale).astype(bf16)
            arg = dot(pack[at, width:counts], half_weights) + half_bias
            tanh = jnp.tanh(arg)
            above = 1.0 + tanh
            act[at, :] = (arg * above).astype(bf16)
            slope = above * (0.5 + (0.5 * arg) * (1.0 - tanh))
            grad = (pack[at, :width].astype(f32) * slope).astype(bf16)
            grad_all[at, :] = grad
            turned = jnp.transpose(grad)
            for which, (source, target) in enumerate(((act, act_hbm), (grad_all, grad_hbm))):
                store = pltpu.make_async_copy(source.at[at, :], target.at[at, :], out_sem.at[which, block - 1])
                store.start()
                stores.append(store)
        total = following

    pieces = width // LANES
    step = 2 * width

    def term_rows(first, count, rows):
        return jnp.transpose(terms[:, first : first + count]).reshape(count // rows, rows, width)

    def lanes(piece):
        return slice(piece * LANES, (piece + 1) * LANES)

    first_core = core_ref[0] == 0
    weights = term_rows(0, step, hub_rows)
    own = jnp.where(first_core, weights[:, :half], weights[:, half:])
    other = jnp.where(first_core, weights[:, half:], weights[:, :half])
    count = step // hub_rows
    tall = pieces * hub_rows

    def flat(value):
        return jnp.concatenate([value[:, :, lanes(piece)] for piece in range(pieces)], axis=1).reshape(-1, LANES)

    for low in range(0, parts, count):
        if low > 0:
            own = other = jnp.zeros_like(own)
        first = step + bounds + low * half
        keep = jnp.concatenate([term_rows(first, count * half, half), own], axis=1)
        give = jnp.concatenate([term_rows(first + hubs // 2, count * half, half), other], axis=1)
        keep_ref[low * tall : (low + count) * tall, :] = flat(keep)
        give_ref[low * tall : (low + count) * tall, :] = flat(give).astype(bf16)
    bias_total = dot(jnp.ones((16, nodes), bf16), grad_all[...])[:1]
    rows = bias_rows([bias_total[:, lanes(piece)] for piece in range(pieces)])
    keep_ref[parts * tall :, :] = rows
    give_ref[parts * tall :, :] = rows.astype(bf16)
    for low in range(0, bounds, step):
        bound_ref[low // slots : (low + step) // slots] = term_rows(step + low, step, slots).astype(bf16)
    for store in stores:
        store.wait()


def bias_rows(parts):
    line = lax.broadcasted_iota(jnp.int32, (16, LANES), 0)
    rows = jnp.zeros((16, LANES), f32)
    for piece, value in enumerate(parts):
        high = value.astype(bf16).astype(f32)
        rows = jnp.where(line == piece, high, rows)
        rows = jnp.where(line == len(parts) + piece, value - high, rows)
    return rows


def bias_pieces(tail, pieces):
    return [tail[piece : piece + 1] + tail[pieces + piece : pieces + piece + 1] for piece in range(pieces)]


def halve_kernel(before, tall, pieces, bit_ref, keep_ref, got_ref, keep_out, give_out):
    both = keep_ref[...] + got_ref[...].astype(f32)
    count = both.shape[0] - 16
    body = both[:count].reshape(before, 2, count // (2 * before * tall) * tall, LANES)
    low_side = bit_ref[0] == 0
    mine = jnp.where(low_side, body[:, 0], body[:, 1]).reshape(count // 2, LANES)
    other = jnp.where(low_side, body[:, 1], body[:, 0]).reshape(count // 2, LANES)
    rows = bias_rows(bias_pieces(both[count:], pieces))
    keep_out[: count // 2, :] = mine
    keep_out[count // 2 :, :] = rows
    give_out[: count // 2, :] = other.astype(bf16)
    give_out[count // 2 :, :] = rows.astype(bf16)


def last_kernel(rows, hub_rows, pieces, core_ref, keep_ref, got_ref, weight_ref, keep_out, give_out, bias_ref):
    half = hub_rows // 2
    both = keep_ref[...] + got_ref[...].astype(f32)
    count = both.shape[0] - 16
    body = both[:count].reshape(2, pieces * hub_rows, LANES)

    def table(core, first):
        return jnp.concatenate(
            [body[core, piece * hub_rows + first : piece * hub_rows + first + half] for piece in range(pieces)], axis=1
        )

    weight = jnp.concatenate([table(0, half), table(1, half)], axis=0)
    weight_ref[...] = by_core(weight.astype(bf16), rows, weight_ref.shape[0] // rows)
    first_core = core_ref[0] == 0
    keep_out[...] = jnp.where(first_core, table(0, 0), table(1, 0))
    give_out[...] = jnp.where(first_core, table(1, 0), table(0, 0))
    bias_ref[...] = jnp.concatenate(bias_pieces(both[count:], pieces), axis=1)


def hub_kernel(scale, core_ref, keep_ref, got_ref, wn_ref, hub_ref):
    first_core = core_ref[0] == 0
    keep, got = keep_ref[...], got_ref[...]
    hub = jnp.concatenate([jnp.where(first_core, keep, got), jnp.where(first_core, got, keep)], axis=0)
    high = hub.astype(bf16)
    low = (hub - high.astype(f32)).astype(bf16)
    hub_ref[...] = (dot(high, wn_ref[...], NT) + dot(low, wn_ref[...], NT)) * scale


def weights_kernel(rows, core_ref, near_ref, far_ref, self_ref, neigh_ref):
    width = self_ref.shape[0]
    parts = near_ref.shape[0]
    cols = parts // rows
    near, far = near_ref[...].astype(f32), far_ref[...].astype(f32)
    first_core = core_ref[0] == 0
    holders = (jnp.where(first_core, near, far), jnp.where(first_core, far, near))
    blocks = []
    for row in range(rows):
        held, pair = holders[row % 2], row // 2 * 2 * cols
        blocks.append(jnp.concatenate([held[pair : pair + cols], held[pair + cols : pair + 2 * cols]], axis=1))
    whole = jnp.concatenate(blocks, axis=0)[: 2 * width // 16].reshape(2 * width, width)
    self_ref[...] = whole[:width]
    neigh_ref[...] = whole[width:]


def scatter_kernel(local_ref, grad_ref, out_ref):
    height = out_ref.shape[0]
    first = pl.program_id(0) * height
    total = None
    for start in range(0, grad_ref.shape[0], TILE):
        rows = index_rows(local_ref, start, TILE)
        part = dot(hits_by_column(rows, first, height), grad_ref[start : start + TILE, :])
        total = part if total is None else total + part
    out_ref[...] = total


def final_kernel(scale, slots, send_ref, back_ref, scat_ref, grad_ref, ws_ref, wn_ref, out_ref):
    height, width = out_ref.shape
    first = pl.program_id(0) * height
    count = send_ref.shape[1]
    returned = back_ref[...].reshape(count, width)
    total = scat_ref[...]
    for start in range(0, count, 512):
        stop = min(count, start + 512)
        hits = hits_by_column([send_ref[:, start:stop]], first, height)
        total = total + dot(hits, returned[start:stop])
    out_ref[...] = dot(grad_ref[...], ws_ref[...], NT) + dot((total * scale).astype(bf16), wn_ref[...], NT)


def call(
    kernel, ins, in_specs, outs, out_specs, name, grid=(), scratch=(), flops=0, moved=0, limit=SOME_VMEM
):
    return pl.pallas_call(
        kernel,
        grid=grid,
        in_specs=in_specs,
        out_specs=out_specs,
        out_shape=outs,
        scratch_shapes=scratch,
        compiler_params=params(limit),
        cost_estimate=cost(flops, moved),
        name=name,
    )(*ins)


def powers(low, high):
    found = []
    while low < high:
        found.append(low)
        low *= 2
    return found


def whole_block(shape):
    return pl.BlockSpec(shape, lambda *_: (0,) * len(shape))


def body(
    features,
    hub_features,
    w_self,
    w_neigh,
    out_bias,
    local_edges,
    hub_edges,
    remote_edges,
    send_rows,
    cotangent,
):
    nodes, width = features.shape
    hub_rows = hub_features.shape[0]
    parts = lax.axis_size(AXES)
    slots = send_rows.shape[1] // parts
    slab = slots + hub_rows
    pieces = width // LANES
    tall = pieces * hub_rows
    core = (lax.axis_index("row") % 2).astype(jnp.int32).reshape(1)
    rows = lax.axis_size("row")
    half = hub_rows // 2
    table = parts * slab
    scale = 1.0 / (local_edges.shape[1] + hub_edges.shape[1] + remote_edges.shape[1])
    local_t, hub_t, remote_t = local_edges.T, hub_edges.T, remote_edges.T
    bias = out_bias.reshape(1, width)
    shape = jax.ShapeDtypeStruct

    def sibling(value):
        return lax.ppermute(value, "row", [(r, r ^ 1) for r in range(rows)])

    def exchange(value):
        return lax.all_to_all(value, AXES, split_axis=0, concat_axis=0, tiled=True)

    sending = call(
        functools.partial(pick_kernel, rows),
        (send_rows, features, hub_features),
        [VMEM, VMEM, VMEM],
        shape((parts, slots + half, width), bf16),
        whole_block((parts, slots + half, width)),
        "pick_rows",
        limit=MOST_VMEM,
        flops=2 * parts * slots * nodes * width,
        moved=nodes * width * 2,
    )
    sending, features = lax.optimization_barrier((sending, features))
    received = exchange(sending)

    block = TILE
    by_block = pl.BlockSpec((block, width), lambda i: (i, 0))
    packed = 2 * width + table
    local_sum, pack = call(
        functools.partial(local_kernel, parts * slots, hub_rows),
        (core, local_t, remote_t, hub_t, features, features, cotangent),
        [SMEM]
        + [pl.BlockSpec((edges.shape[0], block), lambda i: (0, i)) for edges in (local_t, remote_t, hub_t)]
        + [whole_block((nodes, width)), by_block, by_block],
        [shape((nodes, width), f32), pltpu.HBM((nodes, packed), bf16)],
        [by_block, pl.BlockSpec((block, packed), lambda i: (i, 0))],
        "local_gather",
        grid=(nodes // block,),
        flops=8 * nodes * nodes * width,
        moved=nodes * packed * 2,
    )

    received, local_sum, pack = lax.optimization_barrier((received, local_sum, pack))
    near_hubs = call(
        functools.partial(half_kernel, slots),
        [received],
        [VMEM],
        shape((parts * half, width), bf16),
        VMEM,
        "take_hubs",
        moved=parts * half * width * 4,
    )
    far_hubs = sibling(near_hubs)

    activated, grad_pre, bound_terms, keep, give = call(
        functools.partial(middle_kernel, scale, slots),
        [core, received, near_hubs, far_hubs, w_self, w_neigh, bias, local_sum, pack],
        [SMEM] + [VMEM] * 7 + [HBM],
        [pltpu.HBM((nodes, width), bf16)] * 2
        + [
            shape((parts, slots, width), bf16),
            shape((parts * tall + 16, LANES), f32),
            shape((parts * tall + 16, LANES), bf16),
        ],
        [HBM] * 2 + [VMEM] * 3,
        "activate",
        limit=MUCH_VMEM,
        scratch=[
            pltpu.VMEM((nodes, packed + width), bf16),
            pltpu.VMEM((nodes, width), bf16),
            pltpu.VMEM((nodes, width), bf16),
            pltpu.VMEM((width, 2 * width + table), f32),
            pltpu.SemaphoreType.DMA((2, nodes // (2 * TILE))),
            pltpu.SemaphoreType.DMA((2, nodes // (2 * TILE))),
        ],
        flops=4 * nodes * table * width,
        moved=nodes * packed * 2,
    )
    got = sibling(give)
    back = exchange(bound_terms)

    scattered = call(
        scatter_kernel,
        (local_t, grad_pre),
        [whole_block(local_t.shape), whole_block((nodes, width))],
        shape((nodes, width), f32),
        pl.BlockSpec((block, width), lambda i: (i, 0)),
        "local_scatter",
        grid=(nodes // block,),
        flops=8 * nodes * nodes * width,
        moved=nodes * width * 6,
    )
    cols = parts // rows
    bits = [("row", bit) for bit in powers(2, rows)[::-1]] + [("col", bit) for bit in powers(1, cols)]
    count = parts
    for stage, (axis, bit) in enumerate(bits):
        before = 1 if axis == "row" else 2 * (cols // (2 * bit))
        side = (lax.axis_index(axis) // bit % 2).astype(jnp.int32).reshape(1)
        count //= 2
        keep, give = call(
            functools.partial(halve_kernel, before, tall, pieces),
            [side, keep, got],
            [SMEM, VMEM, VMEM],
            [shape((count * tall + 16, LANES), f32), shape((count * tall + 16, LANES), bf16)],
            [VMEM, VMEM],
            "halve",
            moved=count * tall * LANES * 8,
        )
        got = lax.ppermute(give, axis, [(i, i ^ bit) for i in range(lax.axis_size(axis))])
        if stage == 0:
            got, scattered = lax.optimization_barrier((got, scattered))
    weight_rows, hub_keep, hub_give, grad_bias = call(
        functools.partial(last_kernel, rows, hub_rows, pieces),
        [core, keep, got],
        [SMEM, VMEM, VMEM],
        [
            shape((parts, 8, width), bf16),
            shape((half, width), f32),
            shape((half, width), f32),
            shape((1, width), f32),
        ],
        [VMEM] * 4,
        "weight_sums",
        moved=parts * 8 * width * 2,
    )
    near_weights = exchange(weight_rows)
    grad_hubs = call(
        functools.partial(hub_kernel, scale),
        [core, hub_keep, sibling(hub_give), w_neigh],
        [SMEM, VMEM, VMEM, VMEM],
        shape((hub_rows, width), f32),
        VMEM,
        "hub_sums",
        moved=width * width * 2,
    )

    height = 2 * TILE
    by_height = pl.BlockSpec((height, width), lambda i: (i, 0))
    grad_features = call(
        functools.partial(final_kernel, scale, slots),
        (send_rows, back, scattered, grad_pre, w_self, w_neigh),
        [whole_block(send_rows.shape), whole_block((parts, slots, width)), by_height, by_height]
        + [whole_block((width, width))] * 2,
        shape((nodes, width), f32),
        by_height,
        "return_scatter",
        grid=(nodes // height,),
        flops=2 * nodes * parts * slots * width,
        moved=nodes * width * 10,
    )
    near_weights, grad_features = lax.optimization_barrier((near_weights, grad_features))
    grad_w_self, grad_w_neigh = call(
        functools.partial(weights_kernel, rows),
        [core, near_weights, sibling(near_weights)],
        [SMEM, VMEM, VMEM],
        [shape((width, width), f32)] * 2,
        [whole_block((width, width))] * 2,
        "weights",
        moved=width * width * 12,
    )
    return (activated, grad_features, grad_hubs, grad_w_self, grad_w_neigh, grad_bias.reshape(width))


def solution(mesh):
    split = P(AXES, None)
    return jax.shard_map(
        body,
        mesh=mesh,
        in_specs=(split, split, P(), P(), P(), split, split, split, split, split),
        out_specs=(split, split, split, P(), P(), P()),
        check_vma=False,
    )
```

```python
import functools

import jax
import jax.numpy as jnp
from jax import lax
from jax.experimental import pallas as pl
from jax.experimental.pallas import tpu as pltpu
from jax.sharding import PartitionSpec as P

AXES = ("row", "col")
LANES = 128
TILE = 256
MOST_VMEM = 61952 * 1024
SOME_VMEM = 44 * 1024 * 1024
MUCH_VMEM = 47 * 1024 * 1024
NT = (((1,), (1,)), ((), ()))
TN = (((0,), (0,)), ((), ()))
VMEM = pl.BlockSpec(memory_space=pltpu.VMEM)
SMEM = pl.BlockSpec(memory_space=pltpu.SMEM)
HBM = pl.BlockSpec(memory_space=pltpu.HBM)
bf16, f32 = jnp.bfloat16, jnp.float32


def params(limit):
    return pltpu.CompilerParams(vmem_limit_bytes=limit)


def cost(flops, moved):
    return pl.CostEstimate(flops=int(flops), bytes_accessed=int(moved), transcendentals=0)


def along_rows(index_row):
    count = index_row.shape[1]
    return jnp.transpose(jnp.broadcast_to(index_row, (LANES, count))).astype(jnp.int16)


def stack_rows(value, height):
    count = value.shape[1]
    return jnp.broadcast_to(value[None], (height // 16, 16, count)).reshape(height, count)


def count_hits(entries, here):
    one, zero = jnp.ones(here.shape, bf16), jnp.zeros(here.shape, bf16)
    total = None
    for entry in entries:
        hit = jnp.where(entry == here, one, zero)
        total = hit if total is None else total + hit
    return total


def hits_by_row(columns, first, width):
    rows = columns[0].shape[0]
    lane = lax.broadcasted_iota(jnp.int32, (16, LANES), 1).astype(jnp.int16)
    tiles = [
        count_hits(columns, stack_rows(lane + jnp.int16(start), rows)) for start in range(first, first + width, LANES)
    ]
    return jnp.concatenate(tiles, axis=1) if len(tiles) > 1 else tiles[0]


def hits_by_column(index_rows, first, height):
    count = index_rows[0].shape[1]
    group = 64
    down = lax.broadcasted_iota(jnp.int32, (group, count), 0).astype(jnp.int16)
    entries = [
        stack_rows(jnp.broadcast_to(row - first, (16, count)).astype(jnp.int16), group) for row in index_rows
    ]
    return jnp.concatenate(
        [count_hits(entries, down + jnp.int16(start)) for start in range(0, height, group)], axis=0
    )


def dot(a, b, dims=(((1,), (0,)), ((), ()))):
    return lax.dot_general(a, b, dims, preferred_element_type=f32)


def index_rows(ref, start, count):
    return [ref[j : j + 1, pl.ds(start, count)] for j in range(ref.shape[0])]


def by_core(value, rows, cols):
    half = value.shape[0] // 2
    value = value.astype(f32)
    halves = [value[core * half : (core + 1) * half] for core in (0, 1)]
    blocks = [jnp.broadcast_to(halves[row % 2][None], (cols,) + halves[0].shape) for row in range(rows)]
    return jnp.concatenate(blocks, axis=0).astype(bf16)


def pick_kernel(rows, send_ref, feat_ref, hub_ref, out_ref):
    parts, slab, width = out_ref.shape
    slots = slab - hub_ref.shape[0] // 2
    total = send_ref.shape[1]
    step = min(512, total)
    for start in range(0, total, step):
        column = along_rows(send_ref[:, start : start + step])
        picked = dot(hits_by_row([column], 0, feat_ref.shape[0]), feat_ref[...])
        out_ref[start // slots : (start + step) // slots, :slots, :] = (
            picked.astype(bf16).reshape(step // slots, slots, width)
        )
    out_ref[:, slots:, :] = by_core(hub_ref[...], rows, parts // rows)


def half_kernel(slots, table_ref, out_ref):
    out_ref[...] = table_ref[:, slots:, :].astype(f32).reshape(out_ref.shape).astype(bf16)


def local_kernel(split, hub_rows, core_ref, local_ref, remote_ref, hub_ref, feat_ref, own_ref, cot_ref, sum_ref, pack_ref):
    nodes, width = feat_ref.shape
    columns = [along_rows(row) for row in index_rows(local_ref, 0, TILE)]
    total = None
    for first in range(0, nodes, TILE):
        part = dot(hits_by_row(columns, first, TILE), feat_ref[first : first + TILE, :])
        total = part if total is None else total + part
    sum_ref[...] = total
    pack_ref[:, :width] = cot_ref[...]
    pack_ref[:, width : 2 * width] = own_ref[...]
    place = 2 * width
    counts = pack_ref.shape[1] - place
    half = hub_rows // 2
    hubs = []
    for hub in index_rows(hub_ref, 0, TILE):
        owner = lax.div(hub, jnp.int32(hub_rows))
        within = hub - owner * hub_rows
        other = (within >= half) != (core_ref[0] == 1)
        within = jnp.where(within >= half, within - half, within)
        hubs.append(owner * half + within + jnp.where(other, (counts - split) // 2, 0))
    for index, share in ((index_rows(remote_ref, 0, TILE), split), (hubs, counts - split)):
        columns = [along_rows(row) for row in index]
        for first in range(0, share, TILE):
            pack_ref[:, place + first : place + first + TILE] = hits_by_row(columns, first, TILE)
        place += share


def middle_kernel(
    scale,
    slots,
    core_ref,
    table_ref,
    near_ref,
    far_ref,
    ws_ref,
    wn_ref,
    bias_ref,
    sum_ref,
    pack_hbm,
    act_hbm,
    grad_hbm,
    bound_ref,
    keep_ref,
    give_ref,
    pack,
    act,
    grad_all,
    terms,
    in_sem,
    out_sem,
):
    nodes, width = sum_ref.shape
    parts, slab, _ = table_ref.shape
    half = slab - slots
    hub_rows = 2 * half
    bounds, hubs = parts * slots, parts * hub_rows
    size = TILE
    blocks = nodes // size
    features, counts = slice(width, 2 * width), 3 * width

    def here(block):
        return slice(block * size, (block + 1) * size)

    def loads(block):
        at = here(block)
        return [
            pltpu.make_async_copy(pack_hbm.at[at, 2 * width :], pack.at[at, counts:], in_sem.at[1, block]),
            pltpu.make_async_copy(pack_hbm.at[at, : 2 * width], pack.at[at, : 2 * width], in_sem.at[0, block]),
        ]

    coming = [loads(block) for block in range(blocks)]
    for group in coming:
        for copy in group:
            copy.start()
    table = jnp.concatenate(
        [table_ref[:, :slots, :].reshape(bounds, width), near_ref[...], far_ref[...]], axis=0
    )
    half_weights = jnp.concatenate([ws_ref[...], wn_ref[...]], axis=0) * jnp.bfloat16(0.5)
    half_bias = 0.5 * bias_ref[...]
    stores = []
    total = None
    turned = None
    for block in range(blocks + 2):
        following = None
        if block < blocks:
            for copy in coming[block]:
                copy.wait()
            following = sum_ref[here(block), :] + dot(pack[here(block), counts:], table)
        if block > 1:
            part = dot(turned, pack[here(block - 2), width:])
            terms[...] = part if block == 2 else terms[...] + part
        if 0 < block <= blocks:
            at = here(block - 1)
            pack[at, 2 * width : counts] = (total * scale).astype(bf16)
            arg = dot(pack[at, width:counts], half_weights) + half_bias
            tanh = jnp.tanh(arg)
            above = 1.0 + tanh
            act[at, :] = (arg * above).astype(bf16)
            slope = above * (0.5 + (0.5 * arg) * (1.0 - tanh))
            grad = (pack[at, :width].astype(f32) * slope).astype(bf16)
            grad_all[at, :] = grad
            turned = jnp.transpose(grad)
            for which, (source, target) in enumerate(((act, act_hbm), (grad_all, grad_hbm))):
                store = pltpu.make_async_copy(source.at[at, :], target.at[at, :], out_sem.at[which, block - 1])
                store.start()
                stores.append(store)
        total = following

    pieces = width // LANES
    step = 2 * width

    def term_rows(first, count, rows):
        return jnp.transpose(terms[:, first : first + count]).reshape(count // rows, rows, width)

    def lanes(piece):
        return slice(piece * LANES, (piece + 1) * LANES)

    first_core = core_ref[0] == 0
    weights = term_rows(0, step, hub_rows)
    own = jnp.where(first_core, weights[:, :half], weights[:, half:])
    other = jnp.where(first_core, weights[:, half:], weights[:, :half])
    count = step // hub_rows
    for low in range(0, parts, count):
        if low > 0:
            own = other = jnp.zeros_like(own)
        first = step + bounds + low * half
        keep = jnp.concatenate([term_rows(first, count * half, half), own], axis=1)
        give = jnp.concatenate([term_rows(first + hubs // 2, count * half, half), other], axis=1).astype(bf16)
        at = slice(low, low + count)
        for piece in range(pieces):
            there = slice(piece * hub_rows, (piece + 1) * hub_rows)
            keep_ref[at, there, :] = keep[:, :, lanes(piece)]
            give_ref[at, there, :] = give[:, :, lanes(piece)]
    bias_total = dot(jnp.ones((16, nodes), bf16), grad_all[...])[:1]
    rows = bias_rows([bias_total[:, lanes(piece)] for piece in range(pieces)])
    keep_ref[:, pieces * hub_rows :, :] = jnp.broadcast_to(rows[None], (parts, 8, LANES))
    give_ref[:, pieces * hub_rows :, :] = jnp.broadcast_to(rows.astype(bf16)[None], (parts, 8, LANES))
    for low in range(0, bounds, step):
        bound_terms = term_rows(step + low, step, slots).astype(bf16)
        for piece in range(pieces):
            bound_ref[low // slots : (low + step) // slots, piece * slots : (piece + 1) * slots, :] = (
                bound_terms[:, :, lanes(piece)]
            )
    for store in stores:
        store.wait()


def bias_rows(parts):
    line = lax.broadcasted_iota(jnp.int32, (8, LANES), 0)
    rows = jnp.zeros((8, LANES), f32)
    for piece, value in enumerate(parts):
        high = value.astype(bf16).astype(f32)
        rows = jnp.where(line == piece, high, rows)
        rows = jnp.where(line == len(parts) + piece, value - high, rows)
    return rows


def join_kernel(bound_ref, keep_ref, got_ref, out_ref):
    parts, tall, _ = keep_ref.shape
    place = bound_ref.shape[1]
    pieces = (tall - 8) // 16
    out_ref[:, :place, :] = bound_ref[...]
    both = keep_ref[:, : tall - 8, :] + got_ref[:, : tall - 8, :].astype(f32)
    out_ref[:, place : place + tall - 8, :] = both.astype(bf16)
    tail = keep_ref[0, tall - 8 :, :] + got_ref[0, tall - 8 :, :].astype(f32)
    rows = bias_rows([tail[piece : piece + 1] + tail[pieces + piece : pieces + piece + 1] for piece in range(pieces)])
    out_ref[:, place + tall - 8 :, :] = jnp.broadcast_to(rows.astype(bf16)[None], (parts, 8, LANES))


def chip_sums(slots, hub_rows, rows, back_ref):
    parts, tall, _ = back_ref.shape
    pieces = (tall - 8) // (slots + hub_rows)
    whole = back_ref[:, pieces * slots :, :].astype(f32)
    count = whole.shape[1]
    whole = whole.reshape(rows // 2, 2, parts // rows, count, LANES)
    return jnp.sum(jnp.sum(whole, axis=2), axis=0), pieces


def both_halves(total, pieces, hub_rows, first):
    half = hub_rows // 2
    columns = []
    for piece in range(pieces):
        place = piece * hub_rows + first
        columns.append(jnp.concatenate([total[0, place : place + half], total[1, place : place + half]], axis=0))
    return jnp.concatenate(columns, axis=1)


def weight_sum_kernel(slots, hub_rows, rows, back_ref, out_ref):
    total, pieces = chip_sums(slots, hub_rows, rows, back_ref)
    weight = both_halves(total, pieces, hub_rows, hub_rows // 2)
    out_ref[...] = by_core(weight.astype(bf16), rows, out_ref.shape[0] // rows)


def other_sums_kernel(scale, slots, hub_rows, rows, back_ref, wn_ref, bias_ref, hub_ref):
    total, pieces = chip_sums(slots, hub_rows, rows, back_ref)
    tail = 0.5 * (total[0, pieces * hub_rows :] + total[1, pieces * hub_rows :])
    bias_ref[...] = jnp.concatenate(
        [tail[piece : piece + 1] + tail[pieces + piece : pieces + piece + 1] for piece in range(pieces)], axis=1
    )
    hub = both_halves(total, pieces, hub_rows, 0)
    high = hub.astype(bf16)
    low = (hub - high.astype(f32)).astype(bf16)
    hub_ref[...] = (dot(high, wn_ref[...], NT) + dot(low, wn_ref[...], NT)) * scale


def weights_kernel(core_ref, near_ref, far_ref, self_ref, neigh_ref):
    width = self_ref.shape[0]
    count = 2 * width // 16
    near, far = near_ref[:count].astype(f32), far_ref[:count].astype(f32)
    first_core = core_ref[0] == 0
    whole = jnp.concatenate([jnp.where(first_core, near, far), jnp.where(first_core, far, near)], axis=1)
    whole = whole.reshape(2 * width, width)
    self_ref[...] = whole[:width]
    neigh_ref[...] = whole[width:]


def scatter_kernel(local_ref, grad_ref, out_ref):
    height = out_ref.shape[0]
    first = pl.program_id(0) * height
    total = None
    for start in range(0, grad_ref.shape[0], TILE):
        rows = index_rows(local_ref, start, TILE)
        part = dot(hits_by_column(rows, first, height), grad_ref[start : start + TILE, :])
        total = part if total is None else total + part
    out_ref[...] = total


def final_kernel(scale, slots, send_ref, back_ref, scat_ref, grad_ref, ws_ref, wn_ref, out_ref):
    height, width = out_ref.shape
    first = pl.program_id(0) * height
    count = send_ref.shape[1]
    returned = jnp.concatenate(
        [
            back_ref[:, piece * slots : (piece + 1) * slots, :].reshape(count, LANES)
            for piece in range(width // LANES)
        ],
        axis=1,
    )
    total = scat_ref[...]
    for start in range(0, count, 512):
        stop = min(count, start + 512)
        hits = hits_by_column([send_ref[:, start:stop]], first, height)
        total = total + dot(hits, returned[start:stop])
    out_ref[...] = dot(grad_ref[...], ws_ref[...], NT) + dot((total * scale).astype(bf16), wn_ref[...], NT)


def call(
    kernel, ins, in_specs, outs, out_specs, name, grid=(), scratch=(), flops=0, moved=0, limit=SOME_VMEM
):
    return pl.pallas_call(
        kernel,
        grid=grid,
        in_specs=in_specs,
        out_specs=out_specs,
        out_shape=outs,
        scratch_shapes=scratch,
        compiler_params=params(limit),
        cost_estimate=cost(flops, moved),
        name=name,
    )(*ins)


def whole_block(shape):
    return pl.BlockSpec(shape, lambda *_: (0,) * len(shape))


def body(
    features,
    hub_features,
    w_self,
    w_neigh,
    out_bias,
    local_edges,
    hub_edges,
    remote_edges,
    send_rows,
    cotangent,
):
    nodes, width = features.shape
    hub_rows = hub_features.shape[0]
    parts = lax.axis_size(AXES)
    slots = send_rows.shape[1] // parts
    slab = slots + hub_rows
    pieces = width // LANES
    pay = pieces * slab + 8
    core = (lax.axis_index("row") % 2).astype(jnp.int32).reshape(1)
    rows = lax.axis_size("row")
    half = hub_rows // 2
    table = parts * slab
    scale = 1.0 / (local_edges.shape[1] + hub_edges.shape[1] + remote_edges.shape[1])
    local_t, hub_t, remote_t = local_edges.T, hub_edges.T, remote_edges.T
    bias = out_bias.reshape(1, width)
    shape = jax.ShapeDtypeStruct

    def sibling(value):
        return lax.ppermute(value, "row", [(r, r ^ 1) for r in range(rows)])

    def exchange(value):
        return lax.all_to_all(value, AXES, split_axis=0, concat_axis=0, tiled=True)

    sending = call(
        functools.partial(pick_kernel, rows),
        (send_rows, features, hub_features),
        [VMEM, VMEM, VMEM],
        shape((parts, slots + half, width), bf16),
        whole_block((parts, slots + half, width)),
        "pick_rows",
        limit=MOST_VMEM,
        flops=2 * parts * slots * nodes * width,
        moved=nodes * width * 2,
    )
    sending, features = lax.optimization_barrier((sending, features))
    received = exchange(sending)

    block = TILE
    by_block = pl.BlockSpec((block, width), lambda i: (i, 0))
    packed = 2 * width + table
    local_sum, pack = call(
        functools.partial(local_kernel, parts * slots, hub_rows),
        (core, local_t, remote_t, hub_t, features, features, cotangent),
        [SMEM]
        + [pl.BlockSpec((edges.shape[0], block), lambda i: (0, i)) for edges in (local_t, remote_t, hub_t)]
        + [whole_block((nodes, width)), by_block, by_block],
        [shape((nodes, width), f32), pltpu.HBM((nodes, packed), bf16)],
        [by_block, pl.BlockSpec((block, packed), lambda i: (i, 0))],
        "local_gather",
        grid=(nodes // block,),
        flops=8 * nodes * nodes * width,
        moved=nodes * packed * 2,
    )

    received, local_sum, pack = lax.optimization_barrier((received, local_sum, pack))
    near_hubs = call(
        functools.partial(half_kernel, slots),
        [received],
        [VMEM],
        shape((parts * half, width), bf16),
        VMEM,
        "take_hubs",
        moved=parts * half * width * 4,
    )
    far_hubs = sibling(near_hubs)

    activated, grad_pre, bound_terms, keep, give = call(
        functools.partial(middle_kernel, scale, slots),
        [core, received, near_hubs, far_hubs, w_self, w_neigh, bias, local_sum, pack],
        [SMEM] + [VMEM] * 7 + [HBM],
        [pltpu.HBM((nodes, width), bf16)] * 2
        + [
            shape((parts, pieces * slots, LANES), bf16),
            shape((parts, pieces * hub_rows + 8, LANES), f32),
            shape((parts, pieces * hub_rows + 8, LANES), bf16),
        ],
        [HBM] * 2 + [VMEM] * 3,
        "activate",
        limit=MUCH_VMEM,
        scratch=[
            pltpu.VMEM((nodes, packed + width), bf16),
            pltpu.VMEM((nodes, width), bf16),
            pltpu.VMEM((nodes, width), bf16),
            pltpu.VMEM((width, 2 * width + table), f32),
            pltpu.SemaphoreType.DMA((2, nodes // TILE)),
            pltpu.SemaphoreType.DMA((2, nodes // TILE)),
        ],
        flops=4 * nodes * table * width,
        moved=nodes * packed * 2,
    )
    got = sibling(give)
    back = exchange(
        call(
            join_kernel,
            [bound_terms, keep, got],
            [VMEM] * 3,
            shape((parts, pay, LANES), bf16),
            VMEM,
            "join_siblings",
            moved=parts * pay * LANES * 6,
        )
    )

    scattered = call(
        scatter_kernel,
        (local_t, grad_pre),
        [whole_block(local_t.shape), whole_block((nodes, width))],
        shape((nodes, width), f32),
        pl.BlockSpec((block, width), lambda i: (i, 0)),
        "local_scatter",
        grid=(nodes // block,),
        flops=8 * nodes * nodes * width,
        moved=nodes * width * 6,
    )
    back, scattered = lax.optimization_barrier((back, scattered))
    weight_rows = call(
        functools.partial(weight_sum_kernel, slots, hub_rows, rows),
        (back,),
        [VMEM],
        shape((parts, 8, width), bf16),
        VMEM,
        "weight_sums",
        moved=parts * pay * width * 2,
    )
    near_weights = exchange(weight_rows)
    grad_bias, grad_hubs = call(
        functools.partial(other_sums_kernel, scale, slots, hub_rows, rows),
        (back, w_neigh),
        [VMEM, VMEM],
        [shape((1, width), f32), shape((hub_rows, width), f32)],
        [whole_block((1, width)), whole_block((hub_rows, width))],
        "hub_sums",
        moved=parts * pay * width * 2,
    )

    height = 2 * TILE
    by_height = pl.BlockSpec((height, width), lambda i: (i, 0))
    grad_features = call(
        functools.partial(final_kernel, scale, slots),
        (send_rows, back, scattered, grad_pre, w_self, w_neigh),
        [whole_block(send_rows.shape), whole_block((parts, pay, LANES)), by_height, by_height]
        + [whole_block((width, width))] * 2,
        shape((nodes, width), f32),
        by_height,
        "return_scatter",
        grid=(nodes // height,),
        flops=2 * nodes * parts * slots * width,
        moved=nodes * width * 10,
    )
    near_weights, grad_features = lax.optimization_barrier((near_weights, grad_features))
    grad_w_self, grad_w_neigh = call(
        weights_kernel,
        [core, near_weights, sibling(near_weights)],
        [SMEM, VMEM, VMEM],
        [shape((width, width), f32)] * 2,
        [whole_block((width, width))] * 2,
        "weights",
        moved=width * width * 12,
    )
    return (activated, grad_features, grad_hubs, grad_w_self, grad_w_neigh, grad_bias.reshape(width))


def solution(mesh):
    split = P(AXES, None)
    return jax.shard_map(
        body,
        mesh=mesh,
        in_specs=(split, split, P(), P(), P(), split, split, split, split, split),
        out_specs=(split, split, split, P(), P(), P()),
        check_vma=False,
    )
```

```python
import functools

import jax
import jax.numpy as jnp
from jax import lax
from jax.experimental import pallas as pl
from jax.experimental.pallas import tpu as pltpu
from jax.sharding import PartitionSpec as P

AXES = ("row", "col")
LANES = 128
TILE = 256
MOST_VMEM = 61952 * 1024
SOME_VMEM = 44 * 1024 * 1024
MUCH_VMEM = 47 * 1024 * 1024
NT = (((1,), (1,)), ((), ()))
TN = (((0,), (0,)), ((), ()))
VMEM = pl.BlockSpec(memory_space=pltpu.VMEM)
SMEM = pl.BlockSpec(memory_space=pltpu.SMEM)
HBM = pl.BlockSpec(memory_space=pltpu.HBM)
bf16, f32 = jnp.bfloat16, jnp.float32


def params(limit):
    return pltpu.CompilerParams(vmem_limit_bytes=limit)


def cost(flops, moved):
    return pl.CostEstimate(flops=int(flops), bytes_accessed=int(moved), transcendentals=0)


def along_rows(index_row):
    count = index_row.shape[1]
    return jnp.transpose(jnp.broadcast_to(index_row, (LANES, count))).astype(jnp.int16)


def stack_rows(value, height):
    count = value.shape[1]
    return jnp.broadcast_to(value[None], (height // 16, 16, count)).reshape(height, count)


def count_hits(entries, here):
    one, zero = jnp.ones(here.shape, bf16), jnp.zeros(here.shape, bf16)
    total = None
    for entry in entries:
        hit = jnp.where(entry == here, one, zero)
        total = hit if total is None else total + hit
    return total


def hits_by_row(columns, first, width):
    rows = columns[0].shape[0]
    lane = lax.broadcasted_iota(jnp.int32, (16, LANES), 1).astype(jnp.int16)
    tiles = [
        count_hits(columns, stack_rows(lane + jnp.int16(start), rows)) for start in range(first, first + width, LANES)
    ]
    return jnp.concatenate(tiles, axis=1) if len(tiles) > 1 else tiles[0]


def hits_by_column(index_rows, first, height):
    count = index_rows[0].shape[1]
    group = 64
    down = lax.broadcasted_iota(jnp.int32, (group, count), 0).astype(jnp.int16)
    entries = [
        stack_rows(jnp.broadcast_to(row - first, (16, count)).astype(jnp.int16), group) for row in index_rows
    ]
    return jnp.concatenate(
        [count_hits(entries, down + jnp.int16(start)) for start in range(0, height, group)], axis=0
    )


def dot(a, b, dims=(((1,), (0,)), ((), ()))):
    return lax.dot_general(a, b, dims, preferred_element_type=f32)


def index_rows(ref, start, count):
    return [ref[j : j + 1, pl.ds(start, count)] for j in range(ref.shape[0])]


def by_core(value, rows, cols):
    half = value.shape[0] // 2
    value = value.astype(f32)
    halves = [value[core * half : (core + 1) * half] for core in (0, 1)]
    blocks = [jnp.broadcast_to(halves[row % 2][None], (cols,) + halves[0].shape) for row in range(rows)]
    return jnp.concatenate(blocks, axis=0).astype(bf16)


def pick_kernel(rows, send_ref, feat_ref, hub_ref, out_ref):
    parts, slab, width = out_ref.shape
    slots = slab - hub_ref.shape[0] // 2
    total = send_ref.shape[1]
    step = min(512, total)
    for start in range(0, total, step):
        column = along_rows(send_ref[:, start : start + step])
        picked = dot(hits_by_row([column], 0, feat_ref.shape[0]), feat_ref[...])
        out_ref[start // slots : (start + step) // slots, :slots, :] = (
            picked.astype(bf16).reshape(step // slots, slots, width)
        )
    out_ref[:, slots:, :] = by_core(hub_ref[...], rows, parts // rows)


def half_kernel(slots, table_ref, out_ref):
    out_ref[...] = table_ref[:, slots:, :].astype(f32).reshape(out_ref.shape).astype(bf16)


def local_kernel(split, hub_rows, core_ref, local_ref, remote_ref, hub_ref, feat_ref, own_ref, cot_ref, sum_ref, pack_ref, turned_ref):
    nodes, width = feat_ref.shape
    columns = [along_rows(row) for row in index_rows(local_ref, 0, TILE)]
    total = None
    for first in range(0, nodes, TILE):
        part = dot(hits_by_row(columns, first, TILE), feat_ref[first : first + TILE, :])
        total = part if total is None else total + part
    sum_ref[...] = total
    pack_ref[:, :width] = cot_ref[...]
    pack_ref[:, width : 2 * width] = own_ref[...]
    place = 2 * width
    counts = pack_ref.shape[1] - place
    half = hub_rows // 2
    hubs = []
    for hub in index_rows(hub_ref, 0, TILE):
        owner = lax.div(hub, jnp.int32(hub_rows))
        within = hub - owner * hub_rows
        other = (within >= half) != (core_ref[0] == 1)
        within = jnp.where(within >= half, within - half, within)
        hubs.append(owner * half + within + jnp.where(other, (counts - split) // 2, 0))
    for index, share in ((index_rows(remote_ref, 0, TILE), split), (hubs, counts - split)):
        columns = [along_rows(row) for row in index]
        for first in range(0, share, TILE):
            there = slice(place - 2 * width + first, place - 2 * width + first + TILE)
            pack_ref[:, place + first : place + first + TILE] = hits_by_row(columns, first, TILE)
            turned_ref[there, :] = hits_by_column(index, first, TILE)
        place += share


def middle_kernel(
    scale,
    slots,
    core_ref,
    table_ref,
    near_ref,
    far_ref,
    ws_ref,
    wn_ref,
    bias_ref,
    sum_ref,
    pack_hbm,
    by_col_hbm,
    act_hbm,
    grad_hbm,
    bound_ref,
    keep_ref,
    give_ref,
    pack,
    by_col,
    act,
    grad_all,
    terms,
    in_sem,
    col_sem,
    out_sem,
):
    nodes, width = sum_ref.shape
    parts, slab, _ = table_ref.shape
    half = slab - slots
    hub_rows = 2 * half
    bounds, hubs = parts * slots, parts * hub_rows
    size = 2 * TILE
    blocks = nodes // size
    features, counts = slice(width, 2 * width), 3 * width

    def here(block):
        return slice(block * size, (block + 1) * size)

    def loads(block):
        at = here(block)
        return [
            pltpu.make_async_copy(pack_hbm.at[at, : 2 * width], pack.at[at, : 2 * width], in_sem.at[0, block]),
            pltpu.make_async_copy(pack_hbm.at[at, 2 * width :], pack.at[at, counts:], in_sem.at[1, block]),
        ]

    coming = [loads(block) for block in range(blocks)]
    for group in coming:
        for copy in group:
            copy.start()
    col_load = pltpu.make_async_copy(by_col_hbm, by_col, col_sem)
    col_load.start()
    table = jnp.concatenate(
        [table_ref[:, :slots, :].reshape(bounds, width), near_ref[...], far_ref[...]], axis=0
    )
    half_weights = jnp.concatenate([ws_ref[...], wn_ref[...]], axis=0) * jnp.bfloat16(0.5)
    half_bias = 0.5 * bias_ref[...]
    stores = []
    total = None
    turned = None
    for block in range(blocks + 2):
        following = None
        if block < blocks:
            for copy in coming[block]:
                copy.wait()
            following = sum_ref[here(block), :] + dot(pack[here(block), counts:], table)
        if block > 1:
            part = dot(turned, pack[here(block - 2), width:counts])
            terms[...] = part if block == 2 else terms[...] + part
        if 0 < block <= blocks:
            at = here(block - 1)
            pack[at, 2 * width : counts] = (total * scale).astype(bf16)
            arg = dot(pack[at, width:counts], half_weights) + half_bias
            tanh = jnp.tanh(arg)
            above = 1.0 + tanh
            act[at, :] = (arg * above).astype(bf16)
            slope = above * (0.5 + (0.5 * arg) * (1.0 - tanh))
            grad = (pack[at, :width].astype(f32) * slope).astype(bf16)
            grad_all[at, :] = grad
            turned = jnp.transpose(grad)
            for which, (source, target) in enumerate(((act, act_hbm), (grad_all, grad_hbm))):
                store = pltpu.make_async_copy(source.at[at, :], target.at[at, :], out_sem.at[which, block - 1])
                store.start()
                stores.append(store)
        total = following

    pieces = width // LANES
    step = 2 * width

    grad = grad_all[...]
    col_load.wait()

    def term_rows(first, count, rows):
        return dot(by_col[first : first + count, :], grad).reshape(count // rows, rows, width)

    def lanes(piece):
        return slice(piece * LANES, (piece + 1) * LANES)

    first_core = core_ref[0] == 0
    weights = jnp.transpose(terms[...]).reshape(step // hub_rows, hub_rows, width)
    own = jnp.where(first_core, weights[:, :half], weights[:, half:])
    other = jnp.where(first_core, weights[:, half:], weights[:, :half])
    count = step // hub_rows
    for low in range(0, parts, count):
        if low > 0:
            own = other = jnp.zeros_like(own)
        first = bounds + low * half
        keep = jnp.concatenate([term_rows(first, count * half, half), own], axis=1)
        give = jnp.concatenate([term_rows(first + hubs // 2, count * half, half), other], axis=1).astype(bf16)
        at = slice(low, low + count)
        for piece in range(pieces):
            there = slice(piece * hub_rows, (piece + 1) * hub_rows)
            keep_ref[at, there, :] = keep[:, :, lanes(piece)]
            give_ref[at, there, :] = give[:, :, lanes(piece)]
    bias_total = dot(jnp.ones((16, nodes), bf16), grad)[:1]
    rows = bias_rows([bias_total[:, lanes(piece)] for piece in range(pieces)])
    keep_ref[:, pieces * hub_rows :, :] = jnp.broadcast_to(rows[None], (parts, 8, LANES))
    give_ref[:, pieces * hub_rows :, :] = jnp.broadcast_to(rows.astype(bf16)[None], (parts, 8, LANES))
    for low in range(0, bounds, step):
        bound_terms = term_rows(low, step, slots).astype(bf16)
        for piece in range(pieces):
            bound_ref[low // slots : (low + step) // slots, piece * slots : (piece + 1) * slots, :] = (
                bound_terms[:, :, lanes(piece)]
            )
    for store in stores:
        store.wait()


def bias_rows(parts):
    line = lax.broadcasted_iota(jnp.int32, (8, LANES), 0)
    rows = jnp.zeros((8, LANES), f32)
    for piece, value in enumerate(parts):
        high = value.astype(bf16).astype(f32)
        rows = jnp.where(line == piece, high, rows)
        rows = jnp.where(line == len(parts) + piece, value - high, rows)
    return rows


def join_kernel(bound_ref, keep_ref, got_ref, out_ref):
    parts, tall, _ = keep_ref.shape
    place = bound_ref.shape[1]
    pieces = (tall - 8) // 16
    out_ref[:, :place, :] = bound_ref[...]
    both = keep_ref[:, : tall - 8, :] + got_ref[:, : tall - 8, :].astype(f32)
    out_ref[:, place : place + tall - 8, :] = both.astype(bf16)
    tail = keep_ref[0, tall - 8 :, :] + got_ref[0, tall - 8 :, :].astype(f32)
    rows = bias_rows([tail[piece : piece + 1] + tail[pieces + piece : pieces + piece + 1] for piece in range(pieces)])
    out_ref[:, place + tall - 8 :, :] = jnp.broadcast_to(rows.astype(bf16)[None], (parts, 8, LANES))


def chip_sums(slots, hub_rows, rows, back_ref):
    parts, tall, _ = back_ref.shape
    pieces = (tall - 8) // (slots + hub_rows)
    whole = back_ref[:, pieces * slots :, :].astype(f32)
    count = whole.shape[1]
    whole = whole.reshape(rows // 2, 2, parts // rows, count, LANES)
    return jnp.sum(jnp.sum(whole, axis=2), axis=0), pieces


def both_halves(total, pieces, hub_rows, first):
    half = hub_rows // 2
    columns = []
    for piece in range(pieces):
        place = piece * hub_rows + first
        columns.append(jnp.concatenate([total[0, place : place + half], total[1, place : place + half]], axis=0))
    return jnp.concatenate(columns, axis=1)


def weight_sum_kernel(slots, hub_rows, rows, back_ref, out_ref):
    total, pieces = chip_sums(slots, hub_rows, rows, back_ref)
    weight = both_halves(total, pieces, hub_rows, hub_rows // 2)
    out_ref[...] = by_core(weight.astype(bf16), rows, out_ref.shape[0] // rows)


def other_sums_kernel(scale, slots, hub_rows, rows, back_ref, wn_ref, bias_ref, hub_ref):
    total, pieces = chip_sums(slots, hub_rows, rows, back_ref)
    tail = 0.5 * (total[0, pieces * hub_rows :] + total[1, pieces * hub_rows :])
    bias_ref[...] = jnp.concatenate(
        [tail[piece : piece + 1] + tail[pieces + piece : pieces + piece + 1] for piece in range(pieces)], axis=1
    )
    hub = both_halves(total, pieces, hub_rows, 0)
    high = hub.astype(bf16)
    low = (hub - high.astype(f32)).astype(bf16)
    hub_ref[...] = (dot(high, wn_ref[...], NT) + dot(low, wn_ref[...], NT)) * scale


def weights_kernel(core_ref, near_ref, far_ref, self_ref, neigh_ref):
    width = self_ref.shape[0]
    count = 2 * width // 16
    near, far = near_ref[:count].astype(f32), far_ref[:count].astype(f32)
    first_core = core_ref[0] == 0
    whole = jnp.concatenate([jnp.where(first_core, near, far), jnp.where(first_core, far, near)], axis=1)
    whole = whole.reshape(2 * width, width)
    self_ref[...] = whole[:width]
    neigh_ref[...] = whole[width:]


def scatter_kernel(local_ref, grad_ref, out_ref):
    height = out_ref.shape[0]
    first = pl.program_id(0) * height
    total = None
    for start in range(0, grad_ref.shape[0], TILE):
        rows = index_rows(local_ref, start, TILE)
        part = dot(hits_by_column(rows, first, height), grad_ref[start : start + TILE, :])
        total = part if total is None else total + part
    out_ref[...] = total


def final_kernel(scale, slots, send_ref, back_ref, scat_ref, grad_ref, ws_ref, wn_ref, out_ref):
    height, width = out_ref.shape
    first = pl.program_id(0) * height
    count = send_ref.shape[1]
    returned = jnp.concatenate(
        [
            back_ref[:, piece * slots : (piece + 1) * slots, :].reshape(count, LANES)
            for piece in range(width // LANES)
        ],
        axis=1,
    )
    total = scat_ref[...]
    for start in range(0, count, 512):
        stop = min(count, start + 512)
        hits = hits_by_column([send_ref[:, start:stop]], first, height)
        total = total + dot(hits, returned[start:stop])
    out_ref[...] = dot(grad_ref[...], ws_ref[...], NT) + dot((total * scale).astype(bf16), wn_ref[...], NT)


def call(
    kernel, ins, in_specs, outs, out_specs, name, grid=(), scratch=(), flops=0, moved=0, limit=SOME_VMEM
):
    return pl.pallas_call(
        kernel,
        grid=grid,
        in_specs=in_specs,
        out_specs=out_specs,
        out_shape=outs,
        scratch_shapes=scratch,
        compiler_params=params(limit),
        cost_estimate=cost(flops, moved),
        name=name,
    )(*ins)


def whole_block(shape):
    return pl.BlockSpec(shape, lambda *_: (0,) * len(shape))


def body(
    features,
    hub_features,
    w_self,
    w_neigh,
    out_bias,
    local_edges,
    hub_edges,
    remote_edges,
    send_rows,
    cotangent,
):
    nodes, width = features.shape
    hub_rows = hub_features.shape[0]
    parts = lax.axis_size(AXES)
    slots = send_rows.shape[1] // parts
    slab = slots + hub_rows
    pieces = width // LANES
    pay = pieces * slab + 8
    core = (lax.axis_index("row") % 2).astype(jnp.int32).reshape(1)
    rows = lax.axis_size("row")
    half = hub_rows // 2
    table = parts * slab
    scale = 1.0 / (local_edges.shape[1] + hub_edges.shape[1] + remote_edges.shape[1])
    local_t, hub_t, remote_t = local_edges.T, hub_edges.T, remote_edges.T
    bias = out_bias.reshape(1, width)
    shape = jax.ShapeDtypeStruct

    def sibling(value):
        return lax.ppermute(value, "row", [(r, r ^ 1) for r in range(rows)])

    def exchange(value):
        return lax.all_to_all(value, AXES, split_axis=0, concat_axis=0, tiled=True)

    sending = call(
        functools.partial(pick_kernel, rows),
        (send_rows, features, hub_features),
        [VMEM, VMEM, VMEM],
        shape((parts, slots + half, width), bf16),
        whole_block((parts, slots + half, width)),
        "pick_rows",
        limit=MOST_VMEM,
        flops=2 * parts * slots * nodes * width,
        moved=nodes * width * 2,
    )
    sending, features = lax.optimization_barrier((sending, features))
    received = exchange(sending)

    block = TILE
    by_block = pl.BlockSpec((block, width), lambda i: (i, 0))
    packed = 2 * width + table
    local_sum, pack, turned_counts = call(
        functools.partial(local_kernel, parts * slots, hub_rows),
        (core, local_t, remote_t, hub_t, features, features, cotangent),
        [SMEM]
        + [pl.BlockSpec((edges.shape[0], block), lambda i: (0, i)) for edges in (local_t, remote_t, hub_t)]
        + [whole_block((nodes, width)), by_block, by_block],
        [shape((nodes, width), f32), pltpu.HBM((nodes, packed), bf16), pltpu.HBM((table, nodes), bf16)],
        [
            by_block,
            pl.BlockSpec((block, packed), lambda i: (i, 0)),
            pl.BlockSpec((table, block), lambda i: (0, i)),
        ],
        "local_gather",
        grid=(nodes // block,),
        flops=8 * nodes * nodes * width,
        moved=nodes * packed * 2,
    )

    received, local_sum, pack = lax.optimization_barrier((received, local_sum, pack))
    near_hubs = call(
        functools.partial(half_kernel, slots),
        [received],
        [VMEM],
        shape((parts * half, width), bf16),
        VMEM,
        "take_hubs",
        moved=parts * half * width * 4,
    )
    far_hubs = sibling(near_hubs)

    activated, grad_pre, bound_terms, keep, give = call(
        functools.partial(middle_kernel, scale, slots),
        [core, received, near_hubs, far_hubs, w_self, w_neigh, bias, local_sum, pack, turned_counts],
        [SMEM] + [VMEM] * 7 + [HBM] * 2,
        [pltpu.HBM((nodes, width), bf16)] * 2
        + [
            shape((parts, pieces * slots, LANES), bf16),
            shape((parts, pieces * hub_rows + 8, LANES), f32),
            shape((parts, pieces * hub_rows + 8, LANES), bf16),
        ],
        [HBM] * 2 + [VMEM] * 3,
        "activate",
        limit=MUCH_VMEM,
        scratch=[
            pltpu.VMEM((nodes, packed + width), bf16),
            pltpu.VMEM((table, nodes), bf16),
            pltpu.VMEM((nodes, width), bf16),
            pltpu.VMEM((nodes, width), bf16),
            pltpu.VMEM((width, 2 * width), f32),
            pltpu.SemaphoreType.DMA((2, nodes // (2 * TILE))),
            pltpu.SemaphoreType.DMA,
            pltpu.SemaphoreType.DMA((2, nodes // (2 * TILE))),
        ],
        flops=4 * nodes * table * width,
        moved=nodes * packed * 2,
    )
    got = sibling(give)
    back = exchange(
        call(
            join_kernel,
            [bound_terms, keep, got],
            [VMEM] * 3,
            shape((parts, pay, LANES), bf16),
            VMEM,
            "join_siblings",
            moved=parts * pay * LANES * 6,
        )
    )

    scattered = call(
        scatter_kernel,
        (local_t, grad_pre),
        [whole_block(local_t.shape), whole_block((nodes, width))],
        shape((nodes, width), f32),
        pl.BlockSpec((block, width), lambda i: (i, 0)),
        "local_scatter",
        grid=(nodes // block,),
        flops=8 * nodes * nodes * width,
        moved=nodes * width * 6,
    )
    back, scattered = lax.optimization_barrier((back, scattered))
    weight_rows = call(
        functools.partial(weight_sum_kernel, slots, hub_rows, rows),
        (back,),
        [VMEM],
        shape((parts, 8, width), bf16),
        VMEM,
        "weight_sums",
        moved=parts * pay * width * 2,
    )
    near_weights = exchange(weight_rows)
    grad_bias, grad_hubs = call(
        functools.partial(other_sums_kernel, scale, slots, hub_rows, rows),
        (back, w_neigh),
        [VMEM, VMEM],
        [shape((1, width), f32), shape((hub_rows, width), f32)],
        [whole_block((1, width)), whole_block((hub_rows, width))],
        "hub_sums",
        moved=parts * pay * width * 2,
    )

    height = 2 * TILE
    by_height = pl.BlockSpec((height, width), lambda i: (i, 0))
    grad_features = call(
        functools.partial(final_kernel, scale, slots),
        (send_rows, back, scattered, grad_pre, w_self, w_neigh),
        [whole_block(send_rows.shape), whole_block((parts, pay, LANES)), by_height, by_height]
        + [whole_block((width, width))] * 2,
        shape((nodes, width), f32),
        by_height,
        "return_scatter",
        grid=(nodes // height,),
        flops=2 * nodes * parts * slots * width,
        moved=nodes * width * 10,
    )
    near_weights, grad_features = lax.optimization_barrier((near_weights, grad_features))
    grad_w_self, grad_w_neigh = call(
        weights_kernel,
        [core, near_weights, sibling(near_weights)],
        [SMEM, VMEM, VMEM],
        [shape((width, width), f32)] * 2,
        [whole_block((width, width))] * 2,
        "weights",
        moved=width * width * 12,
    )
    return (activated, grad_features, grad_hubs, grad_w_self, grad_w_neigh, grad_bias.reshape(width))


def solution(mesh):
    split = P(AXES, None)
    return jax.shard_map(
        body,
        mesh=mesh,
        in_specs=(split, split, P(), P(), P(), split, split, split, split, split),
        out_specs=(split, split, split, P(), P(), P()),
        check_vma=False,
    )
```

```python
import functools

import jax
import jax.numpy as jnp
from jax import lax
from jax.experimental import pallas as pl
from jax.experimental.pallas import tpu as pltpu
from jax.sharding import PartitionSpec as P

AXES = ("row", "col")
LANES = 128
TILE = 256
MOST_VMEM = 61952 * 1024
SOME_VMEM = 44 * 1024 * 1024
MUCH_VMEM = 47 * 1024 * 1024
NT = (((1,), (1,)), ((), ()))
TN = (((0,), (0,)), ((), ()))
VMEM = pl.BlockSpec(memory_space=pltpu.VMEM)
SMEM = pl.BlockSpec(memory_space=pltpu.SMEM)
HBM = pl.BlockSpec(memory_space=pltpu.HBM)
bf16, f32 = jnp.bfloat16, jnp.float32


def params(limit):
    return pltpu.CompilerParams(vmem_limit_bytes=limit)


def cost(flops, moved):
    return pl.CostEstimate(flops=int(flops), bytes_accessed=int(moved), transcendentals=0)


def along_rows(index_row):
    count = index_row.shape[1]
    return jnp.transpose(jnp.broadcast_to(index_row, (LANES, count))).astype(jnp.int16)


def stack_rows(value, height):
    count = value.shape[1]
    return jnp.broadcast_to(value[None], (height // 16, 16, count)).reshape(height, count)


def count_hits(entries, here):
    one, zero = jnp.ones(here.shape, bf16), jnp.zeros(here.shape, bf16)
    total = None
    for entry in entries:
        hit = jnp.where(entry == here, one, zero)
        total = hit if total is None else total + hit
    return total


def hits_by_row(columns, first, width):
    rows = columns[0].shape[0]
    lane = lax.broadcasted_iota(jnp.int32, (16, LANES), 1).astype(jnp.int16)
    tiles = [
        count_hits(columns, stack_rows(lane + jnp.int16(start), rows)) for start in range(first, first + width, LANES)
    ]
    return jnp.concatenate(tiles, axis=1) if len(tiles) > 1 else tiles[0]


def hits_by_column(index_rows, first, height):
    count = index_rows[0].shape[1]
    group = 64
    down = lax.broadcasted_iota(jnp.int32, (group, count), 0).astype(jnp.int16)
    entries = [
        stack_rows(jnp.broadcast_to(row - first, (16, count)).astype(jnp.int16), group) for row in index_rows
    ]
    return jnp.concatenate(
        [count_hits(entries, down + jnp.int16(start)) for start in range(0, height, group)], axis=0
    )


def dot(a, b, dims=(((1,), (0,)), ((), ()))):
    return lax.dot_general(a, b, dims, preferred_element_type=f32)


def index_rows(ref, start, count):
    return [ref[j : j + 1, pl.ds(start, count)] for j in range(ref.shape[0])]


def by_core(value, rows, cols):
    half = value.shape[0] // 2
    value = value.astype(f32)
    halves = [value[core * half : (core + 1) * half] for core in (0, 1)]
    blocks = [jnp.broadcast_to(halves[row % 2][None], (cols,) + halves[0].shape) for row in range(rows)]
    return jnp.concatenate(blocks, axis=0).astype(bf16)


def pick_kernel(rows, send_ref, feat_ref, hub_ref, out_ref):
    parts, slab, width = out_ref.shape
    slots = slab - hub_ref.shape[0] // 2
    total = send_ref.shape[1]
    step = min(512, total)
    for start in range(0, total, step):
        column = along_rows(send_ref[:, start : start + step])
        picked = dot(hits_by_row([column], 0, feat_ref.shape[0]), feat_ref[...])
        out_ref[start // slots : (start + step) // slots, :slots, :] = (
            picked.astype(bf16).reshape(step // slots, slots, width)
        )
    out_ref[:, slots:, :] = by_core(hub_ref[...], rows, parts // rows)


def half_kernel(slots, table_ref, out_ref):
    out_ref[...] = table_ref[:, slots:, :].astype(f32).reshape(out_ref.shape).astype(bf16)


def local_kernel(split, hub_rows, core_ref, local_ref, remote_ref, hub_ref, feat_ref, own_ref, cot_ref, sum_ref, pack_ref):
    nodes, width = feat_ref.shape
    columns = [along_rows(row) for row in index_rows(local_ref, 0, TILE)]
    total = None
    for first in range(0, nodes, TILE):
        part = dot(hits_by_row(columns, first, TILE), feat_ref[first : first + TILE, :])
        total = part if total is None else total + part
    sum_ref[...] = total
    pack_ref[:, :width] = cot_ref[...]
    pack_ref[:, width : 2 * width] = own_ref[...]
    place = 2 * width
    counts = pack_ref.shape[1] - place
    half = hub_rows // 2
    hubs = []
    for hub in index_rows(hub_ref, 0, TILE):
        owner = lax.div(hub, jnp.int32(hub_rows))
        within = hub - owner * hub_rows
        other = (within >= half) != (core_ref[0] == 1)
        within = jnp.where(within >= half, within - half, within)
        hubs.append(owner * half + within + jnp.where(other, (counts - split) // 2, 0))
    for index, share in ((index_rows(remote_ref, 0, TILE), split), (hubs, counts - split)):
        columns = [along_rows(row) for row in index]
        for first in range(0, share, TILE):
            pack_ref[:, place + first : place + first + TILE] = hits_by_row(columns, first, TILE)
        place += share


def middle_kernel(
    scale,
    slots,
    core_ref,
    table_ref,
    near_ref,
    far_ref,
    ws_ref,
    wn_ref,
    bias_ref,
    sum_ref,
    pack_hbm,
    act_hbm,
    grad_hbm,
    bound_ref,
    keep_ref,
    give_ref,
    pack,
    act,
    grad_all,
    terms,
    in_sem,
    out_sem,
):
    nodes, width = sum_ref.shape
    parts, slab, _ = table_ref.shape
    half = slab - slots
    hub_rows = 2 * half
    bounds, hubs = parts * slots, parts * hub_rows
    size = 2 * TILE
    blocks = nodes // size
    features, counts = slice(width, 2 * width), 3 * width

    def here(block):
        return slice(block * size, (block + 1) * size)

    def loads(block):
        at = here(block)
        return [
            pltpu.make_async_copy(pack_hbm.at[at, : 2 * width], pack.at[at, : 2 * width], in_sem.at[0, block]),
            pltpu.make_async_copy(pack_hbm.at[at, 2 * width :], pack.at[at, counts:], in_sem.at[1, block]),
        ]

    coming = [loads(block) for block in range(blocks)]
    for group in coming:
        for copy in group:
            copy.start()
    table = jnp.concatenate(
        [table_ref[:, :slots, :].reshape(bounds, width), near_ref[...], far_ref[...]], axis=0
    )
    half_weights = jnp.concatenate([ws_ref[...], wn_ref[...]], axis=0) * jnp.bfloat16(0.5)
    half_bias = 0.5 * bias_ref[...]
    stores = []
    total = None
    turned = None
    for block in range(blocks + 2):
        following = None
        if block < blocks:
            for copy in coming[block]:
                copy.wait()
            following = sum_ref[here(block), :] + dot(pack[here(block), counts:], table)
        if block > 1:
            part = dot(turned, pack[here(block - 2), width:])
            terms[...] = part if block == 2 else terms[...] + part
        if 0 < block <= blocks:
            at = here(block - 1)
            pack[at, 2 * width : counts] = (total * scale).astype(bf16)
            arg = dot(pack[at, width:counts], half_weights) + half_bias
            tanh = jnp.tanh(arg)
            above = 1.0 + tanh
            act[at, :] = (arg * above).astype(bf16)
            slope = above * (0.5 + (0.5 * arg) * (1.0 - tanh))
            grad = (pack[at, :width].astype(f32) * slope).astype(bf16)
            grad_all[at, :] = grad
            turned = jnp.transpose(grad)
            for which, (source, target) in enumerate(((act, act_hbm), (grad_all, grad_hbm))):
                store = pltpu.make_async_copy(source.at[at, :], target.at[at, :], out_sem.at[which, block - 1])
                store.start()
                stores.append(store)
        total = following

    pieces = width // LANES
    step = 2 * width

    def term_rows(first, count, rows):
        return jnp.transpose(terms[:, first : first + count]).reshape(count // rows, rows, width)

    def lanes(piece):
        return slice(piece * LANES, (piece + 1) * LANES)

    first_core = core_ref[0] == 0
    weights = term_rows(0, step, hub_rows)
    own = jnp.where(first_core, weights[:, :half], weights[:, half:])
    other = jnp.where(first_core, weights[:, half:], weights[:, :half])
    count = step // hub_rows
    for low in range(0, parts, count):
        if low > 0:
            own = other = jnp.zeros_like(own)
        first = step + bounds + low * half
        keep = jnp.concatenate([term_rows(first, count * half, half), own], axis=1)
        give = jnp.concatenate([term_rows(first + hubs // 2, count * half, half), other], axis=1).astype(bf16)
        at = slice(low, low + count)
        for piece in range(pieces):
            there = slice(piece * hub_rows, (piece + 1) * hub_rows)
            keep_ref[at, there, :] = keep[:, :, lanes(piece)]
            give_ref[at, there, :] = give[:, :, lanes(piece)]
    bias_total = dot(jnp.ones((16, nodes), bf16), grad_all[...])[:1]
    rows = bias_rows([bias_total[:, lanes(piece)] for piece in range(pieces)])
    keep_ref[:, pieces * hub_rows :, :] = jnp.broadcast_to(rows[None], (parts, 8, LANES))
    give_ref[:, pieces * hub_rows :, :] = jnp.broadcast_to(rows.astype(bf16)[None], (parts, 8, LANES))
    for low in range(0, bounds, step):
        bound_terms = term_rows(step + low, step, slots).astype(bf16)
        for piece in range(pieces):
            bound_ref[low // slots : (low + step) // slots, piece * slots : (piece + 1) * slots, :] = (
                bound_terms[:, :, lanes(piece)]
            )
    for store in stores:
        store.wait()


def bias_rows(parts):
    line = lax.broadcasted_iota(jnp.int32, (8, LANES), 0)
    rows = jnp.zeros((8, LANES), f32)
    for piece, value in enumerate(parts):
        high = value.astype(bf16).astype(f32)
        rows = jnp.where(line == piece, high, rows)
        rows = jnp.where(line == len(parts) + piece, value - high, rows)
    return rows


def join_kernel(bound_ref, keep_ref, got_ref, out_ref):
    parts, tall, _ = keep_ref.shape
    place = bound_ref.shape[1]
    pieces = (tall - 8) // 16
    out_ref[:, :place, :] = bound_ref[...]
    both = keep_ref[:, : tall - 8, :] + got_ref[:, : tall - 8, :].astype(f32)
    out_ref[:, place : place + tall - 8, :] = both.astype(bf16)
    tail = keep_ref[0, tall - 8 :, :] + got_ref[0, tall - 8 :, :].astype(f32)
    rows = bias_rows([tail[piece : piece + 1] + tail[pieces + piece : pieces + piece + 1] for piece in range(pieces)])
    out_ref[:, place + tall - 8 :, :] = jnp.broadcast_to(rows.astype(bf16)[None], (parts, 8, LANES))


def chip_sums(slots, hub_rows, rows, back_ref):
    parts, tall, _ = back_ref.shape
    pieces = (tall - 8) // (slots + hub_rows)
    whole = back_ref[:, pieces * slots :, :].astype(f32)
    count = whole.shape[1]
    whole = whole.reshape(rows // 2, 2, parts // rows, count, LANES)
    return jnp.sum(jnp.sum(whole, axis=2), axis=0), pieces


def both_halves(total, pieces, hub_rows, first):
    half = hub_rows // 2
    columns = []
    for piece in range(pieces):
        place = piece * hub_rows + first
        columns.append(jnp.concatenate([total[0, place : place + half], total[1, place : place + half]], axis=0))
    return jnp.concatenate(columns, axis=1)


def weight_sum_kernel(slots, hub_rows, rows, back_ref, out_ref):
    total, pieces = chip_sums(slots, hub_rows, rows, back_ref)
    weight = both_halves(total, pieces, hub_rows, hub_rows // 2)
    out_ref[...] = by_core(weight.astype(bf16), rows, out_ref.shape[0] // rows)


def other_sums_kernel(scale, slots, hub_rows, rows, back_ref, wn_ref, bias_ref, hub_ref):
    total, pieces = chip_sums(slots, hub_rows, rows, back_ref)
    tail = 0.5 * (total[0, pieces * hub_rows :] + total[1, pieces * hub_rows :])
    bias_ref[...] = jnp.concatenate(
        [tail[piece : piece + 1] + tail[pieces + piece : pieces + piece + 1] for piece in range(pieces)], axis=1
    )
    hub = both_halves(total, pieces, hub_rows, 0)
    high = hub.astype(bf16)
    low = (hub - high.astype(f32)).astype(bf16)
    hub_ref[...] = (dot(high, wn_ref[...], NT) + dot(low, wn_ref[...], NT)) * scale


def weights_kernel(core_ref, near_ref, far_ref, self_ref, neigh_ref):
    width = self_ref.shape[0]
    count = 2 * width // 16
    near, far = near_ref[:count].astype(f32), far_ref[:count].astype(f32)
    first_core = core_ref[0] == 0
    whole = jnp.concatenate([jnp.where(first_core, near, far), jnp.where(first_core, far, near)], axis=1)
    whole = whole.reshape(2 * width, width)
    self_ref[...] = whole[:width]
    neigh_ref[...] = whole[width:]


def scatter_kernel(local_ref, grad_ref, out_ref):
    height = out_ref.shape[0]
    first = pl.program_id(0) * height
    total = None
    for start in range(0, grad_ref.shape[0], TILE):
        rows = index_rows(local_ref, start, TILE)
        part = dot(hits_by_column(rows, first, height), grad_ref[start : start + TILE, :])
        total = part if total is None else total + part
    out_ref[...] = total


def final_kernel(scale, slots, send_ref, back_ref, scat_ref, grad_ref, ws_ref, wn_ref, out_ref):
    height, width = out_ref.shape
    first = pl.program_id(0) * height
    count = send_ref.shape[1]
    returned = jnp.concatenate(
        [
            back_ref[:, piece * slots : (piece + 1) * slots, :].reshape(count, LANES)
            for piece in range(width // LANES)
        ],
        axis=1,
    )
    total = scat_ref[...]
    for start in range(0, count, 512):
        stop = min(count, start + 512)
        hits = hits_by_column([send_ref[:, start:stop]], first, height)
        total = total + dot(hits, returned[start:stop])
    out_ref[...] = dot(grad_ref[...], ws_ref[...], NT) + dot((total * scale).astype(bf16), wn_ref[...], NT)


def call(
    kernel, ins, in_specs, outs, out_specs, name, grid=(), scratch=(), flops=0, moved=0, limit=SOME_VMEM
):
    return pl.pallas_call(
        kernel,
        grid=grid,
        in_specs=in_specs,
        out_specs=out_specs,
        out_shape=outs,
        scratch_shapes=scratch,
        compiler_params=params(limit),
        cost_estimate=cost(flops, moved),
        name=name,
    )(*ins)


def whole_block(shape):
    return pl.BlockSpec(shape, lambda *_: (0,) * len(shape))


def body(
    features,
    hub_features,
    w_self,
    w_neigh,
    out_bias,
    local_edges,
    hub_edges,
    remote_edges,
    send_rows,
    cotangent,
):
    nodes, width = features.shape
    hub_rows = hub_features.shape[0]
    parts = lax.axis_size(AXES)
    slots = send_rows.shape[1] // parts
    slab = slots + hub_rows
    pieces = width // LANES
    pay = pieces * slab + 8
    core = (lax.axis_index("row") % 2).astype(jnp.int32).reshape(1)
    rows = lax.axis_size("row")
    half = hub_rows // 2
    table = parts * slab
    scale = 1.0 / (local_edges.shape[1] + hub_edges.shape[1] + remote_edges.shape[1])
    local_t, hub_t, remote_t = local_edges.T, hub_edges.T, remote_edges.T
    bias = out_bias.reshape(1, width)
    shape = jax.ShapeDtypeStruct

    def sibling(value):
        return lax.ppermute(value, "row", [(r, r ^ 1) for r in range(rows)])

    def exchange(value):
        return lax.all_to_all(value, AXES, split_axis=0, concat_axis=0, tiled=True)

    sending = call(
        functools.partial(pick_kernel, rows),
        (send_rows, features, hub_features),
        [VMEM, VMEM, VMEM],
        shape((parts, slots + half, width), bf16),
        whole_block((parts, slots + half, width)),
        "pick_rows",
        limit=MOST_VMEM,
        flops=2 * parts * slots * nodes * width,
        moved=nodes * width * 2,
    )
    sending, features = lax.optimization_barrier((sending, features))
    received = exchange(sending)

    block = TILE
    by_block = pl.BlockSpec((block, width), lambda i: (i, 0))
    packed = 2 * width + table
    local_sum, pack = call(
        functools.partial(local_kernel, parts * slots, hub_rows),
        (core, local_t, remote_t, hub_t, features, features, cotangent),
        [SMEM]
        + [pl.BlockSpec((edges.shape[0], block), lambda i: (0, i)) for edges in (local_t, remote_t, hub_t)]
        + [whole_block((nodes, width)), by_block, by_block],
        [shape((nodes, width), f32), pltpu.HBM((nodes, packed), bf16)],
        [by_block, pl.BlockSpec((block, packed), lambda i: (i, 0))],
        "local_gather",
        grid=(nodes // block,),
        flops=8 * nodes * nodes * width,
        moved=nodes * packed * 2,
    )

    received, local_sum, pack = lax.optimization_barrier((received, local_sum, pack))
    near_hubs = call(
        functools.partial(half_kernel, slots),
        [received],
        [VMEM],
        shape((parts * half, width), bf16),
        VMEM,
        "take_hubs",
        moved=parts * half * width * 4,
    )
    far_hubs = sibling(near_hubs)

    activated, grad_pre, bound_terms, keep, give = call(
        functools.partial(middle_kernel, scale, slots),
        [core, received, near_hubs, far_hubs, w_self, w_neigh, bias, local_sum, pack],
        [SMEM] + [VMEM] * 7 + [HBM],
        [pltpu.HBM((nodes, width), bf16)] * 2
        + [
            shape((parts, pieces * slots, LANES), bf16),
            shape((parts, pieces * hub_rows + 8, LANES), f32),
            shape((parts, pieces * hub_rows + 8, LANES), bf16),
        ],
        [HBM] * 2 + [VMEM] * 3,
        "activate",
        limit=MUCH_VMEM,
        scratch=[
            pltpu.VMEM((nodes, packed + width), bf16),
            pltpu.VMEM((nodes, width), bf16),
            pltpu.VMEM((nodes, width), bf16),
            pltpu.VMEM((width, 2 * width + table), f32),
            pltpu.SemaphoreType.DMA((2, nodes // (2 * TILE))),
            pltpu.SemaphoreType.DMA((2, nodes // (2 * TILE))),
        ],
        flops=4 * nodes * table * width,
        moved=nodes * packed * 2,
    )
    got = sibling(give)
    back = exchange(
        call(
            join_kernel,
            [bound_terms, keep, got],
            [VMEM] * 3,
            shape((parts, pay, LANES), bf16),
            VMEM,
            "join_siblings",
            moved=parts * pay * LANES * 6,
        )
    )

    scattered = call(
        scatter_kernel,
        (local_t, grad_pre),
        [whole_block(local_t.shape), whole_block((nodes, width))],
        shape((nodes, width), f32),
        pl.BlockSpec((2 * TILE, width), lambda i: (i, 0)),
        "local_scatter",
        grid=(nodes // (2 * TILE),),
        flops=8 * nodes * nodes * width,
        moved=nodes * width * 6,
    )
    weight_rows = call(
        functools.partial(weight_sum_kernel, slots, hub_rows, rows),
        (back,),
        [VMEM],
        shape((parts, 8, width), bf16),
        VMEM,
        "weight_sums",
        moved=parts * pay * width * 2,
    )
    near_weights = exchange(weight_rows)
    grad_bias, grad_hubs = call(
        functools.partial(other_sums_kernel, scale, slots, hub_rows, rows),
        (back, w_neigh),
        [VMEM, VMEM],
        [shape((1, width), f32), shape((hub_rows, width), f32)],
        [whole_block((1, width)), whole_block((hub_rows, width))],
        "hub_sums",
        moved=parts * pay * width * 2,
    )

    height = 2 * TILE
    by_height = pl.BlockSpec((height, width), lambda i: (i, 0))
    grad_features = call(
        functools.partial(final_kernel, scale, slots),
        (send_rows, back, scattered, grad_pre, w_self, w_neigh),
        [whole_block(send_rows.shape), whole_block((parts, pay, LANES)), by_height, by_height]
        + [whole_block((width, width))] * 2,
        shape((nodes, width), f32),
        by_height,
        "return_scatter",
        grid=(nodes // height,),
        flops=2 * nodes * parts * slots * width,
        moved=nodes * width * 10,
    )
    near_weights, grad_features = lax.optimization_barrier((near_weights, grad_features))
    grad_w_self, grad_w_neigh = call(
        weights_kernel,
        [core, near_weights, sibling(near_weights)],
        [SMEM, VMEM, VMEM],
        [shape((width, width), f32)] * 2,
        [whole_block((width, width))] * 2,
        "weights",
        moved=width * width * 12,
    )
    return (activated, grad_features, grad_hubs, grad_w_self, grad_w_neigh, grad_bias.reshape(width))


def solution(mesh):
    split = P(AXES, None)
    return jax.shard_map(
        body,
        mesh=mesh,
        in_specs=(split, split, P(), P(), P(), split, split, split, split, split),
        out_specs=(split, split, split, P(), P(), P()),
        check_vma=False,
    )
```

```python
import functools

import jax
import jax.numpy as jnp
from jax import lax
from jax.experimental import pallas as pl
from jax.experimental.pallas import tpu as pltpu
from jax.sharding import PartitionSpec as P

AXES = ("row", "col")
LANES = 128
TILE = 256
MOST_VMEM = 61952 * 1024
SOME_VMEM = 44 * 1024 * 1024
MUCH_VMEM = 47 * 1024 * 1024
NT = (((1,), (1,)), ((), ()))
TN = (((0,), (0,)), ((), ()))
VMEM = pl.BlockSpec(memory_space=pltpu.VMEM)
SMEM = pl.BlockSpec(memory_space=pltpu.SMEM)
HBM = pl.BlockSpec(memory_space=pltpu.HBM)
bf16, f32 = jnp.bfloat16, jnp.float32


def params(limit):
    return pltpu.CompilerParams(vmem_limit_bytes=limit)


def cost(flops, moved):
    return pl.CostEstimate(flops=int(flops), bytes_accessed=int(moved), transcendentals=0)


def along_rows(index_row):
    count = index_row.shape[1]
    return jnp.transpose(jnp.broadcast_to(index_row, (LANES, count))).astype(jnp.int16)


def stack_rows(value, height):
    count = value.shape[1]
    return jnp.broadcast_to(value[None], (height // 16, 16, count)).reshape(height, count)


def count_hits(entries, here):
    one, zero = jnp.ones(here.shape, bf16), jnp.zeros(here.shape, bf16)
    total = None
    for entry in entries:
        hit = jnp.where(entry == here, one, zero)
        total = hit if total is None else total + hit
    return total


def hits_by_row(columns, first, width):
    rows = columns[0].shape[0]
    lane = lax.broadcasted_iota(jnp.int32, (16, LANES), 1).astype(jnp.int16)
    tiles = [
        count_hits(columns, stack_rows(lane + jnp.int16(start), rows)) for start in range(first, first + width, LANES)
    ]
    return jnp.concatenate(tiles, axis=1) if len(tiles) > 1 else tiles[0]


def hits_by_column(index_rows, first, height):
    count = index_rows[0].shape[1]
    group = 64
    down = lax.broadcasted_iota(jnp.int32, (group, count), 0).astype(jnp.int16)
    entries = [
        stack_rows(jnp.broadcast_to(row - first, (16, count)).astype(jnp.int16), group) for row in index_rows
    ]
    return jnp.concatenate(
        [count_hits(entries, down + jnp.int16(start)) for start in range(0, height, group)], axis=0
    )


def dot(a, b, dims=(((1,), (0,)), ((), ()))):
    return lax.dot_general(a, b, dims, preferred_element_type=f32)


def index_rows(ref, start, count):
    return [ref[j : j + 1, pl.ds(start, count)] for j in range(ref.shape[0])]


def by_core(value, rows, cols):
    half = value.shape[0] // 2
    value = value.astype(f32)
    halves = [value[core * half : (core + 1) * half] for core in (0, 1)]
    blocks = [jnp.broadcast_to(halves[row % 2][None], (cols,) + halves[0].shape) for row in range(rows)]
    return jnp.concatenate(blocks, axis=0).astype(bf16)


def pick_kernel(rows, send_ref, feat_ref, hub_ref, out_ref):
    parts, slab, width = out_ref.shape
    slots = slab - hub_ref.shape[0] // 2
    total = send_ref.shape[1]
    step = min(512, total)
    for start in range(0, total, step):
        column = along_rows(send_ref[:, start : start + step])
        picked = dot(hits_by_row([column], 0, feat_ref.shape[0]), feat_ref[...])
        out_ref[start // slots : (start + step) // slots, :slots, :] = (
            picked.astype(bf16).reshape(step // slots, slots, width)
        )
    out_ref[:, slots:, :] = by_core(hub_ref[...], rows, parts // rows)


def half_kernel(slots, table_ref, out_ref):
    out_ref[...] = table_ref[:, slots:, :].astype(f32).reshape(out_ref.shape).astype(bf16)


def local_kernel(split, hub_rows, core_ref, local_ref, remote_ref, hub_ref, feat_ref, own_ref, cot_ref, sum_ref, pack_ref):
    nodes, width = feat_ref.shape
    columns = [along_rows(row) for row in index_rows(local_ref, 0, TILE)]
    total = None
    for first in range(0, nodes, TILE):
        part = dot(hits_by_row(columns, first, TILE), feat_ref[first : first + TILE, :])
        total = part if total is None else total + part
    sum_ref[...] = total
    pack_ref[:, :width] = cot_ref[...]
    pack_ref[:, width : 2 * width] = own_ref[...]
    place = 2 * width
    counts = pack_ref.shape[1] - place
    half = hub_rows // 2
    hubs = []
    for hub in index_rows(hub_ref, 0, TILE):
        owner = lax.div(hub, jnp.int32(hub_rows))
        within = hub - owner * hub_rows
        other = (within >= half) != (core_ref[0] == 1)
        within = jnp.where(within >= half, within - half, within)
        hubs.append(owner * half + within + jnp.where(other, (counts - split) // 2, 0))
    for index, share in ((index_rows(remote_ref, 0, TILE), split), (hubs, counts - split)):
        columns = [along_rows(row) for row in index]
        for first in range(0, share, TILE):
            pack_ref[:, place + first : place + first + TILE] = hits_by_row(columns, first, TILE)
        place += share


def middle_kernel(
    scale,
    slots,
    core_ref,
    table_ref,
    near_ref,
    far_ref,
    ws_ref,
    wn_ref,
    bias_ref,
    sum_ref,
    pack_hbm,
    act_hbm,
    grad_hbm,
    bound_ref,
    keep_ref,
    give_ref,
    pack,
    act,
    grad_all,
    terms,
    in_sem,
    out_sem,
):
    nodes, width = sum_ref.shape
    parts, slab, _ = table_ref.shape
    half = slab - slots
    hub_rows = 2 * half
    bounds, hubs = parts * slots, parts * hub_rows
    edges = [0] + list(range(TILE, nodes, 2 * TILE)) + [nodes]
    blocks = len(edges) - 1
    features, counts = slice(width, 2 * width), 3 * width

    def here(block):
        return slice(edges[block], edges[block + 1])

    def loads(block):
        at = here(block)
        return [
            pltpu.make_async_copy(pack_hbm.at[at, : 2 * width], pack.at[at, : 2 * width], in_sem.at[0, block]),
            pltpu.make_async_copy(pack_hbm.at[at, 2 * width :], pack.at[at, counts:], in_sem.at[1, block]),
        ]

    coming = [loads(block) for block in range(blocks)]
    for group in coming:
        for copy in group:
            copy.start()
    table = jnp.concatenate(
        [table_ref[:, :slots, :].reshape(bounds, width), near_ref[...], far_ref[...]], axis=0
    )
    half_weights = jnp.concatenate([ws_ref[...], wn_ref[...]], axis=0) * jnp.bfloat16(0.5)
    half_bias = 0.5 * bias_ref[...]
    stores = []
    total = None
    turned = None
    for block in range(blocks + 2):
        following = None
        if block < blocks:
            for copy in coming[block]:
                copy.wait()
            following = sum_ref[here(block), :] + dot(pack[here(block), counts:], table)
        if block > 1:
            part = dot(turned, pack[here(block - 2), width:])
            terms[...] = part if block == 2 else terms[...] + part
        if 0 < block <= blocks:
            at = here(block - 1)
            pack[at, 2 * width : counts] = (total * scale).astype(bf16)
            arg = dot(pack[at, width:counts], half_weights) + half_bias
            tanh = jnp.tanh(arg)
            above = 1.0 + tanh
            act[at, :] = (arg * above).astype(bf16)
            slope = above * (0.5 + (0.5 * arg) * (1.0 - tanh))
            grad = (pack[at, :width].astype(f32) * slope).astype(bf16)
            grad_all[at, :] = grad
            turned = jnp.transpose(grad)
            for which, (source, target) in enumerate(((act, act_hbm), (grad_all, grad_hbm))):
                store = pltpu.make_async_copy(source.at[at, :], target.at[at, :], out_sem.at[which, block - 1])
                store.start()
                stores.append(store)
        total = following

    pieces = width // LANES
    step = 2 * width

    def term_rows(first, count, rows):
        return jnp.transpose(terms[:, first : first + count]).reshape(count // rows, rows, width)

    def lanes(piece):
        return slice(piece * LANES, (piece + 1) * LANES)

    first_core = core_ref[0] == 0
    weights = term_rows(0, step, hub_rows)
    own = jnp.where(first_core, weights[:, :half], weights[:, half:])
    other = jnp.where(first_core, weights[:, half:], weights[:, :half])
    count = step // hub_rows
    for low in range(0, parts, count):
        if low > 0:
            own = other = jnp.zeros_like(own)
        first = step + bounds + low * half
        keep = jnp.concatenate([term_rows(first, count * half, half), own], axis=1)
        give = jnp.concatenate([term_rows(first + hubs // 2, count * half, half), other], axis=1).astype(bf16)
        at = slice(low, low + count)
        for piece in range(pieces):
            there = slice(piece * hub_rows, (piece + 1) * hub_rows)
            keep_ref[at, there, :] = keep[:, :, lanes(piece)]
            give_ref[at, there, :] = give[:, :, lanes(piece)]
    bias_total = dot(jnp.ones((16, nodes), bf16), grad_all[...])[:1]
    rows = bias_rows([bias_total[:, lanes(piece)] for piece in range(pieces)])
    keep_ref[:, pieces * hub_rows :, :] = jnp.broadcast_to(rows[None], (parts, 8, LANES))
    give_ref[:, pieces * hub_rows :, :] = jnp.broadcast_to(rows.astype(bf16)[None], (parts, 8, LANES))
    for low in range(0, bounds, step):
        bound_terms = term_rows(step + low, step, slots).astype(bf16)
        for piece in range(pieces):
            bound_ref[low // slots : (low + step) // slots, piece * slots : (piece + 1) * slots, :] = (
                bound_terms[:, :, lanes(piece)]
            )
    for store in stores:
        store.wait()


def bias_rows(parts):
    line = lax.broadcasted_iota(jnp.int32, (8, LANES), 0)
    rows = jnp.zeros((8, LANES), f32)
    for piece, value in enumerate(parts):
        high = value.astype(bf16).astype(f32)
        rows = jnp.where(line == piece, high, rows)
        rows = jnp.where(line == len(parts) + piece, value - high, rows)
    return rows


def join_kernel(bound_ref, keep_ref, got_ref, out_ref):
    parts, tall, _ = keep_ref.shape
    place = bound_ref.shape[1]
    pieces = (tall - 8) // 16
    out_ref[:, :place, :] = bound_ref[...]
    both = keep_ref[:, : tall - 8, :] + got_ref[:, : tall - 8, :].astype(f32)
    out_ref[:, place : place + tall - 8, :] = both.astype(bf16)
    tail = keep_ref[0, tall - 8 :, :] + got_ref[0, tall - 8 :, :].astype(f32)
    rows = bias_rows([tail[piece : piece + 1] + tail[pieces + piece : pieces + piece + 1] for piece in range(pieces)])
    out_ref[:, place + tall - 8 :, :] = jnp.broadcast_to(rows.astype(bf16)[None], (parts, 8, LANES))


def chip_sums(slots, hub_rows, rows, back_ref):
    parts, tall, _ = back_ref.shape
    pieces = (tall - 8) // (slots + hub_rows)
    whole = back_ref[:, pieces * slots :, :].astype(f32)
    count = whole.shape[1]
    whole = whole.reshape(rows // 2, 2, parts // rows, count, LANES)
    return jnp.sum(jnp.sum(whole, axis=2), axis=0), pieces


def both_halves(total, pieces, hub_rows, first):
    half = hub_rows // 2
    columns = []
    for piece in range(pieces):
        place = piece * hub_rows + first
        columns.append(jnp.concatenate([total[0, place : place + half], total[1, place : place + half]], axis=0))
    return jnp.concatenate(columns, axis=1)


def weight_sum_kernel(slots, hub_rows, rows, back_ref, out_ref):
    total, pieces = chip_sums(slots, hub_rows, rows, back_ref)
    weight = both_halves(total, pieces, hub_rows, hub_rows // 2)
    out_ref[...] = by_core(weight.astype(bf16), rows, out_ref.shape[0] // rows)


def other_sums_kernel(scale, slots, hub_rows, rows, back_ref, wn_ref, bias_ref, hub_ref):
    total, pieces = chip_sums(slots, hub_rows, rows, back_ref)
    tail = 0.5 * (total[0, pieces * hub_rows :] + total[1, pieces * hub_rows :])
    bias_ref[...] = jnp.concatenate(
        [tail[piece : piece + 1] + tail[pieces + piece : pieces + piece + 1] for piece in range(pieces)], axis=1
    )
    hub = both_halves(total, pieces, hub_rows, 0)
    high = hub.astype(bf16)
    low = (hub - high.astype(f32)).astype(bf16)
    hub_ref[...] = (dot(high, wn_ref[...], NT) + dot(low, wn_ref[...], NT)) * scale


def weights_kernel(core_ref, near_ref, far_ref, self_ref, neigh_ref):
    width = self_ref.shape[0]
    count = 2 * width // 16
    near, far = near_ref[:count].astype(f32), far_ref[:count].astype(f32)
    first_core = core_ref[0] == 0
    whole = jnp.concatenate([jnp.where(first_core, near, far), jnp.where(first_core, far, near)], axis=1)
    whole = whole.reshape(2 * width, width)
    self_ref[...] = whole[:width]
    neigh_ref[...] = whole[width:]


def scatter_kernel(local_ref, grad_ref, out_ref):
    height = out_ref.shape[0]
    first = pl.program_id(0) * height
    total = None
    for start in range(0, grad_ref.shape[0], TILE):
        rows = index_rows(local_ref, start, TILE)
        part = dot(hits_by_column(rows, first, height), grad_ref[start : start + TILE, :])
        total = part if total is None else total + part
    out_ref[...] = total


def final_kernel(scale, slots, send_ref, back_ref, scat_ref, grad_ref, ws_ref, wn_ref, out_ref):
    height, width = out_ref.shape
    first = pl.program_id(0) * height
    count = send_ref.shape[1]
    returned = jnp.concatenate(
        [
            back_ref[:, piece * slots : (piece + 1) * slots, :].reshape(count, LANES)
            for piece in range(width // LANES)
        ],
        axis=1,
    )
    total = scat_ref[...]
    for start in range(0, count, 512):
        stop = min(count, start + 512)
        hits = hits_by_column([send_ref[:, start:stop]], first, height)
        total = total + dot(hits, returned[start:stop])
    out_ref[...] = dot(grad_ref[...], ws_ref[...], NT) + dot((total * scale).astype(bf16), wn_ref[...], NT)


def call(
    kernel, ins, in_specs, outs, out_specs, name, grid=(), scratch=(), flops=0, moved=0, limit=SOME_VMEM
):
    return pl.pallas_call(
        kernel,
        grid=grid,
        in_specs=in_specs,
        out_specs=out_specs,
        out_shape=outs,
        scratch_shapes=scratch,
        compiler_params=params(limit),
        cost_estimate=cost(flops, moved),
        name=name,
    )(*ins)


def whole_block(shape):
    return pl.BlockSpec(shape, lambda *_: (0,) * len(shape))


def body(
    features,
    hub_features,
    w_self,
    w_neigh,
    out_bias,
    local_edges,
    hub_edges,
    remote_edges,
    send_rows,
    cotangent,
):
    nodes, width = features.shape
    hub_rows = hub_features.shape[0]
    parts = lax.axis_size(AXES)
    slots = send_rows.shape[1] // parts
    slab = slots + hub_rows
    pieces = width // LANES
    pay = pieces * slab + 8
    core = (lax.axis_index("row") % 2).astype(jnp.int32).reshape(1)
    rows = lax.axis_size("row")
    half = hub_rows // 2
    table = parts * slab
    scale = 1.0 / (local_edges.shape[1] + hub_edges.shape[1] + remote_edges.shape[1])
    local_t, hub_t, remote_t = local_edges.T, hub_edges.T, remote_edges.T
    bias = out_bias.reshape(1, width)
    shape = jax.ShapeDtypeStruct

    def sibling(value):
        return lax.ppermute(value, "row", [(r, r ^ 1) for r in range(rows)])

    def exchange(value):
        return lax.all_to_all(value, AXES, split_axis=0, concat_axis=0, tiled=True)

    sending = call(
        functools.partial(pick_kernel, rows),
        (send_rows, features, hub_features),
        [VMEM, VMEM, VMEM],
        shape((parts, slots + half, width), bf16),
        whole_block((parts, slots + half, width)),
        "pick_rows",
        limit=MOST_VMEM,
        flops=2 * parts * slots * nodes * width,
        moved=nodes * width * 2,
    )
    sending, features = lax.optimization_barrier((sending, features))
    received = exchange(sending)

    block = TILE
    by_block = pl.BlockSpec((block, width), lambda i: (i, 0))
    packed = 2 * width + table
    local_sum, pack = call(
        functools.partial(local_kernel, parts * slots, hub_rows),
        (core, local_t, remote_t, hub_t, features, features, cotangent),
        [SMEM]
        + [pl.BlockSpec((edges.shape[0], block), lambda i: (0, i)) for edges in (local_t, remote_t, hub_t)]
        + [whole_block((nodes, width)), by_block, by_block],
        [shape((nodes, width), f32), pltpu.HBM((nodes, packed), bf16)],
        [by_block, pl.BlockSpec((block, packed), lambda i: (i, 0))],
        "local_gather",
        grid=(nodes // block,),
        flops=8 * nodes * nodes * width,
        moved=nodes * packed * 2,
    )

    received, local_sum, pack = lax.optimization_barrier((received, local_sum, pack))
    near_hubs = call(
        functools.partial(half_kernel, slots),
        [received],
        [VMEM],
        shape((parts * half, width), bf16),
        VMEM,
        "take_hubs",
        moved=parts * half * width * 4,
    )
    far_hubs = sibling(near_hubs)

    activated, grad_pre, bound_terms, keep, give = call(
        functools.partial(middle_kernel, scale, slots),
        [core, received, near_hubs, far_hubs, w_self, w_neigh, bias, local_sum, pack],
        [SMEM] + [VMEM] * 7 + [HBM],
        [pltpu.HBM((nodes, width), bf16)] * 2
        + [
            shape((parts, pieces * slots, LANES), bf16),
            shape((parts, pieces * hub_rows + 8, LANES), f32),
            shape((parts, pieces * hub_rows + 8, LANES), bf16),
        ],
        [HBM] * 2 + [VMEM] * 3,
        "activate",
        limit=MUCH_VMEM,
        scratch=[
            pltpu.VMEM((nodes, packed + width), bf16),
            pltpu.VMEM((nodes, width), bf16),
            pltpu.VMEM((nodes, width), bf16),
            pltpu.VMEM((width, 2 * width + table), f32),
            pltpu.SemaphoreType.DMA((2, nodes // (2 * TILE) + 1)),
            pltpu.SemaphoreType.DMA((2, nodes // (2 * TILE) + 1)),
        ],
        flops=4 * nodes * table * width,
        moved=nodes * packed * 2,
    )
    got = sibling(give)
    back = exchange(
        call(
            join_kernel,
            [bound_terms, keep, got],
            [VMEM] * 3,
            shape((parts, pay, LANES), bf16),
            VMEM,
            "join_siblings",
            moved=parts * pay * LANES * 6,
        )
    )

    scattered = call(
        scatter_kernel,
        (local_t, grad_pre),
        [whole_block(local_t.shape), whole_block((nodes, width))],
        shape((nodes, width), f32),
        pl.BlockSpec((2 * TILE, width), lambda i: (i, 0)),
        "local_scatter",
        grid=(nodes // (2 * TILE),),
        flops=8 * nodes * nodes * width,
        moved=nodes * width * 6,
    )
    weight_rows = call(
        functools.partial(weight_sum_kernel, slots, hub_rows, rows),
        (back,),
        [VMEM],
        shape((parts, 8, width), bf16),
        VMEM,
        "weight_sums",
        moved=parts * pay * width * 2,
    )
    near_weights = exchange(weight_rows)
    grad_bias, grad_hubs = call(
        functools.partial(other_sums_kernel, scale, slots, hub_rows, rows),
        (back, w_neigh),
        [VMEM, VMEM],
        [shape((1, width), f32), shape((hub_rows, width), f32)],
        [whole_block((1, width)), whole_block((hub_rows, width))],
        "hub_sums",
        moved=parts * pay * width * 2,
    )

    height = 2 * TILE
    by_height = pl.BlockSpec((height, width), lambda i: (i, 0))
    grad_features = call(
        functools.partial(final_kernel, scale, slots),
        (send_rows, back, scattered, grad_pre, w_self, w_neigh),
        [whole_block(send_rows.shape), whole_block((parts, pay, LANES)), by_height, by_height]
        + [whole_block((width, width))] * 2,
        shape((nodes, width), f32),
        by_height,
        "return_scatter",
        grid=(nodes // height,),
        flops=2 * nodes * parts * slots * width,
        moved=nodes * width * 10,
    )
    near_weights, grad_features = lax.optimization_barrier((near_weights, grad_features))
    grad_w_self, grad_w_neigh = call(
        weights_kernel,
        [core, near_weights, sibling(near_weights)],
        [SMEM, VMEM, VMEM],
        [shape((width, width), f32)] * 2,
        [whole_block((width, width))] * 2,
        "weights",
        moved=width * width * 12,
    )
    return (activated, grad_features, grad_hubs, grad_w_self, grad_w_neigh, grad_bias.reshape(width))


def solution(mesh):
    split = P(AXES, None)
    return jax.shard_map(
        body,
        mesh=mesh,
        in_specs=(split, split, P(), P(), P(), split, split, split, split, split),
        out_specs=(split, split, split, P(), P(), P()),
        check_vma=False,
    )
```

```python
import functools

import jax
import jax.numpy as jnp
from jax import lax
from jax.experimental import pallas as pl
from jax.experimental.pallas import tpu as pltpu
from jax.sharding import PartitionSpec as P

AXES = ("row", "col")
LANES = 128
TILE = 256
MOST_VMEM = 61952 * 1024
SOME_VMEM = 44 * 1024 * 1024
MUCH_VMEM = 47 * 1024 * 1024
NT = (((1,), (1,)), ((), ()))
TN = (((0,), (0,)), ((), ()))
VMEM = pl.BlockSpec(memory_space=pltpu.VMEM)
SMEM = pl.BlockSpec(memory_space=pltpu.SMEM)
HBM = pl.BlockSpec(memory_space=pltpu.HBM)
bf16, f32 = jnp.bfloat16, jnp.float32


def params(limit):
    return pltpu.CompilerParams(vmem_limit_bytes=limit)


def cost(flops, moved):
    return pl.CostEstimate(flops=int(flops), bytes_accessed=int(moved), transcendentals=0)


def along_rows(index_row):
    count = index_row.shape[1]
    return jnp.transpose(jnp.broadcast_to(index_row, (LANES, count))).astype(jnp.int16)


def stack_rows(value, height):
    count = value.shape[1]
    return jnp.broadcast_to(value[None], (height // 16, 16, count)).reshape(height, count)


def count_hits(entries, here):
    one, zero = jnp.ones(here.shape, bf16), jnp.zeros(here.shape, bf16)
    total = None
    for entry in entries:
        hit = jnp.where(entry == here, one, zero)
        total = hit if total is None else total + hit
    return total


def hits_by_row(columns, first, width):
    rows = columns[0].shape[0]
    lane = lax.broadcasted_iota(jnp.int32, (16, LANES), 1).astype(jnp.int16)
    tiles = [
        count_hits(columns, stack_rows(lane + jnp.int16(start), rows)) for start in range(first, first + width, LANES)
    ]
    return jnp.concatenate(tiles, axis=1) if len(tiles) > 1 else tiles[0]


def hits_by_column(index_rows, first, height):
    count = index_rows[0].shape[1]
    group = 64
    down = lax.broadcasted_iota(jnp.int32, (group, count), 0).astype(jnp.int16)
    entries = [
        stack_rows(jnp.broadcast_to(row - first, (16, count)).astype(jnp.int16), group) for row in index_rows
    ]
    return jnp.concatenate(
        [count_hits(entries, down + jnp.int16(start)) for start in range(0, height, group)], axis=0
    )


def dot(a, b, dims=(((1,), (0,)), ((), ()))):
    return lax.dot_general(a, b, dims, preferred_element_type=f32)


def index_rows(ref, start, count):
    return [ref[j : j + 1, pl.ds(start, count)] for j in range(ref.shape[0])]


def by_core(value, rows, cols):
    half = value.shape[0] // 2
    value = value.astype(f32)
    halves = [value[core * half : (core + 1) * half] for core in (0, 1)]
    blocks = [jnp.broadcast_to(halves[row % 2][None], (cols,) + halves[0].shape) for row in range(rows)]
    return jnp.concatenate(blocks, axis=0).astype(bf16)


def pick_kernel(rows, send_ref, feat_ref, hub_ref, out_ref):
    parts, slab, width = out_ref.shape
    slots = slab - hub_ref.shape[0] // 2
    total = send_ref.shape[1]
    step = min(512, total)
    for start in range(0, total, step):
        column = along_rows(send_ref[:, start : start + step])
        picked = dot(hits_by_row([column], 0, feat_ref.shape[0]), feat_ref[...])
        out_ref[start // slots : (start + step) // slots, :slots, :] = (
            picked.astype(bf16).reshape(step // slots, slots, width)
        )
    out_ref[:, slots:, :] = by_core(hub_ref[...], rows, parts // rows)


def half_kernel(slots, table_ref, out_ref):
    out_ref[...] = table_ref[:, slots:, :].astype(f32).reshape(out_ref.shape).astype(bf16)


def local_kernel(split, hub_rows, core_ref, local_ref, remote_ref, hub_ref, feat_ref, own_ref, cot_ref, sum_ref, pack_ref):
    nodes, width = feat_ref.shape
    columns = [along_rows(row) for row in index_rows(local_ref, 0, TILE)]
    total = None
    for first in range(0, nodes, TILE):
        part = dot(hits_by_row(columns, first, TILE), feat_ref[first : first + TILE, :])
        total = part if total is None else total + part
    sum_ref[...] = total
    pack_ref[:, :width] = cot_ref[...]
    pack_ref[:, width : 2 * width] = own_ref[...]
    place = 2 * width
    counts = pack_ref.shape[1] - place
    half = hub_rows // 2
    hubs = []
    for hub in index_rows(hub_ref, 0, TILE):
        owner = lax.div(hub, jnp.int32(hub_rows))
        within = hub - owner * hub_rows
        other = (within >= half) != (core_ref[0] == 1)
        within = jnp.where(within >= half, within - half, within)
        hubs.append(owner * half + within + jnp.where(other, (counts - split) // 2, 0))
    for index, share in ((index_rows(remote_ref, 0, TILE), split), (hubs, counts - split)):
        columns = [along_rows(row) for row in index]
        for first in range(0, share, TILE):
            pack_ref[:, place + first : place + first + TILE] = hits_by_row(columns, first, TILE)
        place += share


def middle_kernel(
    scale,
    slots,
    core_ref,
    table_ref,
    near_ref,
    far_ref,
    ws_ref,
    wn_ref,
    bias_ref,
    sum_ref,
    pack_hbm,
    act_hbm,
    grad_hbm,
    bound_ref,
    keep_ref,
    give_ref,
    pack,
    act,
    grad_all,
    terms,
    in_sem,
    out_sem,
):
    nodes, width = sum_ref.shape
    parts, slab, _ = table_ref.shape
    half = slab - slots
    hub_rows = 2 * half
    bounds, hubs = parts * slots, parts * hub_rows
    edges = [0, nodes // 4, nodes * 5 // 8, nodes]
    blocks = len(edges) - 1
    features, counts = slice(width, 2 * width), 3 * width

    def here(block):
        return slice(edges[block], edges[block + 1])

    def loads(block):
        at = here(block)
        return [
            pltpu.make_async_copy(pack_hbm.at[at, : 2 * width], pack.at[at, : 2 * width], in_sem.at[0, block]),
            pltpu.make_async_copy(pack_hbm.at[at, 2 * width :], pack.at[at, counts:], in_sem.at[1, block]),
        ]

    coming = [loads(block) for block in range(blocks)]
    for group in coming:
        for copy in group:
            copy.start()
    table = jnp.concatenate(
        [table_ref[:, :slots, :].reshape(bounds, width), near_ref[...], far_ref[...]], axis=0
    )
    half_weights = jnp.concatenate([ws_ref[...], wn_ref[...]], axis=0) * jnp.bfloat16(0.5)
    half_bias = 0.5 * bias_ref[...]
    stores = []
    total = None
    turned = None
    for block in range(blocks + 2):
        following = None
        if block < blocks:
            for copy in coming[block]:
                copy.wait()
            following = sum_ref[here(block), :] + dot(pack[here(block), counts:], table)
        if block > 1:
            part = dot(turned, pack[here(block - 2), width:])
            terms[...] = part if block == 2 else terms[...] + part
        if 0 < block <= blocks:
            at = here(block - 1)
            pack[at, 2 * width : counts] = (total * scale).astype(bf16)
            arg = dot(pack[at, width:counts], half_weights) + half_bias
            tanh = jnp.tanh(arg)
            above = 1.0 + tanh
            act[at, :] = (arg * above).astype(bf16)
            slope = above * (0.5 + (0.5 * arg) * (1.0 - tanh))
            grad = (pack[at, :width].astype(f32) * slope).astype(bf16)
            grad_all[at, :] = grad
            turned = jnp.transpose(grad)
            for which, (source, target) in enumerate(((act, act_hbm), (grad_all, grad_hbm))):
                store = pltpu.make_async_copy(source.at[at, :], target.at[at, :], out_sem.at[which, block - 1])
                store.start()
                stores.append(store)
        total = following

    pieces = width // LANES
    step = 2 * width

    def term_rows(first, count, rows):
        return jnp.transpose(terms[:, first : first + count]).reshape(count // rows, rows, width)

    def lanes(piece):
        return slice(piece * LANES, (piece + 1) * LANES)

    first_core = core_ref[0] == 0
    weights = term_rows(0, step, hub_rows)
    own = jnp.where(first_core, weights[:, :half], weights[:, half:])
    other = jnp.where(first_core, weights[:, half:], weights[:, :half])
    count = step // hub_rows
    for low in range(0, parts, count):
        if low > 0:
            own = other = jnp.zeros_like(own)
        first = step + bounds + low * half
        keep = jnp.concatenate([term_rows(first, count * half, half), own], axis=1)
        give = jnp.concatenate([term_rows(first + hubs // 2, count * half, half), other], axis=1).astype(bf16)
        at = slice(low, low + count)
        for piece in range(pieces):
            there = slice(piece * hub_rows, (piece + 1) * hub_rows)
            keep_ref[at, there, :] = keep[:, :, lanes(piece)]
            give_ref[at, there, :] = give[:, :, lanes(piece)]
    bias_total = dot(jnp.ones((16, nodes), bf16), grad_all[...])[:1]
    rows = bias_rows([bias_total[:, lanes(piece)] for piece in range(pieces)])
    keep_ref[:, pieces * hub_rows :, :] = jnp.broadcast_to(rows[None], (parts, 8, LANES))
    give_ref[:, pieces * hub_rows :, :] = jnp.broadcast_to(rows.astype(bf16)[None], (parts, 8, LANES))
    for low in range(0, bounds, step):
        bound_terms = term_rows(step + low, step, slots).astype(bf16)
        for piece in range(pieces):
            bound_ref[low // slots : (low + step) // slots, piece * slots : (piece + 1) * slots, :] = (
                bound_terms[:, :, lanes(piece)]
            )
    for store in stores:
        store.wait()


def bias_rows(parts):
    line = lax.broadcasted_iota(jnp.int32, (8, LANES), 0)
    rows = jnp.zeros((8, LANES), f32)
    for piece, value in enumerate(parts):
        high = value.astype(bf16).astype(f32)
        rows = jnp.where(line == piece, high, rows)
        rows = jnp.where(line == len(parts) + piece, value - high, rows)
    return rows


def join_kernel(bound_ref, keep_ref, got_ref, out_ref):
    parts, tall, _ = keep_ref.shape
    place = bound_ref.shape[1]
    pieces = (tall - 8) // 16
    out_ref[:, :place, :] = bound_ref[...]
    both = keep_ref[:, : tall - 8, :] + got_ref[:, : tall - 8, :].astype(f32)
    out_ref[:, place : place + tall - 8, :] = both.astype(bf16)
    tail = keep_ref[0, tall - 8 :, :] + got_ref[0, tall - 8 :, :].astype(f32)
    rows = bias_rows([tail[piece : piece + 1] + tail[pieces + piece : pieces + piece + 1] for piece in range(pieces)])
    out_ref[:, place + tall - 8 :, :] = jnp.broadcast_to(rows.astype(bf16)[None], (parts, 8, LANES))


def chip_sums(slots, hub_rows, rows, back_ref):
    parts, tall, _ = back_ref.shape
    pieces = (tall - 8) // (slots + hub_rows)
    whole = back_ref[:, pieces * slots :, :].astype(f32)
    count = whole.shape[1]
    whole = whole.reshape(rows // 2, 2, parts // rows, count, LANES)
    return jnp.sum(jnp.sum(whole, axis=2), axis=0), pieces


def both_halves(total, pieces, hub_rows, first):
    half = hub_rows // 2
    columns = []
    for piece in range(pieces):
        place = piece * hub_rows + first
        columns.append(jnp.concatenate([total[0, place : place + half], total[1, place : place + half]], axis=0))
    return jnp.concatenate(columns, axis=1)


def weight_sum_kernel(slots, hub_rows, rows, back_ref, out_ref):
    total, pieces = chip_sums(slots, hub_rows, rows, back_ref)
    weight = both_halves(total, pieces, hub_rows, hub_rows // 2)
    out_ref[...] = by_core(weight.astype(bf16), rows, out_ref.shape[0] // rows)


def other_sums_kernel(scale, slots, hub_rows, rows, back_ref, wn_ref, bias_ref, hub_ref):
    total, pieces = chip_sums(slots, hub_rows, rows, back_ref)
    tail = 0.5 * (total[0, pieces * hub_rows :] + total[1, pieces * hub_rows :])
    bias_ref[...] = jnp.concatenate(
        [tail[piece : piece + 1] + tail[pieces + piece : pieces + piece + 1] for piece in range(pieces)], axis=1
    )
    hub = both_halves(total, pieces, hub_rows, 0)
    high = hub.astype(bf16)
    low = (hub - high.astype(f32)).astype(bf16)
    hub_ref[...] = (dot(high, wn_ref[...], NT) + dot(low, wn_ref[...], NT)) * scale


def weights_kernel(core_ref, near_ref, far_ref, self_ref, neigh_ref):
    width = self_ref.shape[0]
    count = 2 * width // 16
    near, far = near_ref[:count].astype(f32), far_ref[:count].astype(f32)
    first_core = core_ref[0] == 0
    whole = jnp.concatenate([jnp.where(first_core, near, far), jnp.where(first_core, far, near)], axis=1)
    whole = whole.reshape(2 * width, width)
    self_ref[...] = whole[:width]
    neigh_ref[...] = whole[width:]


def scatter_kernel(local_ref, grad_ref, out_ref):
    height = out_ref.shape[0]
    first = pl.program_id(0) * height
    total = None
    for start in range(0, grad_ref.shape[0], TILE):
        rows = index_rows(local_ref, start, TILE)
        part = dot(hits_by_column(rows, first, height), grad_ref[start : start + TILE, :])
        total = part if total is None else total + part
    out_ref[...] = total


def final_kernel(scale, slots, send_ref, back_ref, scat_ref, grad_ref, ws_ref, wn_ref, out_ref):
    height, width = out_ref.shape
    first = pl.program_id(0) * height
    count = send_ref.shape[1]
    returned = jnp.concatenate(
        [
            back_ref[:, piece * slots : (piece + 1) * slots, :].reshape(count, LANES)
            for piece in range(width // LANES)
        ],
        axis=1,
    )
    total = scat_ref[...]
    for start in range(0, count, 512):
        stop = min(count, start + 512)
        hits = hits_by_column([send_ref[:, start:stop]], first, height)
        total = total + dot(hits, returned[start:stop])
    out_ref[...] = dot(grad_ref[...], ws_ref[...], NT) + dot((total * scale).astype(bf16), wn_ref[...], NT)


def call(
    kernel, ins, in_specs, outs, out_specs, name, grid=(), scratch=(), flops=0, moved=0, limit=SOME_VMEM
):
    return pl.pallas_call(
        kernel,
        grid=grid,
        in_specs=in_specs,
        out_specs=out_specs,
        out_shape=outs,
        scratch_shapes=scratch,
        compiler_params=params(limit),
        cost_estimate=cost(flops, moved),
        name=name,
    )(*ins)


def whole_block(shape):
    return pl.BlockSpec(shape, lambda *_: (0,) * len(shape))


def body(
    features,
    hub_features,
    w_self,
    w_neigh,
    out_bias,
    local_edges,
    hub_edges,
    remote_edges,
    send_rows,
    cotangent,
):
    nodes, width = features.shape
    hub_rows = hub_features.shape[0]
    parts = lax.axis_size(AXES)
    slots = send_rows.shape[1] // parts
    slab = slots + hub_rows
    pieces = width // LANES
    pay = pieces * slab + 8
    core = (lax.axis_index("row") % 2).astype(jnp.int32).reshape(1)
    rows = lax.axis_size("row")
    half = hub_rows // 2
    table = parts * slab
    scale = 1.0 / (local_edges.shape[1] + hub_edges.shape[1] + remote_edges.shape[1])
    local_t, hub_t, remote_t = local_edges.T, hub_edges.T, remote_edges.T
    bias = out_bias.reshape(1, width)
    shape = jax.ShapeDtypeStruct

    def sibling(value):
        return lax.ppermute(value, "row", [(r, r ^ 1) for r in range(rows)])

    def exchange(value):
        return lax.all_to_all(value, AXES, split_axis=0, concat_axis=0, tiled=True)

    sending = call(
        functools.partial(pick_kernel, rows),
        (send_rows, features, hub_features),
        [VMEM, VMEM, VMEM],
        shape((parts, slots + half, width), bf16),
        whole_block((parts, slots + half, width)),
        "pick_rows",
        limit=MOST_VMEM,
        flops=2 * parts * slots * nodes * width,
        moved=nodes * width * 2,
    )
    sending, features = lax.optimization_barrier((sending, features))
    received = exchange(sending)

    block = TILE
    by_block = pl.BlockSpec((block, width), lambda i: (i, 0))
    packed = 2 * width + table
    local_sum, pack = call(
        functools.partial(local_kernel, parts * slots, hub_rows),
        (core, local_t, remote_t, hub_t, features, features, cotangent),
        [SMEM]
        + [pl.BlockSpec((edges.shape[0], block), lambda i: (0, i)) for edges in (local_t, remote_t, hub_t)]
        + [whole_block((nodes, width)), by_block, by_block],
        [shape((nodes, width), f32), pltpu.HBM((nodes, packed), bf16)],
        [by_block, pl.BlockSpec((block, packed), lambda i: (i, 0))],
        "local_gather",
        grid=(nodes // block,),
        flops=8 * nodes * nodes * width,
        moved=nodes * packed * 2,
    )

    received, local_sum, pack = lax.optimization_barrier((received, local_sum, pack))
    near_hubs = call(
        functools.partial(half_kernel, slots),
        [received],
        [VMEM],
        shape((parts * half, width), bf16),
        VMEM,
        "take_hubs",
        moved=parts * half * width * 4,
    )
    far_hubs = sibling(near_hubs)

    activated, grad_pre, bound_terms, keep, give = call(
        functools.partial(middle_kernel, scale, slots),
        [core, received, near_hubs, far_hubs, w_self, w_neigh, bias, local_sum, pack],
        [SMEM] + [VMEM] * 7 + [HBM],
        [pltpu.HBM((nodes, width), bf16)] * 2
        + [
            shape((parts, pieces * slots, LANES), bf16),
            shape((parts, pieces * hub_rows + 8, LANES), f32),
            shape((parts, pieces * hub_rows + 8, LANES), bf16),
        ],
        [HBM] * 2 + [VMEM] * 3,
        "activate",
        limit=MUCH_VMEM,
        scratch=[
            pltpu.VMEM((nodes, packed + width), bf16),
            pltpu.VMEM((nodes, width), bf16),
            pltpu.VMEM((nodes, width), bf16),
            pltpu.VMEM((width, 2 * width + table), f32),
            pltpu.SemaphoreType.DMA((2, 3)),
            pltpu.SemaphoreType.DMA((2, 3)),
        ],
        flops=4 * nodes * table * width,
        moved=nodes * packed * 2,
    )
    got = sibling(give)
    back = exchange(
        call(
            join_kernel,
            [bound_terms, keep, got],
            [VMEM] * 3,
            shape((parts, pay, LANES), bf16),
            VMEM,
            "join_siblings",
            moved=parts * pay * LANES * 6,
        )
    )

    scattered = call(
        scatter_kernel,
        (local_t, grad_pre),
        [whole_block(local_t.shape), whole_block((nodes, width))],
        shape((nodes, width), f32),
        pl.BlockSpec((2 * TILE, width), lambda i: (i, 0)),
        "local_scatter",
        grid=(nodes // (2 * TILE),),
        flops=8 * nodes * nodes * width,
        moved=nodes * width * 6,
    )
    weight_rows = call(
        functools.partial(weight_sum_kernel, slots, hub_rows, rows),
        (back,),
        [VMEM],
        shape((parts, 8, width), bf16),
        VMEM,
        "weight_sums",
        moved=parts * pay * width * 2,
    )
    near_weights = exchange(weight_rows)
    grad_bias, grad_hubs = call(
        functools.partial(other_sums_kernel, scale, slots, hub_rows, rows),
        (back, w_neigh),
        [VMEM, VMEM],
        [shape((1, width), f32), shape((hub_rows, width), f32)],
        [whole_block((1, width)), whole_block((hub_rows, width))],
        "hub_sums",
        moved=parts * pay * width * 2,
    )

    height = 2 * TILE
    by_height = pl.BlockSpec((height, width), lambda i: (i, 0))
    grad_features = call(
        functools.partial(final_kernel, scale, slots),
        (send_rows, back, scattered, grad_pre, w_self, w_neigh),
        [whole_block(send_rows.shape), whole_block((parts, pay, LANES)), by_height, by_height]
        + [whole_block((width, width))] * 2,
        shape((nodes, width), f32),
        by_height,
        "return_scatter",
        grid=(nodes // height,),
        flops=2 * nodes * parts * slots * width,
        moved=nodes * width * 10,
    )
    near_weights, grad_features = lax.optimization_barrier((near_weights, grad_features))
    grad_w_self, grad_w_neigh = call(
        weights_kernel,
        [core, near_weights, sibling(near_weights)],
        [SMEM, VMEM, VMEM],
        [shape((width, width), f32)] * 2,
        [whole_block((width, width))] * 2,
        "weights",
        moved=width * width * 12,
    )
    return (activated, grad_features, grad_hubs, grad_w_self, grad_w_neigh, grad_bias.reshape(width))


def solution(mesh):
    split = P(AXES, None)
    return jax.shard_map(
        body,
        mesh=mesh,
        in_specs=(split, split, P(), P(), P(), split, split, split, split, split),
        out_specs=(split, split, split, P(), P(), P()),
        check_vma=False,
    )
```

```python
import functools

import jax
import jax.numpy as jnp
from jax import lax
from jax.experimental import pallas as pl
from jax.experimental.pallas import tpu as pltpu
from jax.sharding import PartitionSpec as P

AXES = ("row", "col")
LANES = 128
TILE = 256
MOST_VMEM = 61952 * 1024
SOME_VMEM = 44 * 1024 * 1024
MUCH_VMEM = 47 * 1024 * 1024
NT = (((1,), (1,)), ((), ()))
TN = (((0,), (0,)), ((), ()))
VMEM = pl.BlockSpec(memory_space=pltpu.VMEM)
SMEM = pl.BlockSpec(memory_space=pltpu.SMEM)
HBM = pl.BlockSpec(memory_space=pltpu.HBM)
bf16, f32 = jnp.bfloat16, jnp.float32


def params(limit):
    return pltpu.CompilerParams(vmem_limit_bytes=limit)


def cost(flops, moved):
    return pl.CostEstimate(flops=int(flops), bytes_accessed=int(moved), transcendentals=0)


def along_rows(index_row):
    count = index_row.shape[1]
    return jnp.transpose(jnp.broadcast_to(index_row, (LANES, count))).astype(jnp.int16)


def stack_rows(value, height):
    count = value.shape[1]
    return jnp.broadcast_to(value[None], (height // 16, 16, count)).reshape(height, count)


def count_hits(entries, here):
    one, zero = jnp.ones(here.shape, bf16), jnp.zeros(here.shape, bf16)
    total = None
    for entry in entries:
        hit = jnp.where(entry == here, one, zero)
        total = hit if total is None else total + hit
    return total


def hits_by_row(columns, first, width):
    rows = columns[0].shape[0]
    lane = lax.broadcasted_iota(jnp.int32, (16, LANES), 1).astype(jnp.int16)
    tiles = [
        count_hits(columns, stack_rows(lane + jnp.int16(start), rows)) for start in range(first, first + width, LANES)
    ]
    return jnp.concatenate(tiles, axis=1) if len(tiles) > 1 else tiles[0]


def hits_by_column(index_rows, first, height):
    count = index_rows[0].shape[1]
    group = 64
    down = lax.broadcasted_iota(jnp.int32, (group, count), 0).astype(jnp.int16)
    entries = [
        stack_rows(jnp.broadcast_to(row - first, (16, count)).astype(jnp.int16), group) for row in index_rows
    ]
    return jnp.concatenate(
        [count_hits(entries, down + jnp.int16(start)) for start in range(0, height, group)], axis=0
    )


def dot(a, b, dims=(((1,), (0,)), ((), ()))):
    return lax.dot_general(a, b, dims, preferred_element_type=f32)


def index_rows(ref, start, count):
    return [ref[j : j + 1, pl.ds(start, count)] for j in range(ref.shape[0])]


def by_core(value, rows, cols):
    half = value.shape[0] // 2
    value = value.astype(f32)
    halves = [value[core * half : (core + 1) * half] for core in (0, 1)]
    blocks = [jnp.broadcast_to(halves[row % 2][None], (cols,) + halves[0].shape) for row in range(rows)]
    return jnp.concatenate(blocks, axis=0).astype(bf16)


def pick_kernel(rows, send_ref, feat_ref, hub_ref, out_ref):
    parts, slab, width = out_ref.shape
    slots = slab - hub_ref.shape[0] // 2
    total = send_ref.shape[1]
    step = min(512, total)
    for start in range(0, total, step):
        column = along_rows(send_ref[:, start : start + step])
        picked = dot(hits_by_row([column], 0, feat_ref.shape[0]), feat_ref[...])
        out_ref[start // slots : (start + step) // slots, :slots, :] = (
            picked.astype(bf16).reshape(step // slots, slots, width)
        )
    out_ref[:, slots:, :] = by_core(hub_ref[...], rows, parts // rows)


def half_kernel(slots, table_ref, out_ref):
    out_ref[...] = table_ref[:, slots:, :].astype(f32).reshape(out_ref.shape).astype(bf16)


def local_kernel(split, hub_rows, core_ref, local_ref, remote_ref, hub_ref, feat_ref, own_ref, cot_ref, sum_ref, pack_ref):
    nodes, width = feat_ref.shape
    columns = [along_rows(row) for row in index_rows(local_ref, 0, TILE)]
    total = None
    for first in range(0, nodes, TILE):
        part = dot(hits_by_row(columns, first, TILE), feat_ref[first : first + TILE, :])
        total = part if total is None else total + part
    sum_ref[...] = total
    pack_ref[:, :width] = cot_ref[...]
    pack_ref[:, width : 2 * width] = own_ref[...]
    place = 2 * width
    counts = pack_ref.shape[1] - place
    half = hub_rows // 2
    hubs = []
    for hub in index_rows(hub_ref, 0, TILE):
        owner = lax.div(hub, jnp.int32(hub_rows))
        within = hub - owner * hub_rows
        other = (within >= half) != (core_ref[0] == 1)
        within = jnp.where(within >= half, within - half, within)
        hubs.append(owner * half + within + jnp.where(other, (counts - split) // 2, 0))
    for index, share in ((index_rows(remote_ref, 0, TILE), split), (hubs, counts - split)):
        columns = [along_rows(row) for row in index]
        for first in range(0, share, TILE):
            pack_ref[:, place + first : place + first + TILE] = hits_by_row(columns, first, TILE)
        place += share


def middle_kernel(
    scale,
    slots,
    core_ref,
    table_ref,
    near_ref,
    far_ref,
    ws_ref,
    wn_ref,
    bias_ref,
    sum_ref,
    pack_hbm,
    act_hbm,
    grad_hbm,
    bound_ref,
    keep_ref,
    give_ref,
    pack,
    act,
    grad_all,
    terms,
    in_sem,
    out_sem,
):
    nodes, width = sum_ref.shape
    parts, slab, _ = table_ref.shape
    half = slab - slots
    hub_rows = 2 * half
    bounds, hubs = parts * slots, parts * hub_rows
    size = 2 * TILE
    blocks = nodes // size
    features, counts = slice(width, 2 * width), 3 * width

    def here(block):
        return slice(block * size, (block + 1) * size)

    def loads(block):
        at = here(block)
        return [
            pltpu.make_async_copy(pack_hbm.at[at, : 2 * width], pack.at[at, : 2 * width], in_sem.at[0, block]),
            pltpu.make_async_copy(pack_hbm.at[at, 2 * width :], pack.at[at, counts:], in_sem.at[1, block]),
        ]

    coming = [loads(block) for block in range(blocks)]
    for group in coming:
        for copy in group:
            copy.start()
    table = jnp.concatenate(
        [table_ref[:, :slots, :].reshape(bounds, width), near_ref[...], far_ref[...]], axis=0
    )
    half_weights = jnp.concatenate([ws_ref[...], wn_ref[...]], axis=0) * jnp.bfloat16(0.5)
    half_bias = 0.5 * bias_ref[...]
    stores = []
    total = None
    turned = None
    for block in range(blocks + 2):
        following = None
        if block < blocks:
            for copy in coming[block]:
                copy.wait()
            following = sum_ref[here(block), :] + dot(pack[here(block), counts:], table)
        if block > 1:
            part = dot(turned, pack[here(block - 2), width:])
            terms[...] = part if block == 2 else terms[...] + part
        if 0 < block <= blocks:
            at = here(block - 1)
            pack[at, 2 * width : counts] = (total * scale).astype(bf16)
            arg = dot(pack[at, width:counts], half_weights) + half_bias
            tanh = jnp.tanh(arg)
            above = 1.0 + tanh
            act[at, :] = (arg * above).astype(bf16)
            slope = above * (0.5 + (0.5 * arg) * (1.0 - tanh))
            grad = (pack[at, :width].astype(f32) * slope).astype(bf16)
            grad_all[at, :] = grad
            turned = jnp.transpose(grad)
            for which, (source, target) in enumerate(((act, act_hbm), (grad_all, grad_hbm))):
                store = pltpu.make_async_copy(source.at[at, :], target.at[at, :], out_sem.at[which, block - 1])
                store.start()
                stores.append(store)
        total = following

    pieces = width // LANES
    step = 2 * width

    def term_rows(first, count, rows):
        return jnp.transpose(terms[:, first : first + count]).reshape(count // rows, rows, width)

    def lanes(piece):
        return slice(piece * LANES, (piece + 1) * LANES)

    first_core = core_ref[0] == 0
    weights = term_rows(0, step, hub_rows)
    own = jnp.where(first_core, weights[:, :half], weights[:, half:])
    other = jnp.where(first_core, weights[:, half:], weights[:, :half])
    count = step // hub_rows
    for low in range(0, parts, count):
        if low > 0:
            own = other = jnp.zeros_like(own)
        first = step + bounds + low * half
        keep = jnp.concatenate([term_rows(first, count * half, half), own], axis=1)
        give = jnp.concatenate([term_rows(first + hubs // 2, count * half, half), other], axis=1).astype(bf16)
        at = slice(low, low + count)
        for piece in range(pieces):
            there = slice(piece * hub_rows, (piece + 1) * hub_rows)
            keep_ref[at, there, :] = keep[:, :, lanes(piece)]
            give_ref[at, there, :] = give[:, :, lanes(piece)]
    bias_total = dot(jnp.ones((16, nodes), bf16), grad_all[...])[:1]
    rows = bias_rows([bias_total[:, lanes(piece)] for piece in range(pieces)])
    keep_ref[:, pieces * hub_rows :, :] = jnp.broadcast_to(rows[None], (parts, 8, LANES))
    give_ref[:, pieces * hub_rows :, :] = jnp.broadcast_to(rows.astype(bf16)[None], (parts, 8, LANES))
    for low in range(0, bounds, step):
        bound_terms = term_rows(step + low, step, slots).astype(bf16)
        for piece in range(pieces):
            bound_ref[low // slots : (low + step) // slots, piece * slots : (piece + 1) * slots, :] = (
                bound_terms[:, :, lanes(piece)]
            )
    for store in stores:
        store.wait()


def bias_rows(parts):
    line = lax.broadcasted_iota(jnp.int32, (8, LANES), 0)
    rows = jnp.zeros((8, LANES), f32)
    for piece, value in enumerate(parts):
        high = value.astype(bf16).astype(f32)
        rows = jnp.where(line == piece, high, rows)
        rows = jnp.where(line == len(parts) + piece, value - high, rows)
    return rows


def join_kernel(bound_ref, keep_ref, got_ref, out_ref):
    parts, tall, _ = keep_ref.shape
    place = bound_ref.shape[1]
    pieces = (tall - 8) // 16
    out_ref[:, :place, :] = bound_ref[...]
    both = keep_ref[:, : tall - 8, :] + got_ref[:, : tall - 8, :].astype(f32)
    out_ref[:, place : place + tall - 8, :] = both.astype(bf16)
    tail = keep_ref[0, tall - 8 :, :] + got_ref[0, tall - 8 :, :].astype(f32)
    rows = bias_rows([tail[piece : piece + 1] + tail[pieces + piece : pieces + piece + 1] for piece in range(pieces)])
    out_ref[:, place + tall - 8 :, :] = jnp.broadcast_to(rows.astype(bf16)[None], (parts, 8, LANES))


def chip_sums(slots, hub_rows, rows, back_ref):
    parts, tall, _ = back_ref.shape
    pieces = (tall - 8) // (slots + hub_rows)
    whole = back_ref[:, pieces * slots :, :].astype(f32)
    count = whole.shape[1]
    whole = whole.reshape(rows // 2, 2, parts // rows, count, LANES)
    return jnp.sum(jnp.sum(whole, axis=2), axis=0), pieces


def both_halves(total, pieces, hub_rows, first):
    half = hub_rows // 2
    columns = []
    for piece in range(pieces):
        place = piece * hub_rows + first
        columns.append(jnp.concatenate([total[0, place : place + half], total[1, place : place + half]], axis=0))
    return jnp.concatenate(columns, axis=1)


def weight_sum_kernel(slots, hub_rows, rows, back_ref, out_ref):
    total, pieces = chip_sums(slots, hub_rows, rows, back_ref)
    weight = both_halves(total, pieces, hub_rows, hub_rows // 2)
    out_ref[...] = by_core(weight.astype(bf16), rows, out_ref.shape[0] // rows)


def other_sums_kernel(scale, slots, hub_rows, rows, back_ref, wn_ref, bias_ref, hub_ref):
    total, pieces = chip_sums(slots, hub_rows, rows, back_ref)
    tail = 0.5 * (total[0, pieces * hub_rows :] + total[1, pieces * hub_rows :])
    bias_ref[...] = jnp.concatenate(
        [tail[piece : piece + 1] + tail[pieces + piece : pieces + piece + 1] for piece in range(pieces)], axis=1
    )
    hub = both_halves(total, pieces, hub_rows, 0)
    high = hub.astype(bf16)
    low = (hub - high.astype(f32)).astype(bf16)
    hub_ref[...] = (dot(high, wn_ref[...], NT) + dot(low, wn_ref[...], NT)) * scale


def weights_kernel(core_ref, near_ref, far_ref, self_ref, neigh_ref):
    width = self_ref.shape[0]
    count = 2 * width // 16
    near, far = near_ref[:count].astype(f32), far_ref[:count].astype(f32)
    first_core = core_ref[0] == 0
    whole = jnp.concatenate([jnp.where(first_core, near, far), jnp.where(first_core, far, near)], axis=1)
    whole = whole.reshape(2 * width, width)
    self_ref[...] = whole[:width]
    neigh_ref[...] = whole[width:]


def scatter_kernel(local_ref, grad_ref, out_ref):
    height = out_ref.shape[0]
    first = pl.program_id(0) * height
    total = None
    for start in range(0, grad_ref.shape[0], TILE):
        rows = index_rows(local_ref, start, TILE)
        part = dot(hits_by_column(rows, first, height), grad_ref[start : start + TILE, :])
        total = part if total is None else total + part
    out_ref[...] = total


def final_kernel(scale, slots, send_ref, back_ref, scat_ref, grad_ref, ws_ref, wn_ref, out_ref):
    height, width = out_ref.shape
    first = pl.program_id(0) * height
    count = send_ref.shape[1]
    returned = jnp.concatenate(
        [
            back_ref[:, piece * slots : (piece + 1) * slots, :].reshape(count, LANES)
            for piece in range(width // LANES)
        ],
        axis=1,
    )
    total = scat_ref[...]
    for start in range(0, count, 512):
        stop = min(count, start + 512)
        hits = hits_by_column([send_ref[:, start:stop]], first, height)
        total = total + dot(hits, returned[start:stop])
    out_ref[...] = dot(grad_ref[...], ws_ref[...], NT) + dot((total * scale).astype(bf16), wn_ref[...], NT)


def call(
    kernel, ins, in_specs, outs, out_specs, name, grid=(), scratch=(), flops=0, moved=0, limit=SOME_VMEM
):
    return pl.pallas_call(
        kernel,
        grid=grid,
        in_specs=in_specs,
        out_specs=out_specs,
        out_shape=outs,
        scratch_shapes=scratch,
        compiler_params=params(limit),
        cost_estimate=cost(flops, moved),
        name=name,
    )(*ins)


def whole_block(shape):
    return pl.BlockSpec(shape, lambda *_: (0,) * len(shape))


def body(
    features,
    hub_features,
    w_self,
    w_neigh,
    out_bias,
    local_edges,
    hub_edges,
    remote_edges,
    send_rows,
    cotangent,
):
    nodes, width = features.shape
    hub_rows = hub_features.shape[0]
    parts = lax.axis_size(AXES)
    slots = send_rows.shape[1] // parts
    slab = slots + hub_rows
    pieces = width // LANES
    pay = pieces * slab + 8
    core = (lax.axis_index("row") % 2).astype(jnp.int32).reshape(1)
    rows = lax.axis_size("row")
    half = hub_rows // 2
    table = parts * slab
    scale = 1.0 / (local_edges.shape[1] + hub_edges.shape[1] + remote_edges.shape[1])
    local_t, hub_t, remote_t = local_edges.T, hub_edges.T, remote_edges.T
    bias = out_bias.reshape(1, width)
    shape = jax.ShapeDtypeStruct

    def sibling(value):
        return lax.ppermute(value, "row", [(r, r ^ 1) for r in range(rows)])

    def exchange(value):
        return lax.all_to_all(value, AXES, split_axis=0, concat_axis=0, tiled=True)

    sending = call(
        functools.partial(pick_kernel, rows),
        (send_rows, features, hub_features),
        [VMEM, VMEM, VMEM],
        shape((parts, slots + half, width), bf16),
        whole_block((parts, slots + half, width)),
        "pick_rows",
        limit=MOST_VMEM,
        flops=2 * parts * slots * nodes * width,
        moved=nodes * width * 2,
    )
    sending, features = lax.optimization_barrier((sending, features))
    received = exchange(sending)

    block = TILE
    by_block = pl.BlockSpec((block, width), lambda i: (i, 0))
    packed = 2 * width + table
    local_sum, pack = call(
        functools.partial(local_kernel, parts * slots, hub_rows),
        (core, local_t, remote_t, hub_t, features, features, cotangent),
        [SMEM]
        + [pl.BlockSpec((edges.shape[0], block), lambda i: (0, i)) for edges in (local_t, remote_t, hub_t)]
        + [whole_block((nodes, width)), by_block, by_block],
        [shape((nodes, width), f32), pltpu.HBM((nodes, packed), bf16)],
        [by_block, pl.BlockSpec((block, packed), lambda i: (i, 0))],
        "local_gather",
        grid=(nodes // block,),
        flops=8 * nodes * nodes * width,
        moved=nodes * packed * 2,
    )

    received, local_sum, pack = lax.optimization_barrier((received, local_sum, pack))
    near_hubs = call(
        functools.partial(half_kernel, slots),
        [received],
        [VMEM],
        shape((parts * half, width), bf16),
        VMEM,
        "take_hubs",
        moved=parts * half * width * 4,
    )
    far_hubs = sibling(near_hubs)

    activated, grad_pre, bound_terms, keep, give = call(
        functools.partial(middle_kernel, scale, slots),
        [core, received, near_hubs, far_hubs, w_self, w_neigh, bias, local_sum, pack],
        [SMEM] + [VMEM] * 7 + [HBM],
        [pltpu.HBM((nodes, width), bf16)] * 2
        + [
            shape((parts, pieces * slots, LANES), bf16),
            shape((parts, pieces * hub_rows + 8, LANES), f32),
            shape((parts, pieces * hub_rows + 8, LANES), bf16),
        ],
        [HBM] * 2 + [VMEM] * 3,
        "activate",
        limit=MUCH_VMEM,
        scratch=[
            pltpu.VMEM((nodes, packed + width), bf16),
            pltpu.VMEM((nodes, width), bf16),
            pltpu.VMEM((nodes, width), bf16),
            pltpu.VMEM((width, 2 * width + table), f32),
            pltpu.SemaphoreType.DMA((2, nodes // (2 * TILE))),
            pltpu.SemaphoreType.DMA((2, nodes // (2 * TILE))),
        ],
        flops=4 * nodes * table * width,
        moved=nodes * packed * 2,
    )
    got = sibling(give)
    back = exchange(
        call(
            join_kernel,
            [bound_terms, keep, got],
            [VMEM] * 3,
            shape((parts, pay, LANES), bf16),
            VMEM,
            "join_siblings",
            moved=parts * pay * LANES * 6,
        )
    )

    scattered = call(
        scatter_kernel,
        (local_t, grad_pre),
        [whole_block(local_t.shape), whole_block((nodes, width))],
        shape((nodes, width), f32),
        pl.BlockSpec((4 * TILE, width), lambda i: (i, 0)),
        "local_scatter",
        grid=(nodes // (4 * TILE),),
        flops=8 * nodes * nodes * width,
        moved=nodes * width * 6,
    )
    weight_rows = call(
        functools.partial(weight_sum_kernel, slots, hub_rows, rows),
        (back,),
        [VMEM],
        shape((parts, 8, width), bf16),
        VMEM,
        "weight_sums",
        moved=parts * pay * width * 2,
    )
    near_weights = exchange(weight_rows)
    grad_bias, grad_hubs = call(
        functools.partial(other_sums_kernel, scale, slots, hub_rows, rows),
        (back, w_neigh),
        [VMEM, VMEM],
        [shape((1, width), f32), shape((hub_rows, width), f32)],
        [whole_block((1, width)), whole_block((hub_rows, width))],
        "hub_sums",
        moved=parts * pay * width * 2,
    )

    height = 2 * TILE
    by_height = pl.BlockSpec((height, width), lambda i: (i, 0))
    grad_features = call(
        functools.partial(final_kernel, scale, slots),
        (send_rows, back, scattered, grad_pre, w_self, w_neigh),
        [whole_block(send_rows.shape), whole_block((parts, pay, LANES)), by_height, by_height]
        + [whole_block((width, width))] * 2,
        shape((nodes, width), f32),
        by_height,
        "return_scatter",
        grid=(nodes // height,),
        flops=2 * nodes * parts * slots * width,
        moved=nodes * width * 10,
    )
    near_weights, grad_features = lax.optimization_barrier((near_weights, grad_features))
    grad_w_self, grad_w_neigh = call(
        weights_kernel,
        [core, near_weights, sibling(near_weights)],
        [SMEM, VMEM, VMEM],
        [shape((width, width), f32)] * 2,
        [whole_block((width, width))] * 2,
        "weights",
        moved=width * width * 12,
    )
    return (activated, grad_features, grad_hubs, grad_w_self, grad_w_neigh, grad_bias.reshape(width))


def solution(mesh):
    split = P(AXES, None)
    return jax.shard_map(
        body,
        mesh=mesh,
        in_specs=(split, split, P(), P(), P(), split, split, split, split, split),
        out_specs=(split, split, split, P(), P(), P()),
        check_vma=False,
    )
```
